32 devices in a mesh: dp: 4 (over z), seq: 4 (over y, x), mp: 2 (over core).
Axes of the slice: x: 2, y: 2, z: 4, core: 2. Of those that a mesh axis runs over, the one named last changes fastest.
Arguments:
- inputs: bfloat16 [32, 2048, 1024], P('dp', ('seq', 'mp')), may hold values from -6 to 6
- gain_one: bfloat16 [1024], replicated, may hold values from 0.5 to 1.5
- w_query: bfloat16 [1024, 1024], P(None, 'mp'), may hold values from -0.1875 to 0.1875
- w_tied: bfloat16 [1024, 256], P(None, 'mp'), may hold values from -0.1875 to 0.1875
- w_rope: bfloat16 [1024, 32], replicated, may hold values from -0.1875 to 0.1875
- w_out: bfloat16 [1024, 1024], P('mp'), may hold values from -2 to 2
- gain_two: bfloat16 [1024], replicated, may hold values from 0.5 to 1.5
- w_gate: bfloat16 [1024, 2816], P(None, 'mp'), may hold values from -0.1875 to 0.1875
- w_up: bfloat16 [1024, 2816], P(None, 'mp'), may hold values from -0.1875 to 0.1875
- w_down: bfloat16 [2816, 1024], P('mp'), may hold values from -0.109375 to 0.109375
- doc_starts: int32 [32, 8], P('dp'), may hold values from 0 to 2048, as said below
- out_grad: bfloat16 [32, 2048, 1024], P('dp', ('seq', 'mp')), may hold values from -6 to 6
Outputs:
- outputs: bfloat16 [32, 2048, 1024], P('dp', ('seq', 'mp'))
- grad_inputs: float32 [32, 2048, 1024], P('dp', ('seq', 'mp'))
- grad_gain_one: float32 [1024], P(('dp', 'seq', 'mp'))
- grad_w_query: float32 [1024, 1024], P(('dp', 'seq'), 'mp')
- grad_w_tied: float32 [1024, 256], P(('dp', 'seq'), 'mp')
- grad_w_rope: float32 [1024, 32], P(('dp', 'seq', 'mp'))
- grad_w_out: float32 [1024, 1024], P('mp', ('dp', 'seq'))
- grad_gain_two: float32 [1024], P(('dp', 'seq', 'mp'))
- grad_w_gate: float32 [1024, 2816], P(('dp', 'seq'), 'mp')
- grad_w_up: float32 [1024, 2816], P(('dp', 'seq'), 'mp')
- grad_w_down: float32 [2816, 1024], P('mp', ('dp', 'seq'))
The draws below stay inside these ranges and needn't reach their ends.
Inputs may be any that keep to these rules, and one draw needn't show every extreme that they name: `doc_starts`: row b lists where the documents of packed sequence b begin: the first entry is 0, entries never fall, and an entry equal to 2048 marks no document.
All inputs are finite; a program needn't handle non-finite values.
Results may differ from the reference program's by a relative error of at most 0.018.
Values may be sent and summed in bfloat16 or wider, within the bound.
A program may use at most 384 MiB of HBM per device.

```python
import jax
import jax.numpy as jnp
from jax import lax

D = 1024
H = 16
HD = 64
G = 4
RD = 32
FF = 2816
HG = 4
SEQ_LEN = 2048
SEQ_DEV = 8
NDOC = 8
SEQS = 32


def draw_doc_starts(key, part):
    key = jax.random.fold_in(key, 7)
    pick_key, cut_key = jax.random.split(key)
    cut_points = jax.random.randint(cut_key, (SEQS, NDOC - 1), 1, SEQ_LEN + SEQ_LEN // 2)
    cut_points = jnp.minimum(cut_points, SEQ_LEN)
    chosen = jax.random.randint(pick_key, (SEQS // SEQ_DEV,), 0, SEQ_DEV)
    row_index = jnp.arange(SEQS, dtype=jnp.int32)
    single_doc = row_index % SEQ_DEV == jnp.repeat(chosen, SEQ_DEV, total_repeat_length=SEQS)
    cut_points = jnp.where(single_doc[:, None], SEQ_LEN, cut_points)
    cut_points = jnp.sort(cut_points, axis=-1)
    return jnp.concatenate([jnp.zeros((SEQS, 1), jnp.int32), cut_points.astype(jnp.int32)], axis=1)


def steps_of(rng, dims, shards, least, largest):
    factor_of, own = 1.0, jax.random.fold_in(rng, 6)
    for dim, shards_of in shards:
        draws = jnp.exp(jax.random.uniform(jax.random.fold_in(own, dim), (shards_of,), jnp.float32, least / len(shards), largest / len(shards)))
        factor_of = factor_of * jnp.repeat(draws, dims[dim] // shards_of).reshape([-1 if axis == dim else 1 for axis in range(len(dims))])
    return factor_of


def noise(rng, dims, spread, limit, cuts=(), kind=jnp.bfloat16):
    values = spread * jax.random.normal(rng, dims, jnp.float32)
    if cuts:
        values = values * steps_of(rng, dims, cuts, -0.22, 0.18)
    return jnp.clip(values, -limit, limit).astype(kind)


def setup_inputs(seed: int = 0) -> dict:
    arg_keys = jax.random.split(jax.random.key(seed), 13)
    return {
        "inputs": noise(arg_keys[0], (SEQS, SEQ_LEN, D), 1.0, 6.0, ((0, 4), (1, 8))),
        "gain_one": jnp.clip(1.0 + 0.1 * jax.random.normal(arg_keys[1], (D,), jnp.float32), 0.5, 1.5).astype(jnp.bfloat16),
        "w_query": noise(arg_keys[2], (D, H * HD), D ** -0.5, 0.1875, ((1, 2),)),
        "w_tied": noise(arg_keys[3], (D, G * HD), D ** -0.5, 0.1875, ((1, 2),)),
        "w_rope": noise(arg_keys[4], (D, RD), D ** -0.5, 0.1875),
        "w_out": noise(arg_keys[5], (H * HD, D), (max(H * HD // 128, 1)) ** -0.5, 2.0, ((0, 2),)),
        "gain_two": jnp.clip(1.0 + 0.1 * jax.random.normal(arg_keys[6], (D,), jnp.float32), 0.5, 1.5).astype(jnp.bfloat16),
        "w_gate": noise(arg_keys[7], (D, FF), D ** -0.5, 0.1875, ((1, 2),)),
        "w_up": noise(arg_keys[8], (D, FF), D ** -0.5, 0.1875, ((1, 2),)),
        "w_down": noise(arg_keys[9], (FF, D), FF ** -0.5, 0.109375, ((0, 2),)),
        "doc_starts": draw_doc_starts(jax.random.fold_in(arg_keys[12], 71), 0),
        "out_grad": noise(arg_keys[11], (SEQS, SEQ_LEN, D), 1.0, 6.0, ((0, 4), (1, 8))),
    }


epsilon = 1e-05
rope_base = 10000.0
precision_highest = lax.Precision.HIGHEST

@jax.custom_vjp
def reduced_precision(v):
    return lax.optimization_barrier(v.astype(jnp.bfloat16)).astype(jnp.float32)

@jax.custom_vjp
def backward_reduced_precision(v):
    return v

def low_keep(v):
    return (reduced_precision(v), None)

def low_pass(kept, grad):
    return (grad,)

def back_keep(v):
    return (v, None)

def back_low(kept, grad):
    return (reduced_precision(grad),)
reduced_precision.defvjp(low_keep, low_pass)
backward_reduced_precision.defvjp(back_keep, back_low)

def rope_tables(length):
    position = jnp.arange(length, dtype=jnp.float32)
    frequency = rope_base ** (-jnp.arange(RD // 2, dtype=jnp.float32) * 2.0 / RD)
    angles = position[:, None] * frequency[None, :]
    return (jnp.cos(angles), jnp.sin(angles))

def rotate(values, cosine, sine_table):
    half_width = values.shape[-1] // 2
    first_half = values[..., :half_width]
    second_half = values[..., half_width:]
    return jnp.concatenate([first_half * cosine - second_half * sine_table, second_half * cosine + first_half * sine_table], axis=-1)

def rms_scale(values, gain):
    return values * lax.rsqrt(lax.optimization_barrier(jnp.mean(values * values, axis=-1, keepdims=True)) + epsilon) * gain

def forward(params, inputs, segment):
    gain_one, w_query, w_tied, w_rope, w_out, gain_two, w_gate, w_up, w_down = params
    batch, length, model_width = inputs.shape
    plain_width = HD - RD
    cosine, sine_table = rope_tables(length)
    positions = jnp.arange(length, dtype=jnp.int32)
    allowed = (segment[:, :, None] == segment[:, None, :]) & (positions[:, None] >= positions[None, :])[None]
    normed = reduced_precision(rms_scale(inputs, gain_one))
    query_lin = backward_reduced_precision(jnp.dot(normed, w_query, precision=precision_highest)).reshape(batch, length, H, HD)
    queries = reduced_precision(jnp.concatenate([query_lin[..., :plain_width], rotate(query_lin[..., plain_width:], cosine[:, None, :], sine_table[:, None, :])], axis=-1))
    tied_state = reduced_precision(backward_reduced_precision(jnp.dot(normed, w_tied, precision=precision_highest))).reshape(batch, length, G, HD)
    rope_keys = reduced_precision(rotate(backward_reduced_precision(jnp.dot(normed, w_rope, precision=precision_highest)), cosine, sine_table))

    def group_attention(operands):
        query_groups, tied_group_rows = operands
        key_rows = jnp.concatenate([tied_group_rows[..., :plain_width], rope_keys], axis=-1)
        unscaled_scores = jnp.einsum('yrzs,yts->yzrt', query_groups, key_rows, precision=precision_highest)
        scores = backward_reduced_precision(unscaled_scores * HD ** (-0.5))
        masked = jnp.where(allowed[:, None], scores, -1e+30)
        row_max = lax.optimization_barrier(jnp.max(masked, axis=-1, keepdims=True))
        weights = jnp.exp(masked - row_max)
        attention_probs = reduced_precision(weights / lax.optimization_barrier(jnp.sum(weights, axis=-1, keepdims=True)))
        return backward_reduced_precision(reduced_precision(jnp.einsum('ewjz,ezc->ejwc', attention_probs, tied_group_rows, precision=precision_highest)))
    grouped_queries = jnp.moveaxis(queries.reshape(batch, length, G, HG, HD), 2, 0)
    grouped_tied = jnp.moveaxis(tied_state, 2, 0)
    group_outputs = lax.map(jax.checkpoint(group_attention), (grouped_queries, grouped_tied))
    head_outputs = jnp.moveaxis(group_outputs, 0, 2).reshape(batch, length, H * HD)
    attended = backward_reduced_precision(jnp.dot(head_outputs, w_out, precision=precision_highest))
    hidden = inputs + attended
    normed_two = reduced_precision(rms_scale(hidden, gain_two))
    gate_values = backward_reduced_precision(jnp.dot(normed_two, w_gate, precision=precision_highest))
    up_values = backward_reduced_precision(jnp.dot(normed_two, w_up, precision=precision_highest))
    active = reduced_precision(jax.nn.silu(gate_values) * up_values)
    result = backward_reduced_precision(jnp.dot(active, w_down, precision=precision_highest))
    return hidden + result

def reference(inputs, gain_one, w_query, w_tied, w_rope, w_out, gain_two, w_gate, w_up, w_down, doc_starts, out_grad):
    params = tuple((member.astype(jnp.float32) for member in (gain_one, w_query, w_tied, w_rope, w_out, gain_two, w_gate, w_up, w_down)))
    positions = jnp.arange(SEQ_LEN, dtype=jnp.int32)
    segments = lax.optimization_barrier(jnp.sum((doc_starts[:, None, :] <= positions[None, :, None]).astype(jnp.int32), axis=-1))
    pair_count = SEQS // 2
    scanned = (inputs.astype(jnp.float32).reshape(pair_count, 2, SEQ_LEN, D), segments.reshape(pair_count, 2, SEQ_LEN), out_grad.astype(jnp.float32).reshape(pair_count, 2, SEQ_LEN, D))

    def accumulate(totals, sample):
        pair_inputs, pair_segments, pair_grad = sample

        def apply_layer(weights, values):
            return forward(weights, values, pair_segments)
        result, pullback = jax.vjp(apply_layer, params, pair_inputs)
        grad_params, grad_pair = pullback(pair_grad)
        return (tuple((running + addend for running, addend in zip(totals, grad_params))), (result, grad_pair))
    zero_totals = tuple((jnp.zeros_like(member) for member in params))
    totals, (results, grad_pairs) = lax.scan(accumulate, zero_totals, scanned)
    grad_gain_one, grad_w_query, grad_w_tied, grad_w_rope, grad_w_out, grad_gain_two, grad_w_gate, grad_w_up, grad_w_down = totals
    return (results.reshape(SEQS, SEQ_LEN, D).astype(jnp.bfloat16), grad_pairs.reshape(SEQS, SEQ_LEN, D), grad_gain_one, grad_w_query, grad_w_tied, grad_w_rope, grad_w_out, grad_gain_two, grad_w_gate, grad_w_up, grad_w_down)
```

```python
import functools

import jax
import jax.numpy as jnp
from jax import lax
from jax.experimental import pallas as pl
from jax.experimental.pallas import tpu as pltpu
from jax.sharding import PartitionSpec as P

HD = 64
RD = 32


epsilon = 1e-05
rope_base = 10000.0
masked_value = -1e30


def rope_tables(offset, count, rope_width):
    position = (offset + jnp.arange(count, dtype=jnp.int32)).astype(jnp.float32)
    frequency = rope_base ** (-jnp.arange(rope_width // 2, dtype=jnp.float32) * 2.0 / rope_width)
    angles = position[:, None] * frequency[None, :]
    return (jnp.cos(angles), jnp.sin(angles))


def rotate(values, cosine, sine_table):
    half_width = values.shape[-1] // 2
    first_half = values[..., :half_width]
    second_half = values[..., half_width:]
    return jnp.concatenate(
        [
            first_half * cosine - second_half * sine_table,
            second_half * cosine + first_half * sine_table,
        ],
        axis=-1,
    )


def rotate_back(grads, cosine, sine_table):
    half_width = grads.shape[-1] // 2
    first_half = grads[..., :half_width]
    second_half = grads[..., half_width:]
    return jnp.concatenate(
        [
            first_half * cosine + second_half * sine_table,
            second_half * cosine - first_half * sine_table,
        ],
        axis=-1,
    )


def contract_rows(left, right):
    return lax.dot_general(
        left, right, (((0,), (0,)), ((), ())), preferred_element_type=jnp.float32
    )


def times_transposed(left, right):
    return lax.dot_general(
        left, right, (((1,), (1,)), ((), ())), preferred_element_type=jnp.float32
    )


def norm_back(grad_normed, values, inverse, gain):
    scaled = grad_normed * gain
    grad_gain = jnp.sum(grad_normed * values * inverse, axis=(0, 1))
    grad_values = inverse * scaled - values * inverse**3 * jnp.mean(
        scaled * values, axis=-1, keepdims=True
    )
    return (grad_values, grad_gain)


def attend(operands):
    queries, key_full, values, allowed = operands
    scores = jnp.einsum(
        "qghd,kgd->ghqk", queries, key_full, preferred_element_type=jnp.float32
    ) * HD ** (-0.5)
    masked = jnp.where(allowed[None, None], scores, masked_value)
    row_max = jnp.max(masked, axis=-1, keepdims=True)
    weights = jnp.exp(masked - row_max)
    row_total = jnp.sum(weights, axis=-1, keepdims=True)
    attention_probs = (weights / row_total).astype(jnp.bfloat16)
    combined = jnp.einsum(
        "ghqk,kgd->qghd", attention_probs, values, preferred_element_type=jnp.float32
    )
    return (combined.astype(jnp.bfloat16), row_max + jnp.log(row_total))


def attend_back(operands):
    queries, key_full, values, allowed, log_total, grad_heads = operands
    score_scale = HD ** (-0.5)
    plain_width = HD - RD
    scores = (
        jnp.einsum("qghd,kgd->ghqk", queries, key_full, preferred_element_type=jnp.float32)
        * score_scale
    )
    masked = jnp.where(allowed[None, None], scores, masked_value)
    probs_float = jnp.exp(masked - log_total)
    grad_probs = jnp.einsum(
        "qghd,kgd->ghqk", grad_heads, values, preferred_element_type=jnp.float32
    )
    row_delta = jnp.sum(probs_float * grad_probs, axis=-1, keepdims=True)
    grad_scores = (probs_float * (grad_probs - row_delta)).astype(jnp.bfloat16)
    grad_queries = (
        jnp.einsum("ghqk,kgd->qghd", grad_scores, key_full, preferred_element_type=jnp.float32)
        * score_scale
    )
    grad_keys = (
        jnp.einsum("ghqk,qghd->kgd", grad_scores, queries, preferred_element_type=jnp.float32)
        * score_scale
    )
    grad_values = jnp.einsum(
        "ghqk,qghd->kgd",
        probs_float.astype(jnp.bfloat16),
        grad_heads,
        preferred_element_type=jnp.float32,
    )
    grad_tied = grad_values + jnp.concatenate(
        [grad_keys[..., :plain_width], jnp.zeros_like(grad_keys[..., plain_width:])], axis=-1
    )
    grad_rope = jnp.sum(grad_keys[..., plain_width:], axis=1)
    return (grad_queries, grad_tied, grad_rope)


def on_device(
    inputs,
    gain_one,
    w_query,
    w_tied,
    w_rope,
    w_out,
    gain_two,
    w_gate,
    w_up,
    w_down,
    doc_starts,
    out_grad,
):
    seq_count, own_count, model_width = inputs.shape
    plain_width = HD - RD
    group_local = w_tied.shape[1] // HD
    head_local = w_query.shape[1] // HD
    seq_index = lax.axis_index("seq")
    mp_index = lax.axis_index("mp")
    gain_one_float = gain_one.astype(jnp.float32)
    gain_two_float = gain_two.astype(jnp.float32)
    inputs_float = inputs.astype(jnp.float32)
    inverse_one = lax.rsqrt(jnp.mean(inputs_float * inputs_float, axis=-1, keepdims=True) + epsilon)
    normed_one = (inputs_float * inverse_one * gain_one_float).astype(jnp.bfloat16)
    gathered_one = lax.all_gather(normed_one, "mp", axis=1, tiled=True)
    context = gathered_one.shape[1]
    token_count = seq_count * context
    flat_one = gathered_one.reshape(token_count, model_width)
    offset = seq_index * context
    cosine, sine_table = rope_tables(offset, context, RD)
    query_lin = jnp.dot(flat_one, w_query, preferred_element_type=jnp.float32).reshape(
        seq_count, context, head_local, HD
    )
    queries = jnp.concatenate(
        [
            query_lin[..., :plain_width],
            rotate(
                query_lin[..., plain_width:], cosine[None, :, None, :], sine_table[None, :, None, :]
            ),
        ],
        axis=-1,
    ).astype(jnp.bfloat16)
    queries = queries.reshape(seq_count, context, group_local, head_local // group_local, HD)
    tied_state = (
        jnp.dot(flat_one, w_tied, preferred_element_type=jnp.float32)
        .astype(jnp.bfloat16)
        .reshape(seq_count, context, group_local * HD)
    )
    rope_lin = jnp.dot(flat_one, w_rope, preferred_element_type=jnp.float32).reshape(
        seq_count, context, RD
    )
    rope_keys = rotate(rope_lin, cosine[None], sine_table[None]).astype(jnp.bfloat16)
    tied_all, rope_all = (
        lax.all_gather(tied_state, "seq", axis=1, tiled=True),
        lax.all_gather(rope_keys, "seq", axis=1, tiled=True),
    )
    length = tied_all.shape[1]
    values_all = tied_all.reshape(seq_count, length, group_local, HD)
    key_full = jnp.concatenate(
        [
            values_all[..., :plain_width],
            jnp.broadcast_to(rope_all[:, :, None, :], (seq_count, length, group_local, RD)),
        ],
        axis=-1,
    )
    key_position = jnp.arange(length, dtype=jnp.int32)
    key_segment = jnp.sum(
        (doc_starts[:, None, :] <= key_position[None, :, None]).astype(jnp.int32), axis=-1
    )
    query_segment = lax.dynamic_slice_in_dim(key_segment, offset, context, 1)
    query_position = offset + jnp.arange(context, dtype=jnp.int32)
    allowed = (query_segment[:, :, None] == key_segment[:, None, :]) & (
        query_position[:, None] >= key_position[None, :]
    )[None]
    head_outputs, log_total = lax.map(attend, (queries, key_full, values_all, allowed))
    flat_heads = head_outputs.reshape(token_count, head_local * HD)
    attended_part = jnp.dot(flat_heads, w_out, preferred_element_type=jnp.float32).reshape(
        seq_count, context, model_width
    )
    attended = lax.psum_scatter(
        attended_part.astype(jnp.bfloat16), "mp", scatter_dimension=1, tiled=True
    ).astype(jnp.float32)
    hidden = inputs_float + attended
    inverse_two = lax.rsqrt(jnp.mean(hidden * hidden, axis=-1, keepdims=True) + epsilon)
    normed_two = (hidden * inverse_two * gain_two_float).astype(jnp.bfloat16)
    gathered_two = lax.all_gather(normed_two, "mp", axis=1, tiled=True)
    flat_two = gathered_two.reshape(token_count, model_width)
    gate_values = jnp.dot(flat_two, w_gate, preferred_element_type=jnp.float32)
    up_values = jnp.dot(flat_two, w_up, preferred_element_type=jnp.float32)
    sigmoid_gate = jax.nn.sigmoid(gate_values)
    silu_gate = gate_values * sigmoid_gate
    active = (silu_gate * up_values).astype(jnp.bfloat16)
    result_part = jnp.dot(active, w_down, preferred_element_type=jnp.float32).reshape(
        seq_count, context, model_width
    )
    result = lax.psum_scatter(
        result_part.astype(jnp.bfloat16), "mp", scatter_dimension=1, tiled=True
    ).astype(jnp.float32)
    outputs = (hidden + result).astype(jnp.bfloat16)
    grad_out_all = lax.all_gather(out_grad, "mp", axis=1, tiled=True)
    flat_grad = grad_out_all.reshape(token_count, model_width)
    grad_active = times_transposed(flat_grad, w_down)
    grad_w_down = contract_rows(active, flat_grad)
    grad_gate = (
        grad_active * up_values * sigmoid_gate * (1.0 + gate_values * (1.0 - sigmoid_gate))
    ).astype(jnp.bfloat16)
    grad_up = (grad_active * silu_gate).astype(jnp.bfloat16)
    grad_w_gate = contract_rows(flat_two, grad_gate)
    grad_w_up = contract_rows(flat_two, grad_up)
    grad_two_part = (times_transposed(grad_gate, w_gate) + times_transposed(grad_up, w_up)).reshape(
        seq_count, context, model_width
    )
    grad_normed_two = lax.psum_scatter(
        grad_two_part.astype(jnp.bfloat16), "mp", scatter_dimension=1, tiled=True
    ).astype(jnp.float32)
    grad_hidden_norm, grad_gain_two = norm_back(
        grad_normed_two, hidden, inverse_two, gain_two_float
    )
    grad_hidden = out_grad.astype(jnp.float32) + grad_hidden_norm
    grad_attended_all = lax.all_gather(grad_hidden.astype(jnp.bfloat16), "mp", axis=1, tiled=True)
    flat_attended = grad_attended_all.reshape(token_count, model_width)
    grad_w_out = contract_rows(flat_heads, flat_attended)
    grad_heads = times_transposed(flat_attended, w_out).astype(jnp.bfloat16).reshape(queries.shape)
    grad_queries, grad_tied, grad_rope = lax.map(
        attend_back, (queries, key_full, values_all, allowed, log_total, grad_heads)
    )
    grad_queries = grad_queries.reshape(seq_count, context, head_local, HD)
    grad_query_lin = (
        jnp.concatenate(
            [
                grad_queries[..., :plain_width],
                rotate_back(
                    grad_queries[..., plain_width:],
                    cosine[None, :, None, :],
                    sine_table[None, :, None, :],
                ),
            ],
            axis=-1,
        )
        .astype(jnp.bfloat16)
        .reshape(token_count, head_local * HD)
    )
    tied_own, rope_context = (
        lax.psum_scatter(
            grad_tied.reshape(seq_count, length, group_local * HD).astype(jnp.bfloat16),
            "seq",
            scatter_dimension=1,
            tiled=True,
        ).astype(jnp.float32),
        lax.psum_scatter(
            grad_rope.astype(jnp.bfloat16), "seq", scatter_dimension=1, tiled=True
        ).astype(jnp.float32),
    )
    grad_tied_flat = tied_own.astype(jnp.bfloat16).reshape(token_count, group_local * HD)
    grad_one_part = (
        times_transposed(grad_query_lin, w_query) + times_transposed(grad_tied_flat, w_tied)
    ).reshape(seq_count, context, model_width)
    grad_normed_one, rope_own = (
        lax.psum_scatter(
            grad_one_part.astype(jnp.bfloat16), "mp", scatter_dimension=1, tiled=True
        ).astype(jnp.float32),
        lax.psum_scatter(
            rope_context.astype(jnp.bfloat16), "mp", scatter_dimension=1, tiled=True
        ).astype(jnp.float32),
    )
    own_offset = offset + mp_index * own_count
    cosine_own, sine_own = rope_tables(own_offset, own_count, RD)
    grad_rope_flat = (
        rotate_back(rope_own, cosine_own[None], sine_own[None])
        .astype(jnp.bfloat16)
        .reshape(seq_count * own_count, RD)
    )
    grad_normed_one = grad_normed_one + times_transposed(grad_rope_flat, w_rope).reshape(
        seq_count, own_count, model_width
    )
    grad_w_rope = contract_rows(
        normed_one.reshape(seq_count * own_count, model_width), grad_rope_flat
    )
    grad_w_query = contract_rows(flat_one, grad_query_lin)
    grad_w_tied = contract_rows(flat_one, grad_tied_flat)
    grad_inputs_norm, grad_gain_one = norm_back(
        grad_normed_one, inputs_float, inverse_one, gain_one_float
    )
    grad_inputs = grad_hidden + grad_inputs_norm
    small_sums = (
        lax.psum_scatter(grad_gain_one, ("dp", "seq", "mp"), scatter_dimension=0, tiled=True),
        lax.psum_scatter(grad_w_rope, ("dp", "seq", "mp"), scatter_dimension=0, tiled=True),
        lax.psum_scatter(grad_gain_two, ("dp", "seq", "mp"), scatter_dimension=0, tiled=True),
    )
    weight_terms = (grad_w_query, grad_w_tied, grad_w_out, grad_w_gate, grad_w_up, grad_w_down)
    weight_sums = (
        lax.psum_scatter(weight_terms[0], ("dp", "seq"), scatter_dimension=0, tiled=True),
        lax.psum_scatter(weight_terms[1], ("dp", "seq"), scatter_dimension=0, tiled=True),
        lax.psum_scatter(weight_terms[2], ("dp", "seq"), scatter_dimension=1, tiled=True),
        lax.psum_scatter(weight_terms[3], ("dp", "seq"), scatter_dimension=0, tiled=True),
        lax.psum_scatter(weight_terms[4], ("dp", "seq"), scatter_dimension=0, tiled=True),
        lax.psum_scatter(weight_terms[5], ("dp", "seq"), scatter_dimension=1, tiled=True),
    )
    return (
        outputs,
        grad_inputs,
        small_sums[0],
        weight_sums[0],
        weight_sums[1],
        small_sums[1],
        weight_sums[2],
        small_sums[2],
        weight_sums[3],
        weight_sums[4],
        weight_sums[5],
    )


BF = jnp.bfloat16
F32 = jnp.float32
NN = (((1,), (0,)), ((), ()))
NT = (((1,), (1,)), ((), ()))
TN = (((0,), (0,)), ((), ()))
BIG = 2.0**100
MIB = 1 << 20
LANE = 128


def mxu(left, right, dims):
    return lax.dot_general(left, right, dims, preferred_element_type=F32)


def params(limit=56):
    return pltpu.CompilerParams(vmem_limit_bytes=limit * MIB)


def swap_cores(value):
    return lax.ppermute(value, "mp", [(0, 1), (1, 0)])


def by_core(own, other, axis):
    first = lax.axis_index("mp") == 0
    return jnp.concatenate(
        [jnp.where(first, own, other), jnp.where(first, other, own)], axis=axis
    )


def rotate_rows(values, cosine, sine_table):
    half = values.shape[0] // 2
    a, b = values[:half], values[half:]
    return jnp.concatenate([a * cosine - b * sine_table, b * cosine + a * sine_table], axis=0)


def project_kernel(heads, x_ref, gain_ref, w_ref, cos_ref, sin_ref, q_ref, kv_ref, nt_ref):
    x = x_ref[0].astype(F32)
    inverse = lax.rsqrt(jnp.mean(x * x, axis=-1, keepdims=True) + epsilon)
    normed = (x * inverse * gain_ref[...]).astype(BF)
    nt_ref[...] = normed.T
    cosine, sine_table = cos_ref[...], sin_ref[...]
    lin = mxu(w_ref[...], normed, NT)
    plain = HD - RD
    pieces = []
    for h in range(heads):
        at = h * HD
        pieces.append(lin[at : at + plain])
        pieces.append(rotate_rows(lin[at + plain : at + HD], cosine, sine_table))
    queries = jnp.concatenate(pieces, axis=0)
    q_ref[...] = (queries.astype(BF) * HD ** (-0.5)).astype(BF)
    tied_end = w_ref.shape[0] - RD
    kv_ref[0, : tied_end - heads * HD] = lin[heads * HD : tied_end].astype(BF)
    kv_ref[0, tied_end - heads * HD :] = rotate_rows(lin[tied_end:], cosine, sine_table).astype(BF)


def project(x, gain, weights, cosine, sine_table, heads):
    count, own, width = x.shape
    rows = weights.shape[0]
    kv_rows = rows - heads * HD
    whole = lambda b: (0, 0)
    return pl.pallas_call(
        functools.partial(project_kernel, heads),
        grid=(count,),
        in_specs=[
            pl.BlockSpec((1, own, width), lambda b: (b, 0, 0)),
            pl.BlockSpec((1, width), whole),
            pl.BlockSpec((rows, width), whole),
            pl.BlockSpec(cosine.shape, whole),
            pl.BlockSpec(cosine.shape, whole),
        ],
        out_specs=[
            pl.BlockSpec((heads * HD, own), lambda b: (0, b)),
            pl.BlockSpec((1, kv_rows, own), lambda b: (b, 0, 0)),
            pl.BlockSpec((width, own), lambda b: (0, b)),
        ],
        out_shape=[
            jax.ShapeDtypeStruct((heads * HD, count * own), BF),
            jax.ShapeDtypeStruct((count, kv_rows, own), BF),
            jax.ShapeDtypeStruct((width, count * own), BF),
        ],
        compiler_params=params(),
        name="project",
    )(x, gain, weights, cosine, sine_table)


def segment_counts(starts, first, width):
    position = first + lax.broadcasted_iota(jnp.int32, (1, width), 1)
    count = jnp.zeros((1, width), jnp.int32)
    for start in starts:
        count = count + (start <= position).astype(jnp.int32)
    return count


def query_rows(starts, first, width):
    row = lax.broadcasted_iota(jnp.int32, (16, width), 0)
    match = segment_counts(starts, first, width) == row + 1
    return jnp.where(match, 1.0, 0.0).astype(BF)


def key_rows(starts, first, width):
    row = lax.broadcasted_iota(jnp.int32, (16, width), 0)
    match = (segment_counts(starts, first, width) == row + 1) | (row >= len(starts))
    return jnp.where(match, 0.0, -BIG).astype(BF)


def first_rows(count, width):
    row = lax.broadcasted_iota(jnp.int32, (16, width), 0)
    return jnp.where(row < count, 1.0, 0.0).astype(BF)


def three_parts(row, width):
    high = row.astype(BF)
    rest = row - high.astype(F32)
    middle = rest.astype(BF)
    low = (rest - middle.astype(F32)).astype(BF)
    at = lax.broadcasted_iota(jnp.int32, (16, width), 0)
    parts = jnp.where(at == 0, high.astype(F32), 0.0)
    parts = jnp.where(at == 1, middle.astype(F32), parts)
    return jnp.where(at == 2, low.astype(F32), parts).astype(BF)


def start_chunk(starts, first, chunk):
    begin = jnp.int32(0)
    for start in starts:
        begin = jnp.where(start <= first, jnp.maximum(begin, start), begin)
    return begin // chunk


def my_chunk():
    return lax.axis_index("seq") * lax.axis_size("mp") + lax.axis_index("mp")


def stack_heads(value, at, heads):
    return jnp.concatenate([value[at + h * HD : at + (h + 1) * HD] for h in range(heads)], axis=1)


def attend_kernel(groups, heads, docs_ref, q_ref, kv_ref, out_ref, lse_ref, qa, ka, va, acc, top):
    b = pl.program_id(0)
    own = q_ref.shape[1]
    ndoc = docs_ref.shape[1]
    starts = [docs_ref[b, k] for k in range(ndoc)]
    me = my_chunk()
    begin = start_chunk(starts, me * own, own)
    wide = heads * own
    tied = groups * HD
    plain = HD - RD
    q_doc = query_rows(starts, me * own, own)
    q_doc = jnp.concatenate([q_doc] * heads, axis=1)
    q_all = q_ref[...]
    for g in range(groups):
        qa[g, :HD] = stack_heads(q_all, g * heads * HD, heads)
        qa[g, HD : HD + 16] = q_doc
        qa[g, HD + 16 :] = jnp.zeros((LANE - HD - 16, wide), BF)
    ones = first_rows(1, own)
    zeros = jnp.zeros((LANE - HD - 16, own), BF)

    def scores(j, g):
        doc = key_rows(starts, j * own, own)
        block = jnp.concatenate(
            [
                kv_ref[j, 0, g * HD : g * HD + plain],
                kv_ref[j, 0, tied : tied + RD],
                doc,
                zeros,
            ],
            axis=0,
        )
        return mxu(block.T, qa[g], NN)

    def weighted(j, g, weights):
        values = jnp.concatenate([kv_ref[j, 0, g * HD : (g + 1) * HD], ones], axis=0)
        return mxu(values, weights.astype(BF), NN)

    key_at = lax.broadcasted_iota(jnp.int32, (own, own), 0)
    query_at = lax.broadcasted_iota(jnp.int32, (own, own), 1)
    causal = jnp.concatenate([key_at <= query_at] * heads, axis=1)
    for g in range(groups):
        logits = jnp.where(causal, scores(me, g), masked_value)
        peak = jnp.max(logits, axis=0, keepdims=True)
        acc[g] = weighted(me, g, jnp.exp(logits - peak))
        top[g] = peak

    def step(i, carry):
        j = me - 1 - i
        for g in range(groups):
            logits = scores(j, g)
            peak = jnp.maximum(top[g], jnp.max(logits, axis=0, keepdims=True))
            shrink = jnp.exp(top[g] - peak)
            acc[g] = acc[g] * shrink + weighted(j, g, jnp.exp(logits - peak))
            top[g] = peak
        return carry

    lax.fori_loop(0, me - begin, step, 0)
    for g in range(groups):
        total = acc[g, HD : HD + 1]
        result = acc[g, :HD] / total
        lse_ref[0, g : g + 1] = top[g] + jnp.log(total)
        for h in range(heads):
            at = (g * heads + h) * HD
            out_ref[at : at + HD] = result[:, h * own : (h + 1) * own].astype(BF)


def attend_forward(docs, q, kv, groups, heads):
    chunks, count, kv_rows, own = kv.shape
    wide = heads * own
    return pl.pallas_call(
        functools.partial(attend_kernel, groups, heads),
        grid=(count,),
        in_specs=[
            pl.BlockSpec(memory_space=pltpu.SMEM),
            pl.BlockSpec((q.shape[0], own), lambda b: (0, b)),
            pl.BlockSpec((chunks, 1, kv_rows, own), lambda b: (0, b, 0, 0)),
        ],
        out_specs=[
            pl.BlockSpec((q.shape[0], own), lambda b: (0, b)),
            pl.BlockSpec((1, groups, wide), lambda b: (b, 0, 0)),
        ],
        out_shape=[
            jax.ShapeDtypeStruct(q.shape, BF),
            jax.ShapeDtypeStruct((count, groups, wide), F32),
        ],
        scratch_shapes=[
            pltpu.VMEM((groups, LANE, wide), BF),
            pltpu.VMEM((8, LANE), BF),
            pltpu.VMEM((8, LANE), BF),
            pltpu.VMEM((groups, HD + 16, wide), F32),
            pltpu.VMEM((groups, 1, wide), F32),
        ],
        compiler_params=params(),
        name="attend",
    )(docs, q, kv)


def attend_back_kernel(
    groups, heads, docs_ref, q_ref, do_ref, lse_ref, delta_ref, kv_ref, rot_ref,
    dq_ref, dkv_ref, qs, qa, ds_, da, dq,
):
    b = pl.program_id(0)
    own = q_ref.shape[1]
    ndoc = docs_ref.shape[1]
    starts = [docs_ref[b, k] for k in range(ndoc)]
    me = my_chunk()
    begin = start_chunk(starts, me * own, own)
    wide = heads * own
    tied = groups * HD
    plain = HD - RD
    q_doc = query_rows(starts, me * own, own)
    q_doc = jnp.concatenate([q_doc] * heads, axis=1)
    q_all, do_all = q_ref[...], do_ref[...]
    pad_q = jnp.zeros((LANE - HD - 32, wide), BF)
    pad_d = jnp.zeros((LANE - HD - 16, wide), BF)
    for g in range(groups):
        q_rows = stack_heads(q_all, g * heads * HD, heads)
        do_rows = stack_heads(do_all, g * heads * HD, heads)
        qs[g] = q_rows
        ds_[g] = do_rows
        lse_rows = three_parts(-lse_ref[0, g : g + 1], wide)
        delta_row = jnp.concatenate(
            [delta_ref[0, g * heads + h : g * heads + h + 1] for h in range(heads)], axis=1
        )
        delta_rows = three_parts(-delta_row, wide)
        qa[g] = jnp.concatenate([q_rows, q_doc, lse_rows, pad_q], axis=0).T
        da[g] = jnp.concatenate([do_rows, delta_rows, pad_d], axis=0).T
    ones = first_rows(3, own)
    pad_k = jnp.zeros((LANE - HD - 32, own), BF)
    pad_v = jnp.zeros((LANE - HD - 16, own), BF)

    def clear(j, carry):
        dkv_ref[j, 0] = jnp.zeros(dkv_ref.shape[2:], BF)
        return carry

    lax.fori_loop(0, begin, clear, 0)
    lax.fori_loop(me + 1, dkv_ref.shape[0], clear, 0)

    def block(j, diagonal):
        doc = key_rows(starts, j * own, own)
        rope_rows = kv_ref[j, 0, tied : tied + RD]
        rope_sum = jnp.zeros((RD, own), F32)
        for g in range(groups):
            values = kv_ref[j, 0, g * HD : (g + 1) * HD]
            keys = jnp.concatenate([values[:plain], rope_rows], axis=0)
            logits = mxu(qa[g], jnp.concatenate([keys, doc, ones, pad_k], axis=0), NN)
            weights = jnp.exp(logits)
            if diagonal:
                query_at = lax.broadcasted_iota(jnp.int32, (own, own), 0)
                key_at = lax.broadcasted_iota(jnp.int32, (own, own), 1)
                causal = jnp.concatenate([key_at <= query_at] * heads, axis=0)
                weights = jnp.where(causal, weights, 0.0)
            slopes = mxu(da[g], jnp.concatenate([values, ones, pad_v], axis=0), NN)
            grads = (weights * slopes).astype(BF)
            grad_values = mxu(ds_[g], weights.astype(BF), NN)
            grad_keys = mxu(qs[g], grads, NN)
            grad_queries = mxu(grads, keys.T, NN)
            if diagonal:
                dq[g] = grad_queries
            else:
                dq[g] += grad_queries
            dkv_ref[j, 0, g * HD : g * HD + plain] = (
                grad_values[:plain] + grad_keys[:plain]
            ).astype(BF)
            dkv_ref[j, 0, g * HD + plain : (g + 1) * HD] = grad_values[plain:].astype(BF)
            rope_sum = rope_sum + grad_keys[plain:]
        dkv_ref[j, 0, tied : tied + RD] = rope_sum.astype(BF)

    block(me, True)

    def step(j, carry):
        block(j, False)
        return carry

    lax.fori_loop(begin, me, step, 0)
    straight, ahead, behind = rot_ref[0], rot_ref[1], rot_ref[2]
    half = RD // 2
    for g in range(groups):
        for pair in range(heads // 2):
            at = 2 * pair * own
            both = jnp.concatenate([dq[g, at : at + own], dq[g, at + own : at + 2 * own]], axis=1)
            both = both * HD ** (-0.5)
            turned = (
                both * straight
                + pltpu.roll(both, LANE - half, 1) * ahead
                + pltpu.roll(both, half, 1) * behind
            )
            to = (g * heads + 2 * pair) * HD
            dq_ref[:, to : to + 2 * HD] = turned.astype(BF)


def attend_backward(docs, q, do, lse, delta, kv, turns, groups, heads):
    chunks, count, kv_rows, own = kv.shape
    wide = heads * own
    width = q.shape[0]
    return pl.pallas_call(
        functools.partial(attend_back_kernel, groups, heads),
        grid=(count,),
        in_specs=[
            pl.BlockSpec(memory_space=pltpu.SMEM),
            pl.BlockSpec((width, own), lambda b: (0, b)),
            pl.BlockSpec((width, own), lambda b: (0, b)),
            pl.BlockSpec((1, groups, wide), lambda b: (b, 0, 0)),
            pl.BlockSpec((1, groups * heads, own), lambda b: (b, 0, 0)),
            pl.BlockSpec((chunks, 1, kv_rows, own), lambda b: (0, b, 0, 0)),
            pl.BlockSpec(turns.shape, lambda b: (0, 0, 0)),
        ],
        out_specs=[
            pl.BlockSpec((own, width), lambda b: (b, 0)),
            pl.BlockSpec((chunks, 1, kv_rows, own), lambda b: (0, b, 0, 0)),
        ],
        out_shape=[
            jax.ShapeDtypeStruct((count * own, width), BF),
            jax.ShapeDtypeStruct(kv.shape, BF),
        ],
        scratch_shapes=[
            pltpu.VMEM((groups, HD, wide), BF),
            pltpu.VMEM((groups, wide, LANE), BF),
            pltpu.VMEM((groups, HD, wide), BF),
            pltpu.VMEM((groups, wide, LANE), BF),
            pltpu.VMEM((groups, wide, HD), F32),
        ],
        compiler_params=params(),
        name="attend_back",
    )(docs, q, do, lse, delta, kv, turns)


def load_weights(refs, targets, sems):
    copies = []
    slot = 0
    for (source, side, axis), target in zip(refs, targets, strict=True):
        blocks = source.shape[axis] // LANE
        for t in range(blocks):
            to = pl.ds((2 * t + side) * LANE, LANE)
            of = pl.ds(t * LANE, LANE)
            src = source.at[:, of] if axis == 1 else source.at[of]
            dst = target.at[:, to] if axis == 1 else target.at[to]
            copies.append(pltpu.make_async_copy(src, dst, sems.at[slot]))
            slot += 1
    return copies


def feed_kernel(
    x_ref, og_ref, o_ref, gain_ref, wo_ref, wgo_ref, wgp_ref, wuo_ref, wup_ref, wdo_ref, wdp_ref,
    out_ref, nt_ref, ogt_ref, act_ref, gg_ref, gu_ref, gh_ref, gat_ref, do_ref, delta_ref, gg2_ref,
    wo, wg, wu, wd, sems,
):
    b = pl.program_id(0)

    @pl.when(b == 0)
    def _():
        copies = [pltpu.make_async_copy(wo_ref, wo, sems.at[sems.shape[0] - 1])]
        copies += load_weights(
            [
                (wgo_ref, 0, 1), (wgp_ref, 1, 1), (wuo_ref, 0, 1), (wup_ref, 1, 1),
                (wdo_ref, 0, 0), (wdp_ref, 1, 0),
            ],
            [wg, wg, wu, wu, wd, wd],
            sems,
        )
        for copy in copies:
            copy.start()
        for copy in copies:
            copy.wait()
        gg2_ref[...] = jnp.zeros(gg2_ref.shape, F32)

    og = og_ref[0]
    heads_out = o_ref[...]
    gain = gain_ref[...]
    hidden = x_ref[0].astype(F32) + mxu(heads_out, wo[...], TN)
    inverse = lax.rsqrt(jnp.mean(hidden * hidden, axis=-1, keepdims=True) + epsilon)
    normed = (hidden * inverse * gain).astype(BF)
    nt_ref[...] = normed.T
    ogt_ref[...] = og.T
    units = wg.shape[1]
    tile = 2 * LANE
    for t in range(units // tile):
        at = slice(t * tile, (t + 1) * tile)
        gate = mxu(normed, wg[:, at], NN)
        up = mxu(normed, wu[:, at], NN)
        grad = mxu(og, wd[at], NT)
        sigmoid = 1.0 / (1.0 + jnp.exp(-gate))
        silu = gate * sigmoid
        act_ref[:, at] = (silu * up).astype(BF)
        gu_ref[:, at] = (grad * silu).astype(BF)
        gg_ref[:, at] = (grad * up * (sigmoid + silu * (1.0 - sigmoid))).astype(BF)
    result = mxu(act_ref[...], wd[...], NN)
    out_ref[0] = (hidden + result).astype(BF)
    grad_normed = mxu(gg_ref[...], wg[...], NT) + mxu(gu_ref[...], wu[...], NT)
    scaled = grad_normed * gain
    gg2_ref[...] += jnp.sum(grad_normed * (hidden * inverse), axis=0, keepdims=True)
    mean = jnp.mean(scaled * hidden, axis=-1, keepdims=True)
    grad_hidden = og.astype(F32) + inverse * scaled - hidden * (inverse * inverse * inverse * mean)
    gh_ref[0] = grad_hidden
    grad_attended = grad_hidden.astype(BF)
    gat_ref[...] = grad_attended.T
    grad_heads = mxu(wo[...], grad_attended, NT).astype(BF)
    do_ref[...] = grad_heads
    product = grad_heads.astype(F32) * heads_out.astype(F32)
    for h in range(product.shape[0] // HD):
        delta_ref[0, h : h + 1] = jnp.sum(product[h * HD : (h + 1) * HD], axis=0, keepdims=True)


def feed(x, og, heads_out, gain, wo, wg, wu, wd):
    count, own, width = x.shape
    hd = heads_out.shape[0]
    half = wg[0].shape[1]
    units = 2 * half
    tokens = count * own
    seq = pl.BlockSpec((1, own, width), lambda b: (b, 0, 0))
    column = lambda rows: pl.BlockSpec((rows, own), lambda b: (0, b))
    row = pl.BlockSpec((own, units), lambda b: (b, 0))
    hbm = pl.BlockSpec(memory_space=pl.ANY)
    return pl.pallas_call(
        feed_kernel,
        grid=(count,),
        in_specs=[seq, seq, column(hd), pl.BlockSpec((1, width), lambda b: (0, 0))] + [hbm] * 7,
        out_specs=[
            seq, column(width), column(width), row, row, row, seq, column(width), column(hd),
            pl.BlockSpec((1, hd // HD, own), lambda b: (b, 0, 0)),
            pl.BlockSpec((1, width), lambda b: (0, 0)),
        ],
        out_shape=[
            jax.ShapeDtypeStruct(x.shape, BF),
            jax.ShapeDtypeStruct((width, tokens), BF),
            jax.ShapeDtypeStruct((width, tokens), BF),
            jax.ShapeDtypeStruct((tokens, units), BF),
            jax.ShapeDtypeStruct((tokens, units), BF),
            jax.ShapeDtypeStruct((tokens, units), BF),
            jax.ShapeDtypeStruct(x.shape, F32),
            jax.ShapeDtypeStruct((width, tokens), BF),
            jax.ShapeDtypeStruct((hd, tokens), BF),
            jax.ShapeDtypeStruct((count, hd // HD, own), F32),
            jax.ShapeDtypeStruct((1, width), F32),
        ],
        scratch_shapes=[
            pltpu.VMEM((hd, width), BF),
            pltpu.VMEM((width, units), BF),
            pltpu.VMEM((width, units), BF),
            pltpu.VMEM((units, width), BF),
            pltpu.SemaphoreType.DMA((6 * (half // LANE) + 1,)),
        ],
        compiler_params=params(),
        name="feed",
    )(x, og, heads_out, gain, wo, *wg, *wu, *wd)


def unit_grads_kernel(left_ref, right_ref, own_ref, other_ref):
    product = mxu(left_ref[...], right_ref[...], NN).astype(BF)
    own_ref[...] = product[:, :LANE]
    other_ref[...] = product[:, LANE:]


def unit_grads(left, right):
    width, tokens = left.shape
    units = right.shape[1]
    tile = 2 * LANE
    part = pl.BlockSpec((width, LANE), lambda t: (0, t))
    return pl.pallas_call(
        unit_grads_kernel,
        grid=(units // tile,),
        in_specs=[
            pl.BlockSpec((width, tokens), lambda t: (0, 0)),
            pl.BlockSpec((tokens, tile), lambda t: (0, t)),
        ],
        out_specs=[part, part],
        out_shape=[jax.ShapeDtypeStruct((width, units // 2), BF)] * 2,
        compiler_params=params(),
        name="unit_grads",
    )(left, right)


def plain_grads_kernel(dims, left_ref, right_ref, out_ref):
    out_ref[...] = mxu(left_ref[...], right_ref[...], dims).astype(BF)


def plain_grads(left, right, dims):
    rows, tokens = left.shape
    columns = right.shape[1] if dims == NN else right.shape[0]
    tile = 2 * LANE
    if dims == NN:
        spec = pl.BlockSpec((tokens, tile), lambda t: (0, t))
    else:
        spec = pl.BlockSpec((tile, tokens), lambda t: (t, 0))
    return pl.pallas_call(
        functools.partial(plain_grads_kernel, dims),
        grid=(columns // tile,),
        in_specs=[pl.BlockSpec((rows, tokens), lambda t: (0, 0)), spec],
        out_specs=pl.BlockSpec((rows, tile), lambda t: (0, t)),
        out_shape=jax.ShapeDtypeStruct((rows, columns), BF),
        compiler_params=params(),
        name="plain_grads",
    )(left, right)


def finish_kernel(
    x_ref, gh_ref, dq_ref, dkv_ref, nt_ref, gain_ref, w_ref, cos_ref, sin_ref,
    gi_ref, gg1_ref, dw_ref,
):
    b = pl.program_id(0)

    @pl.when(b == 0)
    def _():
        gg1_ref[...] = jnp.zeros(gg1_ref.shape, F32)
        dw_ref[...] = jnp.zeros(dw_ref.shape, F32)

    rows = w_ref.shape[0]
    kv_rows = dkv_ref.shape[1]
    tied = kv_rows - RD
    summed = dkv_ref[0].astype(F32)
    turned = rotate_rows(summed[tied:], cos_ref[...], -sin_ref[...])
    dkv = jnp.concatenate([summed[:tied], turned], axis=0).astype(BF)
    grad_normed = mxu(dq_ref[...], w_ref[: rows - kv_rows], NN)
    grad_normed = grad_normed + mxu(dkv, w_ref[rows - kv_rows :], TN)
    dw_ref[...] += mxu(nt_ref[...], dkv, NT)
    x = x_ref[0].astype(F32)
    inverse = lax.rsqrt(jnp.mean(x * x, axis=-1, keepdims=True) + epsilon)
    scaled = grad_normed * gain_ref[...]
    gg1_ref[...] += jnp.sum(grad_normed * (x * inverse), axis=0, keepdims=True)
    mean = jnp.mean(scaled * x, axis=-1, keepdims=True)
    gi_ref[0] = gh_ref[0] + inverse * scaled - x * (inverse * inverse * inverse * mean)


def finish(x, grad_hidden, dq, dkv, nt, gain, weights, cosine, sine_table):
    count, own, width = x.shape
    kv_rows = dkv.shape[1]
    seq = pl.BlockSpec((1, own, width), lambda b: (b, 0, 0))
    whole = lambda b: (0, 0)
    return pl.pallas_call(
        finish_kernel,
        grid=(count,),
        in_specs=[
            seq, seq,
            pl.BlockSpec((own, dq.shape[1]), lambda b: (b, 0)),
            pl.BlockSpec((1, kv_rows, own), lambda b: (b, 0, 0)),
            pl.BlockSpec((width, own), lambda b: (0, b)),
            pl.BlockSpec((1, width), whole),
            pl.BlockSpec(weights.shape, whole),
            pl.BlockSpec(cosine.shape, whole),
            pl.BlockSpec(cosine.shape, whole),
        ],
        out_specs=[
            seq, pl.BlockSpec((1, width), whole), pl.BlockSpec((width, kv_rows), whole),
        ],
        out_shape=[
            jax.ShapeDtypeStruct(x.shape, F32),
            jax.ShapeDtypeStruct((1, width), F32),
            jax.ShapeDtypeStruct((width, kv_rows), F32),
        ],
        compiler_params=params(),
        name="finish",
    )(x, grad_hidden, dq, dkv, nt, gain, weights, cosine, sine_table)


def turn_tables(cosine, sine_table):
    plain = HD - RD
    one = jnp.ones((cosine.shape[0], plain), F32)
    none = jnp.zeros_like(one)
    quiet = jnp.zeros_like(sine_table)
    straight = jnp.concatenate([one, cosine, cosine], axis=1)
    ahead = jnp.concatenate([none, sine_table, quiet], axis=1)
    behind = jnp.concatenate([none, quiet, -sine_table], axis=1)
    return jnp.stack([jnp.concatenate([t, t], axis=1) for t in (straight, ahead, behind)])


def on_device_fast(
    inputs, gain_one, w_query, w_tied, w_rope, w_out, gain_two, w_gate, w_up, w_down,
    doc_starts, out_grad,
):
    count, own, width = inputs.shape
    cores = lax.axis_size("mp")
    groups = cores * w_tied.shape[1] // HD
    all_heads = cores * w_query.shape[1] // HD
    heads = all_heads // groups
    mp_index = lax.axis_index("mp")
    query_t, tied_t = w_query.T, w_tied.T
    tied_both = by_core(tied_t, swap_cores(tied_t), 0)
    query_both = by_core(query_t, swap_cores(query_t), 0)
    weights_one = jnp.concatenate([query_both, tied_both, w_rope.T], axis=0)
    out_other = swap_cores(w_out)
    gate_other, up_other, down_other = swap_cores(w_gate), swap_cores(w_up), swap_cores(w_down)
    gain_one_float = gain_one.astype(F32)[None]
    gain_two_float = gain_two.astype(F32)[None]
    cosine, sine_table = rope_tables(my_chunk() * own, own, RD)
    cosine_t, sine_t = cosine.T, sine_table.T
    q, kv, normed_t = project(inputs, gain_one_float, weights_one, cosine_t, sine_t, all_heads)
    kv_all = lax.all_gather(kv, ("seq", "mp"), axis=0, tiled=False)
    heads_out, lse = attend_forward(doc_starts, q, kv_all, groups, heads)
    out_both = by_core(w_out, out_other, 0)
    (
        outputs, normed_two_t, out_grad_t, active, grad_gate, grad_up, grad_hidden, grad_attended_t,
        grad_heads, delta, grad_gain_two,
    ) = feed(
        inputs, out_grad, heads_out, gain_two_float, out_both, (w_gate, gate_other),
        (w_up, up_other), (w_down, down_other),
    )
    unit_own, unit_other = [], []
    for left, right in (
        (normed_two_t, grad_gate), (normed_two_t, grad_up), (out_grad_t, active),
    ):
        own_part, other_part = unit_grads(left, right)
        unit_own.append(own_part)
        unit_other.append(swap_cores(other_part))
    unit_sum = jnp.concatenate([a + c for a, c in zip(unit_own, unit_other)], axis=1)
    unit_scattered = lax.psum_scatter(unit_sum, ("dp", "seq"), scatter_dimension=0, tiled=True)

    dq, dkv = attend_backward(
        doc_starts, q, grad_heads, lse, delta, kv_all, turn_tables(cosine, sine_table), groups, heads
    )
    dkv_own = lax.psum_scatter(dkv, ("seq", "mp"), scatter_dimension=0, tiled=False)
    grad_out = plain_grads(grad_attended_t, heads_out, NT)
    grad_query = plain_grads(normed_t, dq, NN)
    grad_inputs, grad_gain_one, grad_kv = finish(
        inputs, grad_hidden, dq, dkv_own, normed_t, gain_one_float, weights_one, cosine_t, sine_t
    )
    tied = groups * HD
    grad_tied = grad_kv[:, :tied].astype(BF)
    late_own, late_other = [], []
    for value in (grad_query, grad_tied, grad_out):
        half = value.shape[1] // cores
        late_own.append(lax.dynamic_slice_in_dim(value, mp_index * half, half, 1))
        late_other.append(lax.dynamic_slice_in_dim(value, (1 - mp_index) * half, half, 1))
    late = jnp.concatenate(late_own, axis=1) + swap_cores(jnp.concatenate(late_other, axis=1))
    late_sum = lax.psum_scatter(late, ("dp", "seq"), scatter_dimension=0, tiled=True)
    small = jnp.concatenate([grad_kv[:, tied:], grad_gain_one.T, grad_gain_two.T], axis=1)
    small_sum = lax.psum_scatter(small, ("dp", "seq", "mp"), scatter_dimension=0, tiled=True)
    unit_scattered = unit_scattered.astype(F32)
    late_sum = late_sum.astype(F32)
    half_units = w_gate.shape[1]
    query_half, tied_half = w_query.shape[1], w_tied.shape[1]
    return (
        outputs,
        grad_inputs,
        small_sum[:, RD],
        late_sum[:, :query_half],
        late_sum[:, query_half : query_half + tied_half],
        small_sum[:, :RD],
        late_sum[:, query_half + tied_half :].T,
        small_sum[:, RD + 1],
        unit_scattered[:, :half_units],
        unit_scattered[:, half_units : 2 * half_units],
        unit_scattered[:, 2 * half_units :].T,
    )


def solution(mesh):
    in_specs = (
        P("dp", ("seq", "mp"), None),
        P(),
        P(None, "mp"),
        P(None, "mp"),
        P(),
        P("mp", None),
        P(),
        P(None, "mp"),
        P(None, "mp"),
        P("mp", None),
        P("dp", None),
        P("dp", ("seq", "mp"), None),
    )
    out_specs = (
        P("dp", ("seq", "mp"), None),
        P("dp", ("seq", "mp"), None),
        P(("dp", "seq", "mp")),
        P(("dp", "seq"), "mp"),
        P(("dp", "seq"), "mp"),
        P(("dp", "seq", "mp"), None),
        P("mp", ("dp", "seq")),
        P(("dp", "seq", "mp")),
        P(("dp", "seq"), "mp"),
        P(("dp", "seq"), "mp"),
        P("mp", ("dp", "seq")),
    )

    def local(inputs, *rest):
        step = on_device_fast if inputs.shape[1] % (2 * LANE) == 0 else on_device
        return step(inputs, *rest)

    return jax.shard_map(
        local, mesh=mesh, in_specs=in_specs, out_specs=out_specs, check_vma=False
    )
```

```python
import functools

import jax
import jax.numpy as jnp
from jax import lax
from jax.experimental import pallas as pl
from jax.experimental.pallas import tpu as pltpu
from jax.sharding import PartitionSpec as P

HD = 64
RD = 32


epsilon = 1e-05
rope_base = 10000.0
masked_value = -1e30


def rope_tables(offset, count, rope_width):
    position = (offset + jnp.arange(count, dtype=jnp.int32)).astype(jnp.float32)
    frequency = rope_base ** (-jnp.arange(rope_width // 2, dtype=jnp.float32) * 2.0 / rope_width)
    angles = position[:, None] * frequency[None, :]
    return (jnp.cos(angles), jnp.sin(angles))


def rotate(values, cosine, sine_table):
    half_width = values.shape[-1] // 2
    first_half = values[..., :half_width]
    second_half = values[..., half_width:]
    return jnp.concatenate(
        [
            first_half * cosine - second_half * sine_table,
            second_half * cosine + first_half * sine_table,
        ],
        axis=-1,
    )


def rotate_back(grads, cosine, sine_table):
    half_width = grads.shape[-1] // 2
    first_half = grads[..., :half_width]
    second_half = grads[..., half_width:]
    return jnp.concatenate(
        [
            first_half * cosine + second_half * sine_table,
            second_half * cosine - first_half * sine_table,
        ],
        axis=-1,
    )


def contract_rows(left, right):
    return lax.dot_general(
        left, right, (((0,), (0,)), ((), ())), preferred_element_type=jnp.float32
    )


def times_transposed(left, right):
    return lax.dot_general(
        left, right, (((1,), (1,)), ((), ())), preferred_element_type=jnp.float32
    )


def norm_back(grad_normed, values, inverse, gain):
    scaled = grad_normed * gain
    grad_gain = jnp.sum(grad_normed * values * inverse, axis=(0, 1))
    grad_values = inverse * scaled - values * inverse**3 * jnp.mean(
        scaled * values, axis=-1, keepdims=True
    )
    return (grad_values, grad_gain)


def attend(operands):
    queries, key_full, values, allowed = operands
    scores = jnp.einsum(
        "qghd,kgd->ghqk", queries, key_full, preferred_element_type=jnp.float32
    ) * HD ** (-0.5)
    masked = jnp.where(allowed[None, None], scores, masked_value)
    row_max = jnp.max(masked, axis=-1, keepdims=True)
    weights = jnp.exp(masked - row_max)
    row_total = jnp.sum(weights, axis=-1, keepdims=True)
    attention_probs = (weights / row_total).astype(jnp.bfloat16)
    combined = jnp.einsum(
        "ghqk,kgd->qghd", attention_probs, values, preferred_element_type=jnp.float32
    )
    return (combined.astype(jnp.bfloat16), row_max + jnp.log(row_total))


def attend_back(operands):
    queries, key_full, values, allowed, log_total, grad_heads = operands
    score_scale = HD ** (-0.5)
    plain_width = HD - RD
    scores = (
        jnp.einsum("qghd,kgd->ghqk", queries, key_full, preferred_element_type=jnp.float32)
        * score_scale
    )
    masked = jnp.where(allowed[None, None], scores, masked_value)
    probs_float = jnp.exp(masked - log_total)
    grad_probs = jnp.einsum(
        "qghd,kgd->ghqk", grad_heads, values, preferred_element_type=jnp.float32
    )
    row_delta = jnp.sum(probs_float * grad_probs, axis=-1, keepdims=True)
    grad_scores = (probs_float * (grad_probs - row_delta)).astype(jnp.bfloat16)
    grad_queries = (
        jnp.einsum("ghqk,kgd->qghd", grad_scores, key_full, preferred_element_type=jnp.float32)
        * score_scale
    )
    grad_keys = (
        jnp.einsum("ghqk,qghd->kgd", grad_scores, queries, preferred_element_type=jnp.float32)
        * score_scale
    )
    grad_values = jnp.einsum(
        "ghqk,qghd->kgd",
        probs_float.astype(jnp.bfloat16),
        grad_heads,
        preferred_element_type=jnp.float32,
    )
    grad_tied = grad_values + jnp.concatenate(
        [grad_keys[..., :plain_width], jnp.zeros_like(grad_keys[..., plain_width:])], axis=-1
    )
    grad_rope = jnp.sum(grad_keys[..., plain_width:], axis=1)
    return (grad_queries, grad_tied, grad_rope)


def on_device(
    inputs,
    gain_one,
    w_query,
    w_tied,
    w_rope,
    w_out,
    gain_two,
    w_gate,
    w_up,
    w_down,
    doc_starts,
    out_grad,
):
    seq_count, own_count, model_width = inputs.shape
    plain_width = HD - RD
    group_local = w_tied.shape[1] // HD
    head_local = w_query.shape[1] // HD
    seq_index = lax.axis_index("seq")
    mp_index = lax.axis_index("mp")
    gain_one_float = gain_one.astype(jnp.float32)
    gain_two_float = gain_two.astype(jnp.float32)
    inputs_float = inputs.astype(jnp.float32)
    inverse_one = lax.rsqrt(jnp.mean(inputs_float * inputs_float, axis=-1, keepdims=True) + epsilon)
    normed_one = (inputs_float * inverse_one * gain_one_float).astype(jnp.bfloat16)
    gathered_one = lax.all_gather(normed_one, "mp", axis=1, tiled=True)
    context = gathered_one.shape[1]
    token_count = seq_count * context
    flat_one = gathered_one.reshape(token_count, model_width)
    offset = seq_index * context
    cosine, sine_table = rope_tables(offset, context, RD)
    query_lin = jnp.dot(flat_one, w_query, preferred_element_type=jnp.float32).reshape(
        seq_count, context, head_local, HD
    )
    queries = jnp.concatenate(
        [
            query_lin[..., :plain_width],
            rotate(
                query_lin[..., plain_width:], cosine[None, :, None, :], sine_table[None, :, None, :]
            ),
        ],
        axis=-1,
    ).astype(jnp.bfloat16)
    queries = queries.reshape(seq_count, context, group_local, head_local // group_local, HD)
    tied_state = (
        jnp.dot(flat_one, w_tied, preferred_element_type=jnp.float32)
        .astype(jnp.bfloat16)
        .reshape(seq_count, context, group_local * HD)
    )
    rope_lin = jnp.dot(flat_one, w_rope, preferred_element_type=jnp.float32).reshape(
        seq_count, context, RD
    )
    rope_keys = rotate(rope_lin, cosine[None], sine_table[None]).astype(jnp.bfloat16)
    tied_all, rope_all = (
        lax.all_gather(tied_state, "seq", axis=1, tiled=True),
        lax.all_gather(rope_keys, "seq", axis=1, tiled=True),
    )
    length = tied_all.shape[1]
    values_all = tied_all.reshape(seq_count, length, group_local, HD)
    key_full = jnp.concatenate(
        [
            values_all[..., :plain_width],
            jnp.broadcast_to(rope_all[:, :, None, :], (seq_count, length, group_local, RD)),
        ],
        axis=-1,
    )
    key_position = jnp.arange(length, dtype=jnp.int32)
    key_segment = jnp.sum(
        (doc_starts[:, None, :] <= key_position[None, :, None]).astype(jnp.int32), axis=-1
    )
    query_segment = lax.dynamic_slice_in_dim(key_segment, offset, context, 1)
    query_position = offset + jnp.arange(context, dtype=jnp.int32)
    allowed = (query_segment[:, :, None] == key_segment[:, None, :]) & (
        query_position[:, None] >= key_position[None, :]
    )[None]
    head_outputs, log_total = lax.map(attend, (queries, key_full, values_all, allowed))
    flat_heads = head_outputs.reshape(token_count, head_local * HD)
    attended_part = jnp.dot(flat_heads, w_out, preferred_element_type=jnp.float32).reshape(
        seq_count, context, model_width
    )
    attended = lax.psum_scatter(
        attended_part.astype(jnp.bfloat16), "mp", scatter_dimension=1, tiled=True
    ).astype(jnp.float32)
    hidden = inputs_float + attended
    inverse_two = lax.rsqrt(jnp.mean(hidden * hidden, axis=-1, keepdims=True) + epsilon)
    normed_two = (hidden * inverse_two * gain_two_float).astype(jnp.bfloat16)
    gathered_two = lax.all_gather(normed_two, "mp", axis=1, tiled=True)
    flat_two = gathered_two.reshape(token_count, model_width)
    gate_values = jnp.dot(flat_two, w_gate, preferred_element_type=jnp.float32)
    up_values = jnp.dot(flat_two, w_up, preferred_element_type=jnp.float32)
    sigmoid_gate = jax.nn.sigmoid(gate_values)
    silu_gate = gate_values * sigmoid_gate
    active = (silu_gate * up_values).astype(jnp.bfloat16)
    result_part = jnp.dot(active, w_down, preferred_element_type=jnp.float32).reshape(
        seq_count, context, model_width
    )
    result = lax.psum_scatter(
        result_part.astype(jnp.bfloat16), "mp", scatter_dimension=1, tiled=True
    ).astype(jnp.float32)
    outputs = (hidden + result).astype(jnp.bfloat16)
    grad_out_all = lax.all_gather(out_grad, "mp", axis=1, tiled=True)
    flat_grad = grad_out_all.reshape(token_count, model_width)
    grad_active = times_transposed(flat_grad, w_down)
    grad_w_down = contract_rows(active, flat_grad)
    grad_gate = (
        grad_active * up_values * sigmoid_gate * (1.0 + gate_values * (1.0 - sigmoid_gate))
    ).astype(jnp.bfloat16)
    grad_up = (grad_active * silu_gate).astype(jnp.bfloat16)
    grad_w_gate = contract_rows(flat_two, grad_gate)
    grad_w_up = contract_rows(flat_two, grad_up)
    grad_two_part = (times_transposed(grad_gate, w_gate) + times_transposed(grad_up, w_up)).reshape(
        seq_count, context, model_width
    )
    grad_normed_two = lax.psum_scatter(
        grad_two_part.astype(jnp.bfloat16), "mp", scatter_dimension=1, tiled=True
    ).astype(jnp.float32)
    grad_hidden_norm, grad_gain_two = norm_back(
        grad_normed_two, hidden, inverse_two, gain_two_float
    )
    grad_hidden = out_grad.astype(jnp.float32) + grad_hidden_norm
    grad_attended_all = lax.all_gather(grad_hidden.astype(jnp.bfloat16), "mp", axis=1, tiled=True)
    flat_attended = grad_attended_all.reshape(token_count, model_width)
    grad_w_out = contract_rows(flat_heads, flat_attended)
    grad_heads = times_transposed(flat_attended, w_out).astype(jnp.bfloat16).reshape(queries.shape)
    grad_queries, grad_tied, grad_rope = lax.map(
        attend_back, (queries, key_full, values_all, allowed, log_total, grad_heads)
    )
    grad_queries = grad_queries.reshape(seq_count, context, head_local, HD)
    grad_query_lin = (
        jnp.concatenate(
            [
                grad_queries[..., :plain_width],
                rotate_back(
                    grad_queries[..., plain_width:],
                    cosine[None, :, None, :],
                    sine_table[None, :, None, :],
                ),
            ],
            axis=-1,
        )
        .astype(jnp.bfloat16)
        .reshape(token_count, head_local * HD)
    )
    tied_own, rope_context = (
        lax.psum_scatter(
            grad_tied.reshape(seq_count, length, group_local * HD).astype(jnp.bfloat16),
            "seq",
            scatter_dimension=1,
            tiled=True,
        ).astype(jnp.float32),
        lax.psum_scatter(
            grad_rope.astype(jnp.bfloat16), "seq", scatter_dimension=1, tiled=True
        ).astype(jnp.float32),
    )
    grad_tied_flat = tied_own.astype(jnp.bfloat16).reshape(token_count, group_local * HD)
    grad_one_part = (
        times_transposed(grad_query_lin, w_query) + times_transposed(grad_tied_flat, w_tied)
    ).reshape(seq_count, context, model_width)
    grad_normed_one, rope_own = (
        lax.psum_scatter(
            grad_one_part.astype(jnp.bfloat16), "mp", scatter_dimension=1, tiled=True
        ).astype(jnp.float32),
        lax.psum_scatter(
            rope_context.astype(jnp.bfloat16), "mp", scatter_dimension=1, tiled=True
        ).astype(jnp.float32),
    )
    own_offset = offset + mp_index * own_count
    cosine_own, sine_own = rope_tables(own_offset, own_count, RD)
    grad_rope_flat = (
        rotate_back(rope_own, cosine_own[None], sine_own[None])
        .astype(jnp.bfloat16)
        .reshape(seq_count * own_count, RD)
    )
    grad_normed_one = grad_normed_one + times_transposed(grad_rope_flat, w_rope).reshape(
        seq_count, own_count, model_width
    )
    grad_w_rope = contract_rows(
        normed_one.reshape(seq_count * own_count, model_width), grad_rope_flat
    )
    grad_w_query = contract_rows(flat_one, grad_query_lin)
    grad_w_tied = contract_rows(flat_one, grad_tied_flat)
    grad_inputs_norm, grad_gain_one = norm_back(
        grad_normed_one, inputs_float, inverse_one, gain_one_float
    )
    grad_inputs = grad_hidden + grad_inputs_norm
    small_sums = (
        lax.psum_scatter(grad_gain_one, ("dp", "seq", "mp"), scatter_dimension=0, tiled=True),
        lax.psum_scatter(grad_w_rope, ("dp", "seq", "mp"), scatter_dimension=0, tiled=True),
        lax.psum_scatter(grad_gain_two, ("dp", "seq", "mp"), scatter_dimension=0, tiled=True),
    )
    weight_terms = (grad_w_query, grad_w_tied, grad_w_out, grad_w_gate, grad_w_up, grad_w_down)
    weight_sums = (
        lax.psum_scatter(weight_terms[0], ("dp", "seq"), scatter_dimension=0, tiled=True),
        lax.psum_scatter(weight_terms[1], ("dp", "seq"), scatter_dimension=0, tiled=True),
        lax.psum_scatter(weight_terms[2], ("dp", "seq"), scatter_dimension=1, tiled=True),
        lax.psum_scatter(weight_terms[3], ("dp", "seq"), scatter_dimension=0, tiled=True),
        lax.psum_scatter(weight_terms[4], ("dp", "seq"), scatter_dimension=0, tiled=True),
        lax.psum_scatter(weight_terms[5], ("dp", "seq"), scatter_dimension=1, tiled=True),
    )
    return (
        outputs,
        grad_inputs,
        small_sums[0],
        weight_sums[0],
        weight_sums[1],
        small_sums[1],
        weight_sums[2],
        small_sums[2],
        weight_sums[3],
        weight_sums[4],
        weight_sums[5],
    )


BF = jnp.bfloat16
F32 = jnp.float32
NN = (((1,), (0,)), ((), ()))
NT = (((1,), (1,)), ((), ()))
TN = (((0,), (0,)), ((), ()))
BIG = 2.0**100
MIB = 1 << 20
LANE = 128


def mxu(left, right, dims):
    return lax.dot_general(left, right, dims, preferred_element_type=F32)


def params(limit=56):
    return pltpu.CompilerParams(vmem_limit_bytes=limit * MIB)


def cost(flops, moved=0):
    return pl.CostEstimate(flops=int(flops), bytes_accessed=int(moved), transcendentals=0)


def swap_cores(value):
    return lax.ppermute(value, "mp", [(0, 1), (1, 0)])


def shift(value, axis, by):
    size = lax.axis_size(axis)
    return lax.ppermute(value, axis, [(i, (i + by) % size) for i in range(size)])


def gather_keys(kv):
    near = [kv] + [shift(kv, "seq", k) for k in range(1, lax.axis_size("seq"))]
    return near + [swap_cores(value) for value in near]


def by_core(own, other, axis):
    first = lax.axis_index("mp") == 0
    return jnp.concatenate(
        [jnp.where(first, own, other), jnp.where(first, other, own)], axis=axis
    )


def rotate_rows(values, cosine, sine_table):
    half = values.shape[0] // 2
    a, b = values[:half], values[half:]
    return jnp.concatenate([a * cosine - b * sine_table, b * cosine + a * sine_table], axis=0)


def keys_kernel(x_ref, gain_ref, w_ref, cos_ref, sin_ref, kv_ref, nt_ref):
    x = x_ref[0].astype(F32)
    inverse = lax.rsqrt(jnp.mean(x * x, axis=-1, keepdims=True) + epsilon)
    normed = (x * inverse * gain_ref[...]).astype(BF)
    nt_ref[...] = normed.T
    lin = mxu(w_ref[...], normed, NT)
    tied = w_ref.shape[0] - RD
    kv_ref[0, :tied] = lin[:tied].astype(BF)
    kv_ref[0, tied:] = rotate_rows(lin[tied:], cos_ref[...], sin_ref[...]).astype(BF)


def project_keys(x, gain, weights, cosine, sine_table):
    count, own, width = x.shape
    rows = weights.shape[0]
    whole = lambda b: (0, 0)
    return pl.pallas_call(
        keys_kernel,
        grid=(count,),
        in_specs=[
            pl.BlockSpec((1, own, width), lambda b: (b, 0, 0)),
            pl.BlockSpec((1, width), whole),
            pl.BlockSpec((rows, width), whole),
            pl.BlockSpec(cosine.shape, whole),
            pl.BlockSpec(cosine.shape, whole),
        ],
        out_specs=[
            pl.BlockSpec((1, rows, own), lambda b: (b, 0, 0)),
            pl.BlockSpec((width, own), lambda b: (0, b)),
        ],
        out_shape=[
            jax.ShapeDtypeStruct((count, rows, own), BF),
            jax.ShapeDtypeStruct((width, count * own), BF),
        ],
        compiler_params=params(),
        cost_estimate=cost(2 * x.size * rows, 4 * x.size),
        name="project_keys",
    )(x, gain, weights, cosine, sine_table)


def queries_kernel(nt_ref, w_ref, cos_ref, sin_ref, q_ref):
    lin = mxu(w_ref[...], nt_ref[...], NN)
    cosine, sine_table = cos_ref[...], sin_ref[...]
    plain = HD - RD
    pieces = []
    for at in range(0, lin.shape[0], HD):
        pieces.append(lin[at : at + plain])
        pieces.append(rotate_rows(lin[at + plain : at + HD], cosine, sine_table))
    queries = jnp.concatenate(pieces, axis=0)
    q_ref[...] = (queries.astype(BF) * HD ** (-0.5)).astype(BF)


def project_queries(normed_t, weights, cosine, sine_table):
    width, tokens = normed_t.shape
    rows, own = weights.shape[0], cosine.shape[1]
    whole = lambda b: (0, 0)
    return pl.pallas_call(
        queries_kernel,
        grid=(tokens // own,),
        in_specs=[
            pl.BlockSpec((width, own), lambda b: (0, b)),
            pl.BlockSpec((rows, width), whole),
            pl.BlockSpec(cosine.shape, whole),
            pl.BlockSpec(cosine.shape, whole),
        ],
        out_specs=pl.BlockSpec((rows, own), lambda b: (0, b)),
        out_shape=jax.ShapeDtypeStruct((rows, tokens), BF),
        compiler_params=params(),
        cost_estimate=cost(2 * normed_t.size * rows, 4 * normed_t.size),
        name="project_queries",
    )(normed_t, weights, cosine, sine_table)


def segment_counts(starts, first, width):
    position = first + lax.broadcasted_iota(jnp.int32, (1, width), 1)
    count = jnp.zeros((1, width), jnp.int32)
    for start in starts:
        count = count + (start <= position).astype(jnp.int32)
    return count


def query_rows(starts, first, width):
    row = lax.broadcasted_iota(jnp.int32, (16, width), 0)
    match = segment_counts(starts, first, width) == row + 1
    return jnp.where(match, 1.0, 0.0).astype(BF)


def key_rows(starts, first, width):
    row = lax.broadcasted_iota(jnp.int32, (16, width), 0)
    match = (segment_counts(starts, first, width) == row + 1) | (row >= len(starts))
    return jnp.where(match, 0.0, -BIG).astype(BF)


def first_rows(count, width):
    row = lax.broadcasted_iota(jnp.int32, (16, width), 0)
    return jnp.where(row < count, 1.0, 0.0).astype(BF)


def three_parts(row, width):
    high = row.astype(BF)
    rest = row - high.astype(F32)
    middle = rest.astype(BF)
    low = (rest - middle.astype(F32)).astype(BF)
    at = lax.broadcasted_iota(jnp.int32, (16, width), 0)
    parts = jnp.where(at == 0, high.astype(F32), 0.0)
    parts = jnp.where(at == 1, middle.astype(F32), parts)
    return jnp.where(at == 2, low.astype(F32), parts).astype(BF)


def start_chunk(starts, first, chunk):
    begin = jnp.int32(0)
    for start in starts:
        begin = jnp.where(start <= first, jnp.maximum(begin, start), begin)
    return begin // chunk


def my_chunk():
    return lax.axis_index("seq") * lax.axis_size("mp") + lax.axis_index("mp")


def place_keys(refs, kv, begin, me):
    steps = len(refs) // 2
    seq, core = lax.axis_index("seq"), lax.axis_index("mp")
    for at, ref in enumerate(refs):
        of = core if at < steps else 1 - core
        j = lax.rem(seq - at % steps + steps, steps) * 2 + of

        @pl.when((j >= begin) & (j <= me))
        def _():
            kv[j] = ref[0]


def stack_heads(value, at, heads):
    return jnp.concatenate([value[at + h * HD : at + (h + 1) * HD] for h in range(heads)], axis=1)


def attend_kernel(groups, heads, first, chunks, docs_ref, q_ref, *refs):
    kv_refs = refs[:chunks]
    out_ref, lse_ref, kv_ref, qa, acc, top = refs[-6:]
    b = pl.program_id(0) + first
    own = q_ref.shape[1]
    ndoc = docs_ref.shape[1]
    starts = [docs_ref[b, k] for k in range(ndoc)]
    me = my_chunk()
    begin = start_chunk(starts, me * own, own)
    place_keys(kv_refs, kv_ref, begin, me)
    wide = heads * own
    tied = groups * HD
    plain = HD - RD
    q_doc = query_rows(starts, me * own, own)
    q_doc = jnp.concatenate([q_doc] * heads, axis=1)
    q_all = q_ref[...]
    for g in range(groups):
        qa[g, :HD] = stack_heads(q_all, g * heads * HD, heads)
        qa[g, HD : HD + 16] = q_doc
        qa[g, HD + 16 :] = jnp.zeros((LANE - HD - 16, wide), BF)
    ones = first_rows(1, own)
    zeros = jnp.zeros((LANE - HD - 16, own), BF)

    def scores(j, g):
        doc = key_rows(starts, j * own, own)
        block = jnp.concatenate(
            [
                kv_ref[j, g * HD : g * HD + plain],
                kv_ref[j, tied : tied + RD],
                doc,
                zeros,
            ],
            axis=0,
        )
        return mxu(block.T, qa[g], NN)

    def weighted(j, g, weights):
        values = jnp.concatenate([kv_ref[j, g * HD : (g + 1) * HD], ones], axis=0)
        return mxu(values, weights.astype(BF), NN)

    key_at = lax.broadcasted_iota(jnp.int32, (own, own), 0)
    query_at = lax.broadcasted_iota(jnp.int32, (own, own), 1)
    causal = jnp.concatenate([key_at <= query_at] * heads, axis=1)
    for g in range(groups):
        logits = jnp.where(causal, scores(me, g), masked_value)
        peak = jnp.max(logits, axis=0, keepdims=True)
        acc[g] = weighted(me, g, jnp.exp(logits - peak))
        top[g] = peak

    def step(i, carry):
        j = me - 1 - i
        for g in range(groups):
            logits = scores(j, g)
            peak = jnp.maximum(top[g], jnp.max(logits, axis=0, keepdims=True))
            shrink = jnp.exp(top[g] - peak)
            acc[g] = acc[g] * shrink + weighted(j, g, jnp.exp(logits - peak))
            top[g] = peak
        return carry

    lax.fori_loop(0, me - begin, step, 0)
    for g in range(groups):
        total = acc[g, HD : HD + 1]
        result = acc[g, :HD] / total
        lse_ref[0, g : g + 1] = top[g] + jnp.log(total)
        for h in range(heads):
            at = (g * heads + h) * HD
            out_ref[at : at + HD] = result[:, h * own : (h + 1) * own].astype(BF)


def attend_forward(docs, q, kv, groups, heads, first, into):
    size, kv_rows, own = kv[0].shape
    count, chunks = docs.shape[0], len(kv)
    wide = heads * own
    hbm = pl.BlockSpec(memory_space=pl.ANY)
    return pl.pallas_call(
        functools.partial(attend_kernel, groups, heads, first, chunks),
        grid=(size,),
        in_specs=[
            pl.BlockSpec(memory_space=pltpu.SMEM),
            pl.BlockSpec((q.shape[0], own), lambda b: (0, b + first)),
        ]
        + [pl.BlockSpec((1, kv_rows, own), lambda b: (b, 0, 0))] * chunks
        + [hbm] * len(into),
        out_specs=[
            pl.BlockSpec((q.shape[0], own), lambda b: (0, b + first)),
            pl.BlockSpec((1, groups, wide), lambda b: (b + first, 0, 0)),
        ],
        out_shape=[
            jax.ShapeDtypeStruct(q.shape, BF),
            jax.ShapeDtypeStruct((count, groups, wide), F32),
        ],
        scratch_shapes=[
            pltpu.VMEM((chunks, kv_rows, own), BF),
            pltpu.VMEM((groups, LANE, wide), BF),
            pltpu.VMEM((groups, HD + 16, wide), F32),
            pltpu.VMEM((groups, 1, wide), F32),
        ],
        input_output_aliases={2 + chunks + i: i for i in range(len(into))},
        compiler_params=params(),
        cost_estimate=cost(10**10 * size),
        name="attend",
    )(docs, q, *kv, *into)


def attend_back_kernel(
    groups, heads, first, chunks, docs_ref, q_ref, do_ref, lse_ref, delta_ref, rot_ref, *refs
):
    kv_refs = refs[:chunks]
    dq_ref, keep_ref, give_ref, kv_ref, stage, qs, qa, ds_, da, dq = refs[-10:]
    b = pl.program_id(0) + first
    own = q_ref.shape[1]
    ndoc = docs_ref.shape[1]
    starts = [docs_ref[b, k] for k in range(ndoc)]
    me = my_chunk()
    begin = start_chunk(starts, me * own, own)
    place_keys(kv_refs, kv_ref, begin, me)
    wide = heads * own
    tied = groups * HD
    plain = HD - RD
    q_doc = query_rows(starts, me * own, own)
    q_doc = jnp.concatenate([q_doc] * heads, axis=1)
    q_all, do_all = q_ref[...], do_ref[...]
    pad_q = jnp.zeros((LANE - HD - 32, wide), BF)
    pad_d = jnp.zeros((LANE - HD - 16, wide), BF)
    row_at = lax.broadcasted_iota(jnp.int32, (own, own), 0)
    column_at = lax.broadcasted_iota(jnp.int32, (own, own), 1)
    identity = jnp.where(row_at == column_at, 1.0, 0.0).astype(BF)

    def turn(rows, ref):
        for h in range(0, heads, 2):
            pair = [rows[:, (h + i) * own : (h + i + 1) * own] for i in range(2)]
            turned = mxu(identity, jnp.concatenate(pair, axis=0), NT).astype(BF)
            ref[h * own : (h + 1) * own] = turned[:, :LANE]
            ref[(h + 1) * own : (h + 2) * own] = turned[:, LANE:]

    for g in range(groups):
        q_rows = stack_heads(q_all, g * heads * HD, heads)
        do_rows = stack_heads(do_all, g * heads * HD, heads)
        qs[g] = q_rows
        ds_[g] = do_rows
        lse_rows = three_parts(-lse_ref[0, g : g + 1], wide)
        delta_row = jnp.concatenate(
            [delta_ref[0, g * heads + h : g * heads + h + 1] for h in range(heads)], axis=1
        )
        delta_rows = three_parts(-delta_row, wide)
        turn(jnp.concatenate([q_rows, q_doc, lse_rows, pad_q], axis=0), qa.at[g])
        turn(jnp.concatenate([do_rows, delta_rows, pad_d], axis=0), da.at[g])
    ones = first_rows(3, own)
    pad_k = jnp.zeros((LANE - HD - 32, own), BF)
    pad_v = jnp.zeros((LANE - HD - 16, own), BF)

    seq, core = lax.axis_index("seq"), lax.axis_index("mp")
    steps = chunks // 2

    def deliver(j, value):
        k = lax.rem(j // 2 - seq + steps, steps)

        @pl.when(lax.rem(j, 2) == core)
        def _():
            keep_ref[k, 0] = value()

        @pl.when(lax.rem(j, 2) != core)
        def _():
            give_ref[k, 0] = value()

    def clear(j, carry):
        deliver(j, lambda: jnp.zeros(keep_ref.shape[2:], BF))
        return carry

    lax.fori_loop(0, begin, clear, 0)
    lax.fori_loop(me + 1, chunks, clear, 0)

    def block(j, diagonal):
        doc = key_rows(starts, j * own, own)
        rope_rows = kv_ref[j, tied : tied + RD]
        rope_sum = jnp.zeros((RD, own), F32)
        for g in range(groups):
            values = kv_ref[j, g * HD : (g + 1) * HD]
            keys = jnp.concatenate([values[:plain], rope_rows], axis=0)
            logits = mxu(qa[g], jnp.concatenate([keys, doc, ones, pad_k], axis=0), NN)
            weights = jnp.exp(logits)
            if diagonal:
                query_at = lax.broadcasted_iota(jnp.int32, (own, own), 0)
                key_at = lax.broadcasted_iota(jnp.int32, (own, own), 1)
                causal = jnp.concatenate([key_at <= query_at] * heads, axis=0)
                weights = jnp.where(causal, weights, 0.0)
            slopes = mxu(da[g], jnp.concatenate([values, ones, pad_v], axis=0), NN)
            grads = (weights * slopes).astype(BF)
            grad_values = mxu(ds_[g], weights.astype(BF), NN)
            grad_keys = mxu(qs[g], grads, NN)
            grad_queries = mxu(grads, keys.T, NN)
            if diagonal:
                dq[g] = grad_queries
            else:
                dq[g] += grad_queries
            stage[g * HD : g * HD + plain] = (
                grad_values[:plain] + grad_keys[:plain]
            ).astype(BF)
            stage[g * HD + plain : (g + 1) * HD] = grad_values[plain:].astype(BF)
            rope_sum = rope_sum + grad_keys[plain:]
        stage[tied : tied + RD] = rope_sum.astype(BF)
        deliver(j, lambda: stage[...])

    block(me, True)

    def step(j, carry):
        block(j, False)
        return carry

    lax.fori_loop(begin, me, step, 0)
    straight, ahead, behind = rot_ref[0], rot_ref[1], rot_ref[2]
    half = RD // 2
    for g in range(groups):
        for pair in range(heads // 2):
            at = 2 * pair * own
            both = jnp.concatenate([dq[g, at : at + own], dq[g, at + own : at + 2 * own]], axis=1)
            both = both * HD ** (-0.5)
            turned = (
                both * straight
                + pltpu.roll(both, LANE - half, 1) * ahead
                + pltpu.roll(both, half, 1) * behind
            )
            to = (g * heads + 2 * pair) * HD
            dq_ref[:, to : to + 2 * HD] = turned.astype(BF)


def attend_backward(docs, q, do, lse, delta, turns, kv, groups, heads, first, into):
    size, kv_rows, own = kv[0].shape
    count, chunks = docs.shape[0], len(kv)
    wide = heads * own
    width = q.shape[0]
    column = pl.BlockSpec((width, own), lambda b: (0, b + first))
    hbm = pl.BlockSpec(memory_space=pl.ANY)
    return pl.pallas_call(
        functools.partial(attend_back_kernel, groups, heads, first, chunks),
        grid=(size,),
        in_specs=[
            pl.BlockSpec(memory_space=pltpu.SMEM),
            column,
            column,
            pl.BlockSpec((1, groups, wide), lambda b: (b + first, 0, 0)),
            pl.BlockSpec((1, groups * heads, own), lambda b: (b + first, 0, 0)),
            pl.BlockSpec(turns.shape, lambda b: (0, 0, 0)),
        ]
        + [pl.BlockSpec((1, kv_rows, own), lambda b: (b, 0, 0))] * chunks
        + [hbm] * len(into),
        out_specs=[
            pl.BlockSpec((own, width), lambda b: (b + first, 0)),
            pl.BlockSpec((chunks // 2, 1, kv_rows, own), lambda b: (0, b, 0, 0)),
            pl.BlockSpec((chunks // 2, 1, kv_rows, own), lambda b: (0, b, 0, 0)),
        ],
        out_shape=[
            jax.ShapeDtypeStruct((count * own, width), BF),
            jax.ShapeDtypeStruct((chunks // 2, size, kv_rows, own), BF),
            jax.ShapeDtypeStruct((chunks // 2, size, kv_rows, own), BF),
        ],
        scratch_shapes=[
            pltpu.VMEM((chunks, kv_rows, own), BF),
            pltpu.VMEM((kv_rows, own), BF),
            pltpu.VMEM((groups, HD, wide), BF),
            pltpu.VMEM((groups, wide, LANE), BF),
            pltpu.VMEM((groups, HD, wide), BF),
            pltpu.VMEM((groups, wide, LANE), BF),
            pltpu.VMEM((groups, wide, HD), F32),
        ],
        input_output_aliases={6 + chunks + i: i for i in range(len(into))},
        compiler_params=params(),
        cost_estimate=cost(15 * 10**9 * size),
        name="attend_back",
    )(docs, q, do, lse, delta, turns, *kv, *into)


def join_cores(keep, give):
    received = swap_cores(give)
    return [
        (keep[k].astype(F32) + received[k].astype(F32)).astype(BF) for k in range(keep.shape[0])
    ]


def send_keys(summed):
    return [summed[0]] + [shift(summed[k], "seq", k) for k in range(1, len(summed))]


def load_weights(refs, targets, sems):
    copies = []
    slot = 0
    for (source, side, axis), target in zip(refs, targets, strict=True):
        blocks = source.shape[axis] // LANE
        for t in range(blocks):
            to = pl.ds((2 * t + side) * LANE, LANE)
            of = pl.ds(t * LANE, LANE)
            src = source.at[:, of] if axis == 1 else source.at[of]
            dst = target.at[:, to] if axis == 1 else target.at[to]
            copies.append(pltpu.make_async_copy(src, dst, sems.at[slot]))
            slot += 1
    return copies


def slopes_kernel(og_ref, wdo_ref, wdp_ref, out_ref, wd, sems):
    @pl.when(pl.program_id(0) == 0)
    def _():
        copies = load_weights([(wdo_ref, 0, 0), (wdp_ref, 1, 0)], [wd, wd], sems)
        for copy in copies:
            copy.start()
        for copy in copies:
            copy.wait()

    og = og_ref[0]
    for at in range(0, wd.shape[0], 2 * LANE):
        to = slice(at, at + 2 * LANE)
        out_ref[:, to] = mxu(og, wd[to], NT).astype(BF)


def unit_slopes(og, wd):
    count, own, width = og.shape
    half = wd[0].shape[0]
    hbm = pl.BlockSpec(memory_space=pl.ANY)
    return pl.pallas_call(
        slopes_kernel,
        grid=(count,),
        in_specs=[pl.BlockSpec((1, own, width), lambda b: (b, 0, 0)), hbm, hbm],
        out_specs=pl.BlockSpec((own, 2 * half), lambda b: (b, 0)),
        out_shape=jax.ShapeDtypeStruct((count * own, 2 * half), BF),
        scratch_shapes=[
            pltpu.VMEM((2 * half, width), BF),
            pltpu.SemaphoreType.DMA((2 * (half // LANE),)),
        ],
        compiler_params=params(),
        cost_estimate=cost(4 * og.size * half),
        name="unit_slopes",
    )(og, *wd)


def feed_kernel(
    x_ref, og_ref, ga_ref, o_ref, gain_ref, wo_ref, wgo_ref, wgp_ref, wuo_ref, wup_ref, wdo_ref, wdp_ref,
    out_ref, nt_ref, ogt_ref, act_ref, gg_ref, gu_ref, gh_ref, gat_ref, do_ref, delta_ref, gg2_ref,
    wo, wg, wu, wd, sems,
):
    b = pl.program_id(0)

    @pl.when(b == 0)
    def _():
        copies = [pltpu.make_async_copy(wo_ref, wo, sems.at[sems.shape[0] - 1])]
        copies += load_weights(
            [
                (wgo_ref, 0, 1), (wgp_ref, 1, 1), (wuo_ref, 0, 1), (wup_ref, 1, 1),
                (wdo_ref, 0, 0), (wdp_ref, 1, 0),
            ],
            [wg, wg, wu, wu, wd, wd],
            sems,
        )
        for copy in copies:
            copy.start()
        for copy in copies:
            copy.wait()
        gg2_ref[...] = jnp.zeros(gg2_ref.shape, F32)

    og = og_ref[0]
    heads_out = o_ref[...]
    gain = gain_ref[...]
    hidden = x_ref[0].astype(F32) + mxu(heads_out, wo[...], TN)
    inverse = lax.rsqrt(jnp.mean(hidden * hidden, axis=-1, keepdims=True) + epsilon)
    normed = (hidden * inverse * gain).astype(BF)
    nt_ref[...] = normed.T
    ogt_ref[...] = og.T
    units = wg.shape[1]
    tile = 2 * LANE
    for t in range(units // tile):
        at = slice(t * tile, (t + 1) * tile)
        gate = mxu(normed, wg[:, at], NN)
        up = mxu(normed, wu[:, at], NN)
        grad = ga_ref[:, at].astype(F32)
        sigmoid = 1.0 / (1.0 + jnp.exp(-gate))
        silu = gate * sigmoid
        act_ref[:, at] = (silu * up).astype(BF)
        gu_ref[:, at] = (grad * silu).astype(BF)
        gg_ref[:, at] = (grad * up * (sigmoid + silu * (1.0 - sigmoid))).astype(BF)
    result = mxu(act_ref[...], wd[...], NN)
    out_ref[0] = (hidden + result).astype(BF)
    grad_normed = mxu(gg_ref[...], wg[...], NT) + mxu(gu_ref[...], wu[...], NT)
    scaled = grad_normed * gain
    gg2_ref[...] += jnp.sum(grad_normed * (hidden * inverse), axis=0, keepdims=True)
    mean = jnp.mean(scaled * hidden, axis=-1, keepdims=True)
    grad_hidden = og.astype(F32) + inverse * scaled - hidden * (inverse * inverse * inverse * mean)
    gh_ref[0] = grad_hidden
    grad_attended = grad_hidden.astype(BF)
    gat_ref[...] = grad_attended.T
    grad_heads = mxu(wo[...], grad_attended, NT).astype(BF)
    do_ref[...] = grad_heads
    product = grad_heads.astype(F32) * heads_out.astype(F32)
    for h in range(product.shape[0] // HD):
        delta_ref[0, h : h + 1] = jnp.sum(product[h * HD : (h + 1) * HD], axis=0, keepdims=True)


def feed(x, og, slopes, heads_out, gain, wo, wg, wu, wd):
    count, own, width = x.shape
    hd = heads_out.shape[0]
    half = wg[0].shape[1]
    units = 2 * half
    tokens = count * own
    seq = pl.BlockSpec((1, own, width), lambda b: (b, 0, 0))
    column = lambda rows: pl.BlockSpec((rows, own), lambda b: (0, b))
    row = pl.BlockSpec((own, units), lambda b: (b, 0))
    hbm = pl.BlockSpec(memory_space=pl.ANY)
    return pl.pallas_call(
        feed_kernel,
        grid=(count,),
        in_specs=[seq, seq, row, column(hd), pl.BlockSpec((1, width), lambda b: (0, 0))] + [hbm] * 7,
        out_specs=[
            seq, column(width), column(width), row, row, row, seq, column(width), column(hd),
            pl.BlockSpec((1, hd // HD, own), lambda b: (b, 0, 0)),
            pl.BlockSpec((1, width), lambda b: (0, 0)),
        ],
        out_shape=[
            jax.ShapeDtypeStruct(x.shape, BF),
            jax.ShapeDtypeStruct((width, tokens), BF),
            jax.ShapeDtypeStruct((width, tokens), BF),
            jax.ShapeDtypeStruct((tokens, units), BF),
            jax.ShapeDtypeStruct((tokens, units), BF),
            jax.ShapeDtypeStruct((tokens, units), BF),
            jax.ShapeDtypeStruct(x.shape, F32),
            jax.ShapeDtypeStruct((width, tokens), BF),
            jax.ShapeDtypeStruct((hd, tokens), BF),
            jax.ShapeDtypeStruct((count, hd // HD, own), F32),
            jax.ShapeDtypeStruct((1, width), F32),
        ],
        scratch_shapes=[
            pltpu.VMEM((hd, width), BF),
            pltpu.VMEM((width, units), BF),
            pltpu.VMEM((width, units), BF),
            pltpu.VMEM((units, width), BF),
            pltpu.SemaphoreType.DMA((6 * (half // LANE) + 1,)),
        ],
        compiler_params=params(),
        cost_estimate=cost(2 * tokens * width * (5 * units + 2 * hd)),
        name="feed",
    )(x, og, slopes, heads_out, gain, wo, *wg, *wu, *wd)


def regroup_rows(value, split):
    if split is None:
        return value
    count_d, count_s = split
    own = value.shape[0] // (count_d * count_s)
    return jnp.concatenate(
        [
            value[(d * count_s + s) * own : (d * count_s + s + 1) * own]
            for s in range(count_s)
            for d in range(count_d)
        ],
        axis=0,
    )


def unit_grads_kernel(split, left_ref, right_ref, own_ref, other_ref):
    product = regroup_rows(mxu(left_ref[...], right_ref[...], NN), split).astype(BF)
    own_ref[...] = product[:, :LANE]
    other_ref[...] = product[:, LANE:]


def unit_grads(left, right, split):
    width, tokens = left.shape
    units = right.shape[1]
    tile = 2 * LANE
    part = pl.BlockSpec((width, LANE), lambda t: (0, t))
    return pl.pallas_call(
        functools.partial(unit_grads_kernel, split),
        grid=(units // tile,),
        in_specs=[
            pl.BlockSpec((width, tokens), lambda t: (0, 0)),
            pl.BlockSpec((tokens, tile), lambda t: (0, t)),
        ],
        out_specs=[part, part],
        out_shape=[jax.ShapeDtypeStruct((width, units // 2), BF)] * 2,
        compiler_params=params(),
        cost_estimate=cost(2 * left.size * units),
        name="unit_grads",
    )(left, right)


def head_grads_kernel(dims, split, core_ref, left_ref, right_ref, out_ref):
    product = regroup_rows(mxu(left_ref[...], right_ref[...], dims), split)
    out_ref[0] = product.astype(BF)


def head_grads(left, right, dims, split):
    rows, tokens = left.shape
    columns = right.shape[1] if dims == NN else right.shape[0]
    tile = 2 * LANE
    tiles = columns // tile
    part = tiles // 2
    at = lambda t, core: (t + core[0] * part) % tiles
    if dims == NN:
        spec = pl.BlockSpec((tokens, tile), lambda t, core: (0, at(t, core)))
    else:
        spec = pl.BlockSpec((tile, tokens), lambda t, core: (at(t, core), 0))
    return pl.pallas_call(
        functools.partial(head_grads_kernel, dims, split),
        grid_spec=pltpu.PrefetchScalarGridSpec(
            num_scalar_prefetch=1,
            grid=(tiles,),
            in_specs=[pl.BlockSpec((rows, tokens), lambda t, core: (0, 0)), spec],
            out_specs=pl.BlockSpec((1, rows, tile), lambda t, core: (t // part, 0, t % part)),
        ),
        out_shape=jax.ShapeDtypeStruct((2, rows, columns // 2), BF),
        compiler_params=params(),
        cost_estimate=cost(2 * left.size * columns),
        name="head_grads",
    )(lax.axis_index("mp").astype(jnp.int32)[None], left, right)


def tail_kernel(
    order, x_ref, gh_ref, dq_ref, nt_ref, gain_ref, wq_ref, wkv_ref, cos_ref, sin_ref, gg2_ref,
    query_ref, early_ref, near_refs, *refs,
):
    count_d, count_s = lax.axis_size("dp"), lax.axis_size("seq")
    me_d, me_s, core = lax.axis_index("dp"), lax.axis_index("seq"), lax.axis_index("mp")
    late = len(order) - 1
    far_refs, refs = refs[:late], refs[late:]
    gi_ref, query_out, small_out, early_out = refs[:4]
    (
        key_in, query_in, query_sum, query_seq, query_part, query_dp, early_in, dw, gg1,
        small_other, small_in, small_sum, small_seq, small_part, small_dp, sends, receives,
    ) = refs[4:]
    rows = query_out.shape[0]
    step = pl.program_id(0)
    other_core = {"mp": 1 - core}
    seq_peers = [{"seq": lax.rem(me_s + k, count_s)} for k in range(1, count_s)]
    dp_peers = [{"dp": lax.rem(me_d + k, count_d)} for k in range(1, count_d)]
    peers = [other_core] + seq_peers + dp_peers
    slots = iter(range(sends.shape[0]))

    def link(source, target, peer):
        slot = next(slots)
        return pltpu.make_async_remote_copy(
            src_ref=source,
            dst_ref=target,
            send_sem=sends.at[slot],
            recv_sem=receives.at[slot],
            device_id=peer,
            device_id_type=pl.DeviceIdType.MESH,
        )

    to_seq = [lax.rem(me_s + k, count_s) for k in range(1, count_s)]
    to_dp = [lax.rem(me_d + k, count_d) for k in range(1, count_d)]
    early_copies = [
        link(early_ref.at[to_dp[k]], early_in.at[k], dp_peers[k]) for k in range(count_d - 1)
    ]
    key_copies, at = [], 0
    for far in far_refs:
        size = far.shape[1]
        key_copies.append(
            [
                link(far.at[k + 1], key_in.at[k, pl.ds(at, size)], seq_peers[k])
                for k in range(count_s - 1)
            ]
        )
        at += size
    query_core = link(query_ref.at[1], query_in, other_core)
    query_seqs = [
        link(query_sum.at[to_seq[k]], query_seq.at[k], seq_peers[k]) for k in range(count_s - 1)
    ]
    query_dps = [
        link(query_part.at[to_dp[k]], query_dp.at[k], dp_peers[k]) for k in range(count_d - 1)
    ]
    small_core = link(small_other, small_in, other_core)
    small_seqs = [
        link(small_sum.at[to_seq[k]], small_seq.at[k], seq_peers[k]) for k in range(count_s - 1)
    ]
    small_dps = [
        link(small_part.at[to_dp[k]], small_dp.at[k], dp_peers[k]) for k in range(count_d - 1)
    ]

    def start(copies):
        for copy in copies:
            copy.start()

    def by_seq(total, target):
        for s in range(count_s):
            for d in range(count_d):
                of = (d * count_s + s) * rows
                target[s, d * rows : (d + 1) * rows] = total[of : of + rows].astype(BF)

    def gather(own, copies, arrived):
        total = own.astype(F32)
        for k, copy in enumerate(copies):
            copy.wait()
            total = total + arrived[k].astype(F32)
        return total

    def by_dp(total, target):
        for d in range(count_d):
            target[d] = total[d * rows : (d + 1) * rows].astype(BF)

    @pl.when(step == 0)
    def _():
        barrier = pltpu.get_barrier_semaphore()
        for peer in peers:
            pl.semaphore_signal(barrier, inc=1, device_id=peer, device_id_type=pl.DeviceIdType.MESH)
        pl.semaphore_wait(barrier, len(peers))
        start([query_core])
        for copies in key_copies:
            start(copies)
        start(early_copies)
        dw[...] = jnp.zeros(dw.shape, F32)
        gg1[...] = jnp.zeros(gg1.shape, F32)

    @pl.when(step == 1)
    def _():
        query_core.wait()
        by_seq(query_ref[0].astype(F32) + query_in[...].astype(F32), query_sum)
        start(query_seqs)

    tied = wkv_ref.shape[0] - RD

    def finish(summed):
        turned = rotate_rows(summed[tied:], cos_ref[...], -sin_ref[...])
        dkv = jnp.concatenate([summed[:tied], turned], axis=0).astype(BF)
        grad_normed = mxu(dq_ref[...], wq_ref[...], NN) + mxu(dkv, wkv_ref[...], TN)
        dw[...] += mxu(nt_ref[...], dkv, NT)
        x = x_ref[0].astype(F32)
        inverse = lax.rsqrt(jnp.mean(x * x, axis=-1, keepdims=True) + epsilon)
        scaled = grad_normed * gain_ref[...]
        gg1[...] += jnp.sum(grad_normed * (x * inverse), axis=0, keepdims=True)
        mean = jnp.mean(scaled * x, axis=-1, keepdims=True)
        gi_ref[0] = gh_ref[0] + inverse * scaled - x * (inverse * inverse * inverse * mean)

    begin = order[0][1]

    @pl.when(step < begin)
    def _():
        summed = near_refs[0][0].astype(F32)
        for ref in near_refs[1:]:
            summed = summed + ref[0].astype(F32)
        finish(summed)

    base = begin
    for part, far in enumerate(far_refs):
        size = far.shape[1]

        @pl.when(step == begin)
        def _():
            for copy in key_copies[part]:
                copy.wait()

        @pl.when((step >= begin) & (step < begin + size))
        def _():
            at = step - base
            summed = far[0, step - begin].astype(F32)
            for k in range(count_s - 1):
                summed = summed + key_in[k, at].astype(F32)
            finish(summed)

        begin += size

    @pl.when(step == begin - 2)
    def _():
        total = gather(query_sum[me_s], query_seqs, query_seq)
        by_dp(total, query_part)
        start(query_dps)

    @pl.when(step == begin - 1)
    def _():
        width = dw.shape[0]
        pad = jnp.zeros((LANE - RD, width), F32)
        row = lax.broadcasted_iota(jnp.int32, (LANE, width), 0)
        gains = jnp.where(row == RD, gg1[...], 0.0)
        gains = jnp.where(row == RD + 1, gg2_ref[...], gains)
        weights = dw[...]
        rope = jnp.concatenate([weights[:, tied:], jnp.zeros((width, LANE - RD), F32)], axis=1)
        small = rope + gains.T
        half = tied // 2
        first, second = weights[:, :half], weights[:, half:tied]
        mine = jnp.concatenate([jnp.where(core == 0, first, second), small], axis=1)
        other = jnp.concatenate([jnp.where(core == 0, second, first), small], axis=1)
        small_other[...] = other.astype(BF)
        start([small_core])
        small_core.wait()
        by_seq(mine + small_in[...].astype(F32), small_sum)
        start(small_seqs)
        by_dp(gather(small_sum[me_s], small_seqs, small_seq), small_part)
        start(small_dps)
        early_out[...] = gather(early_ref[me_d], early_copies, early_in)
        query_out[...] = gather(query_part[me_d], query_dps, query_dp)
        small_out[...] = gather(small_part[me_d], small_dps, small_dp)


def tail(
    order, x, grad_hidden, dq, nt, gain, wq, wkv, cosine, sine_table, grad_gain_two, grad_query,
    early, near, far,
):
    count, own, width = x.shape
    count_d, count_s = lax.axis_size("dp"), lax.axis_size("seq")
    rows = width // (count_d * count_s)
    kv_rows = wkv.shape[0]
    tied = kv_rows - RD
    wide = grad_query.shape[2]
    narrow = tied // 2 + LANE
    sent = sum(part.shape[1] for part in far)

    def place(i):
        done, at = 0, i
        for first, size in order:
            at = jnp.where((i >= done) & (i < done + size), first + i - done, at)
            done += size
        return at

    seq = pl.BlockSpec((1, own, width), lambda i: (place(i), 0, 0))
    whole = lambda array: pl.BlockSpec(array.shape, lambda i: (0,) * array.ndim)
    last = order[0][1] - 1
    near_spec = pl.BlockSpec((1, kv_rows, own), lambda i: (jnp.minimum(i, last), 0, 0))
    fixed = [gain, wq, wkv, cosine, sine_table, grad_gain_two, grad_query, early]
    outs = [
        jax.ShapeDtypeStruct(x.shape, F32),
        jax.ShapeDtypeStruct((rows, wide), F32),
        jax.ShapeDtypeStruct((rows, narrow), F32),
        jax.ShapeDtypeStruct((rows, early.shape[2]), F32),
    ]
    terms = len(near)

    def kernel(*refs):
        head, nears, rest = refs[:12], refs[12 : 12 + terms], refs[12 + terms :]
        tail_kernel(order, *head, nears, *rest)

    slots = 3 * (count_d - 1) + (2 + len(far)) * (count_s - 1) + 2
    return pl.pallas_call(
        kernel,
        grid=(count,),
        in_specs=[
            seq, seq,
            pl.BlockSpec((own, dq.shape[1]), lambda i: (place(i), 0)),
            pl.BlockSpec((width, own), lambda i: (0, place(i))),
        ]
        + [whole(array) for array in fixed]
        + [near_spec] * terms
        + [whole(array) for array in far],
        out_specs=[seq] + [whole(out) for out in outs[1:]],
        out_shape=outs,
        scratch_shapes=[
            pltpu.VMEM((count_s - 1, sent, kv_rows, own), BF),
            pltpu.VMEM((width, wide), BF),
            pltpu.VMEM((count_s, count_d * rows, wide), BF),
            pltpu.VMEM((count_s - 1, count_d * rows, wide), BF),
            pltpu.VMEM((count_d, rows, wide), BF),
            pltpu.VMEM((count_d - 1, rows, wide), BF),
            pltpu.VMEM((count_d - 1, rows, early.shape[2]), BF),
            pltpu.VMEM((width, kv_rows), F32),
            pltpu.VMEM((1, width), F32),
            pltpu.VMEM((width, narrow), BF),
            pltpu.VMEM((width, narrow), BF),
            pltpu.VMEM((count_s, count_d * rows, narrow), BF),
            pltpu.VMEM((count_s - 1, count_d * rows, narrow), BF),
            pltpu.VMEM((count_d, rows, narrow), BF),
            pltpu.VMEM((count_d - 1, rows, narrow), BF),
            pltpu.SemaphoreType.DMA((slots,)),
            pltpu.SemaphoreType.DMA((slots,)),
        ],
        compiler_params=pltpu.CompilerParams(
            vmem_limit_bytes=56 * MIB, collective_id=1, has_side_effects=True
        ),
        cost_estimate=cost(4 * 10**10),
        name="tail",
    )(x, grad_hidden, dq, nt, *fixed, *near, *far)


def turn_tables(cosine, sine_table):
    plain = HD - RD
    one = jnp.ones((cosine.shape[0], plain), F32)
    none = jnp.zeros_like(one)
    quiet = jnp.zeros_like(sine_table)
    straight = jnp.concatenate([one, cosine, cosine], axis=1)
    ahead = jnp.concatenate([none, sine_table, quiet], axis=1)
    behind = jnp.concatenate([none, quiet, -sine_table], axis=1)
    return jnp.stack([jnp.concatenate([t, t], axis=1) for t in (straight, ahead, behind)])


def after(value, *others):
    return lax.optimization_barrier((value, *others))[0]


def spans(count, shares):
    if count % 4:
        return [(0, count)]
    cuts, at = [], 0
    for share in shares:
        size = share * count // 4
        cuts.append((at, size))
        at += size
    return cuts


def on_device_fast(
    inputs, gain_one, w_query, w_tied, w_rope, w_out, gain_two, w_gate, w_up, w_down,
    doc_starts, out_grad,
):
    count, own, width = inputs.shape
    cores = lax.axis_size("mp")
    groups = cores * w_tied.shape[1] // HD
    all_heads = cores * w_query.shape[1] // HD
    heads = all_heads // groups
    mp_index = lax.axis_index("mp")
    split = (lax.axis_size("dp"), lax.axis_size("seq"))
    tied_t = w_tied.T
    tied_both = by_core(tied_t, swap_cores(tied_t), 0)
    keys_weights = jnp.concatenate([tied_both, w_rope.T], axis=0)
    query_t = w_query.T
    queries_weights = by_core(query_t, swap_cores(query_t), 0)
    down_other = swap_cores(w_down)
    gain_one_float = gain_one.astype(F32)[None]
    gain_two_float = gain_two.astype(F32)[None]
    cosine, sine_table = rope_tables(my_chunk() * own, own, RD)
    cosine_t, sine_t = cosine.T, sine_table.T
    kv, normed_t = project_keys(inputs, gain_one_float, keys_weights, cosine_t, sine_t)
    forward = spans(count, (1, 1, 2))
    gathered = [gather_keys(kv[at : at + size]) for at, size in forward]
    q = project_queries(normed_t, queries_weights, cosine_t, sine_t)
    slopes = unit_slopes(out_grad, (w_down, down_other))
    out_other = swap_cores(w_out)
    gate_other, up_other = swap_cores(w_gate), swap_cores(w_up)
    gathered[0] = list(after(tuple(gathered[0]), slopes))
    made = ()
    for (at, _), kv_part in zip(forward, gathered):
        made = attend_forward(doc_starts, q, kv_part, groups, heads, at, made)
    heads_out, lse = made
    out_both = by_core(w_out, out_other, 0)
    (
        outputs, normed_two_t, out_grad_t, active, grad_gate, grad_up, grad_hidden, grad_attended_t,
        grad_heads, delta, grad_gain_two,
    ) = feed(
        inputs, out_grad, slopes, heads_out, gain_two_float, out_both, (w_gate, gate_other),
        (w_up, up_other), (w_down, down_other),
    )
    def unit_part(left, right, parts):
        own_part, other_part = unit_grads(left, right, parts)
        return own_part, swap_cores(other_part)

    parts = [
        unit_part(normed_two_t, grad_gate, split),
        unit_part(normed_two_t, grad_up, split),
        unit_part(out_grad_t, active, split),
    ]
    out = head_grads(grad_attended_t, heads_out, NT, split)
    parts.append((out[0], swap_cores(out[1])))
    first_sum = jnp.concatenate([mine + other for mine, other in parts], axis=1)
    first_sum, grad_heads = lax.optimization_barrier((first_sum, grad_heads))
    first_sum = lax.psum_scatter(first_sum, "seq", scatter_dimension=0, tiled=True)

    turns = turn_tables(cosine, sine_table)
    backward = list(zip(forward, gathered))[::-1]
    dq, summed = (), []
    for part, ((at, _), kv_part) in enumerate(backward):
        first_q = q
        if part == 1:
            near = send_keys(summed[0])
            first_q = after(q, near[0])
        if part == 2:
            first_q = after(q, *near)
        made_dq, keep, give = attend_backward(
            doc_starts, first_q, grad_heads, lse, delta, turns, kv_part, groups, heads, at, dq
        )
        dq = (made_dq,)
        summed.append(join_cores(keep, give))
    if len(backward) == 1:
        near = send_keys(summed[0])
    early = first_sum.reshape(split[0], -1, first_sum.shape[1])
    grad_query = head_grads(normed_t, dq[0], NN, None)
    order = [span for span, _ in backward]
    grad_inputs, query_sum, small_sum, first_sum = tail(
        order, inputs, grad_hidden, dq[0], normed_t, gain_one_float, queries_weights, keys_weights,
        cosine_t, sine_t, grad_gain_two, grad_query, early, near,
        [jnp.stack(terms) for terms in summed[1:]],
    )
    half_tied = groups * HD // cores
    late_sum, small_sum = small_sum[:, :half_tied], small_sum[:, half_tied:]
    rows = small_sum.shape[0] // cores
    small_sum = lax.dynamic_slice_in_dim(small_sum, mp_index * rows, rows, 0)
    units = w_gate.shape[1]
    return (
        outputs,
        grad_inputs,
        small_sum[:, RD],
        query_sum,
        late_sum,
        small_sum[:, :RD],
        first_sum[:, 3 * units :].T,
        small_sum[:, RD + 1],
        first_sum[:, :units],
        first_sum[:, units : 2 * units],
        first_sum[:, 2 * units : 3 * units].T,
    )


def solution(mesh):
    in_specs = (
        P("dp", ("seq", "mp"), None),
        P(),
        P(None, "mp"),
        P(None, "mp"),
        P(),
        P("mp", None),
        P(),
        P(None, "mp"),
        P(None, "mp"),
        P("mp", None),
        P("dp", None),
        P("dp", ("seq", "mp"), None),
    )
    out_specs = (
        P("dp", ("seq", "mp"), None),
        P("dp", ("seq", "mp"), None),
        P(("dp", "seq", "mp")),
        P(("dp", "seq"), "mp"),
        P(("dp", "seq"), "mp"),
        P(("dp", "seq", "mp"), None),
        P("mp", ("dp", "seq")),
        P(("dp", "seq", "mp")),
        P(("dp", "seq"), "mp"),
        P(("dp", "seq"), "mp"),
        P("mp", ("dp", "seq")),
    )

    def local(inputs, *rest):
        step = on_device_fast if inputs.shape[1] % (2 * LANE) == 0 else on_device
        return step(inputs, *rest)

    return jax.shard_map(
        local, mesh=mesh, in_specs=in_specs, out_specs=out_specs, check_vma=False
    )
```

```python
import functools

import jax
import jax.numpy as jnp
from jax import lax
from jax.experimental import pallas as pl
from jax.experimental.pallas import tpu as pltpu
from jax.sharding import PartitionSpec as P

HD = 64
RD = 32


epsilon = 1e-05
rope_base = 10000.0
masked_value = -1e30


def rope_tables(offset, count, rope_width):
    position = (offset + jnp.arange(count, dtype=jnp.int32)).astype(jnp.float32)
    frequency = rope_base ** (-jnp.arange(rope_width // 2, dtype=jnp.float32) * 2.0 / rope_width)
    angles = position[:, None] * frequency[None, :]
    return (jnp.cos(angles), jnp.sin(angles))


def rotate(values, cosine, sine_table):
    half_width = values.shape[-1] // 2
    first_half = values[..., :half_width]
    second_half = values[..., half_width:]
    return jnp.concatenate(
        [
            first_half * cosine - second_half * sine_table,
            second_half * cosine + first_half * sine_table,
        ],
        axis=-1,
    )


def rotate_back(grads, cosine, sine_table):
    half_width = grads.shape[-1] // 2
    first_half = grads[..., :half_width]
    second_half = grads[..., half_width:]
    return jnp.concatenate(
        [
            first_half * cosine + second_half * sine_table,
            second_half * cosine - first_half * sine_table,
        ],
        axis=-1,
    )


def contract_rows(left, right):
    return lax.dot_general(
        left, right, (((0,), (0,)), ((), ())), preferred_element_type=jnp.float32
    )


def times_transposed(left, right):
    return lax.dot_general(
        left, right, (((1,), (1,)), ((), ())), preferred_element_type=jnp.float32
    )


def norm_back(grad_normed, values, inverse, gain):
    scaled = grad_normed * gain
    grad_gain = jnp.sum(grad_normed * values * inverse, axis=(0, 1))
    grad_values = inverse * scaled - values * inverse**3 * jnp.mean(
        scaled * values, axis=-1, keepdims=True
    )
    return (grad_values, grad_gain)


def attend(operands):
    queries, key_full, values, allowed = operands
    scores = jnp.einsum(
        "qghd,kgd->ghqk", queries, key_full, preferred_element_type=jnp.float32
    ) * HD ** (-0.5)
    masked = jnp.where(allowed[None, None], scores, masked_value)
    row_max = jnp.max(masked, axis=-1, keepdims=True)
    weights = jnp.exp(masked - row_max)
    row_total = jnp.sum(weights, axis=-1, keepdims=True)
    attention_probs = (weights / row_total).astype(jnp.bfloat16)
    combined = jnp.einsum(
        "ghqk,kgd->qghd", attention_probs, values, preferred_element_type=jnp.float32
    )
    return (combined.astype(jnp.bfloat16), row_max + jnp.log(row_total))


def attend_back(operands):
    queries, key_full, values, allowed, log_total, grad_heads = operands
    score_scale = HD ** (-0.5)
    plain_width = HD - RD
    scores = (
        jnp.einsum("qghd,kgd->ghqk", queries, key_full, preferred_element_type=jnp.float32)
        * score_scale
    )
    masked = jnp.where(allowed[None, None], scores, masked_value)
    probs_float = jnp.exp(masked - log_total)
    grad_probs = jnp.einsum(
        "qghd,kgd->ghqk", grad_heads, values, preferred_element_type=jnp.float32
    )
    row_delta = jnp.sum(probs_float * grad_probs, axis=-1, keepdims=True)
    grad_scores = (probs_float * (grad_probs - row_delta)).astype(jnp.bfloat16)
    grad_queries = (
        jnp.einsum("ghqk,kgd->qghd", grad_scores, key_full, preferred_element_type=jnp.float32)
        * score_scale
    )
    grad_keys = (
        jnp.einsum("ghqk,qghd->kgd", grad_scores, queries, preferred_element_type=jnp.float32)
        * score_scale
    )
    grad_values = jnp.einsum(
        "ghqk,qghd->kgd",
        probs_float.astype(jnp.bfloat16),
        grad_heads,
        preferred_element_type=jnp.float32,
    )
    grad_tied = grad_values + jnp.concatenate(
        [grad_keys[..., :plain_width], jnp.zeros_like(grad_keys[..., plain_width:])], axis=-1
    )
    grad_rope = jnp.sum(grad_keys[..., plain_width:], axis=1)
    return (grad_queries, grad_tied, grad_rope)


def on_device(
    inputs,
    gain_one,
    w_query,
    w_tied,
    w_rope,
    w_out,
    gain_two,
    w_gate,
    w_up,
    w_down,
    doc_starts,
    out_grad,
):
    seq_count, own_count, model_width = inputs.shape
    plain_width = HD - RD
    group_local = w_tied.shape[1] // HD
    head_local = w_query.shape[1] // HD
    seq_index = lax.axis_index("seq")
    mp_index = lax.axis_index("mp")
    gain_one_float = gain_one.astype(jnp.float32)
    gain_two_float = gain_two.astype(jnp.float32)
    inputs_float = inputs.astype(jnp.float32)
    inverse_one = lax.rsqrt(jnp.mean(inputs_float * inputs_float, axis=-1, keepdims=True) + epsilon)
    normed_one = (inputs_float * inverse_one * gain_one_float).astype(jnp.bfloat16)
    gathered_one = lax.all_gather(normed_one, "mp", axis=1, tiled=True)
    context = gathered_one.shape[1]
    token_count = seq_count * context
    flat_one = gathered_one.reshape(token_count, model_width)
    offset = seq_index * context
    cosine, sine_table = rope_tables(offset, context, RD)
    query_lin = jnp.dot(flat_one, w_query, preferred_element_type=jnp.float32).reshape(
        seq_count, context, head_local, HD
    )
    queries = jnp.concatenate(
        [
            query_lin[..., :plain_width],
            rotate(
                query_lin[..., plain_width:], cosine[None, :, None, :], sine_table[None, :, None, :]
            ),
        ],
        axis=-1,
    ).astype(jnp.bfloat16)
    queries = queries.reshape(seq_count, context, group_local, head_local // group_local, HD)
    tied_state = (
        jnp.dot(flat_one, w_tied, preferred_element_type=jnp.float32)
        .astype(jnp.bfloat16)
        .reshape(seq_count, context, group_local * HD)
    )
    rope_lin = jnp.dot(flat_one, w_rope, preferred_element_type=jnp.float32).reshape(
        seq_count, context, RD
    )
    rope_keys = rotate(rope_lin, cosine[None], sine_table[None]).astype(jnp.bfloat16)
    tied_all, rope_all = (
        lax.all_gather(tied_state, "seq", axis=1, tiled=True),
        lax.all_gather(rope_keys, "seq", axis=1, tiled=True),
    )
    length = tied_all.shape[1]
    values_all = tied_all.reshape(seq_count, length, group_local, HD)
    key_full = jnp.concatenate(
        [
            values_all[..., :plain_width],
            jnp.broadcast_to(rope_all[:, :, None, :], (seq_count, length, group_local, RD)),
        ],
        axis=-1,
    )
    key_position = jnp.arange(length, dtype=jnp.int32)
    key_segment = jnp.sum(
        (doc_starts[:, None, :] <= key_position[None, :, None]).astype(jnp.int32), axis=-1
    )
    query_segment = lax.dynamic_slice_in_dim(key_segment, offset, context, 1)
    query_position = offset + jnp.arange(context, dtype=jnp.int32)
    allowed = (query_segment[:, :, None] == key_segment[:, None, :]) & (
        query_position[:, None] >= key_position[None, :]
    )[None]
    head_outputs, log_total = lax.map(attend, (queries, key_full, values_all, allowed))
    flat_heads = head_outputs.reshape(token_count, head_local * HD)
    attended_part = jnp.dot(flat_heads, w_out, preferred_element_type=jnp.float32).reshape(
        seq_count, context, model_width
    )
    attended = lax.psum_scatter(
        attended_part.astype(jnp.bfloat16), "mp", scatter_dimension=1, tiled=True
    ).astype(jnp.float32)
    hidden = inputs_float + attended
    inverse_two = lax.rsqrt(jnp.mean(hidden * hidden, axis=-1, keepdims=True) + epsilon)
    normed_two = (hidden * inverse_two * gain_two_float).astype(jnp.bfloat16)
    gathered_two = lax.all_gather(normed_two, "mp", axis=1, tiled=True)
    flat_two = gathered_two.reshape(token_count, model_width)
    gate_values = jnp.dot(flat_two, w_gate, preferred_element_type=jnp.float32)
    up_values = jnp.dot(flat_two, w_up, preferred_element_type=jnp.float32)
    sigmoid_gate = jax.nn.sigmoid(gate_values)
    silu_gate = gate_values * sigmoid_gate
    active = (silu_gate * up_values).astype(jnp.bfloat16)
    result_part = jnp.dot(active, w_down, preferred_element_type=jnp.float32).reshape(
        seq_count, context, model_width
    )
    result = lax.psum_scatter(
        result_part.astype(jnp.bfloat16), "mp", scatter_dimension=1, tiled=True
    ).astype(jnp.float32)
    outputs = (hidden + result).astype(jnp.bfloat16)
    grad_out_all = lax.all_gather(out_grad, "mp", axis=1, tiled=True)
    flat_grad = grad_out_all.reshape(token_count, model_width)
    grad_active = times_transposed(flat_grad, w_down)
    grad_w_down = contract_rows(active, flat_grad)
    grad_gate = (
        grad_active * up_values * sigmoid_gate * (1.0 + gate_values * (1.0 - sigmoid_gate))
    ).astype(jnp.bfloat16)
    grad_up = (grad_active * silu_gate).astype(jnp.bfloat16)
    grad_w_gate = contract_rows(flat_two, grad_gate)
    grad_w_up = contract_rows(flat_two, grad_up)
    grad_two_part = (times_transposed(grad_gate, w_gate) + times_transposed(grad_up, w_up)).reshape(
        seq_count, context, model_width
    )
    grad_normed_two = lax.psum_scatter(
        grad_two_part.astype(jnp.bfloat16), "mp", scatter_dimension=1, tiled=True
    ).astype(jnp.float32)
    grad_hidden_norm, grad_gain_two = norm_back(
        grad_normed_two, hidden, inverse_two, gain_two_float
    )
    grad_hidden = out_grad.astype(jnp.float32) + grad_hidden_norm
    grad_attended_all = lax.all_gather(grad_hidden.astype(jnp.bfloat16), "mp", axis=1, tiled=True)
    flat_attended = grad_attended_all.reshape(token_count, model_width)
    grad_w_out = contract_rows(flat_heads, flat_attended)
    grad_heads = times_transposed(flat_attended, w_out).astype(jnp.bfloat16).reshape(queries.shape)
    grad_queries, grad_tied, grad_rope = lax.map(
        attend_back, (queries, key_full, values_all, allowed, log_total, grad_heads)
    )
    grad_queries = grad_queries.reshape(seq_count, context, head_local, HD)
    grad_query_lin = (
        jnp.concatenate(
            [
                grad_queries[..., :plain_width],
                rotate_back(
                    grad_queries[..., plain_width:],
                    cosine[None, :, None, :],
                    sine_table[None, :, None, :],
                ),
            ],
            axis=-1,
        )
        .astype(jnp.bfloat16)
        .reshape(token_count, head_local * HD)
    )
    tied_own, rope_context = (
        lax.psum_scatter(
            grad_tied.reshape(seq_count, length, group_local * HD).astype(jnp.bfloat16),
            "seq",
            scatter_dimension=1,
            tiled=True,
        ).astype(jnp.float32),
        lax.psum_scatter(
            grad_rope.astype(jnp.bfloat16), "seq", scatter_dimension=1, tiled=True
        ).astype(jnp.float32),
    )
    grad_tied_flat = tied_own.astype(jnp.bfloat16).reshape(token_count, group_local * HD)
    grad_one_part = (
        times_transposed(grad_query_lin, w_query) + times_transposed(grad_tied_flat, w_tied)
    ).reshape(seq_count, context, model_width)
    grad_normed_one, rope_own = (
        lax.psum_scatter(
            grad_one_part.astype(jnp.bfloat16), "mp", scatter_dimension=1, tiled=True
        ).astype(jnp.float32),
        lax.psum_scatter(
            rope_context.astype(jnp.bfloat16), "mp", scatter_dimension=1, tiled=True
        ).astype(jnp.float32),
    )
    own_offset = offset + mp_index * own_count
    cosine_own, sine_own = rope_tables(own_offset, own_count, RD)
    grad_rope_flat = (
        rotate_back(rope_own, cosine_own[None], sine_own[None])
        .astype(jnp.bfloat16)
        .reshape(seq_count * own_count, RD)
    )
    grad_normed_one = grad_normed_one + times_transposed(grad_rope_flat, w_rope).reshape(
        seq_count, own_count, model_width
    )
    grad_w_rope = contract_rows(
        normed_one.reshape(seq_count * own_count, model_width), grad_rope_flat
    )
    grad_w_query = contract_rows(flat_one, grad_query_lin)
    grad_w_tied = contract_rows(flat_one, grad_tied_flat)
    grad_inputs_norm, grad_gain_one = norm_back(
        grad_normed_one, inputs_float, inverse_one, gain_one_float
    )
    grad_inputs = grad_hidden + grad_inputs_norm
    small_sums = (
        lax.psum_scatter(grad_gain_one, ("dp", "seq", "mp"), scatter_dimension=0, tiled=True),
        lax.psum_scatter(grad_w_rope, ("dp", "seq", "mp"), scatter_dimension=0, tiled=True),
        lax.psum_scatter(grad_gain_two, ("dp", "seq", "mp"), scatter_dimension=0, tiled=True),
    )
    weight_terms = (grad_w_query, grad_w_tied, grad_w_out, grad_w_gate, grad_w_up, grad_w_down)
    weight_sums = (
        lax.psum_scatter(weight_terms[0], ("dp", "seq"), scatter_dimension=0, tiled=True),
        lax.psum_scatter(weight_terms[1], ("dp", "seq"), scatter_dimension=0, tiled=True),
        lax.psum_scatter(weight_terms[2], ("dp", "seq"), scatter_dimension=1, tiled=True),
        lax.psum_scatter(weight_terms[3], ("dp", "seq"), scatter_dimension=0, tiled=True),
        lax.psum_scatter(weight_terms[4], ("dp", "seq"), scatter_dimension=0, tiled=True),
        lax.psum_scatter(weight_terms[5], ("dp", "seq"), scatter_dimension=1, tiled=True),
    )
    return (
        outputs,
        grad_inputs,
        small_sums[0],
        weight_sums[0],
        weight_sums[1],
        small_sums[1],
        weight_sums[2],
        small_sums[2],
        weight_sums[3],
        weight_sums[4],
        weight_sums[5],
    )


BF = jnp.bfloat16
F32 = jnp.float32
NN = (((1,), (0,)), ((), ()))
NT = (((1,), (1,)), ((), ()))
TN = (((0,), (0,)), ((), ()))
BIG = 2.0**100
MIB = 1 << 20
LANE = 128


def mxu(left, right, dims):
    return lax.dot_general(left, right, dims, preferred_element_type=F32)


def params(limit=56):
    return pltpu.CompilerParams(vmem_limit_bytes=limit * MIB)


def cost(flops, moved=0):
    return pl.CostEstimate(flops=int(flops), bytes_accessed=int(moved), transcendentals=0)


def swap_cores(value):
    return lax.ppermute(value, "mp", [(0, 1), (1, 0)])


def shift(value, axis, by):
    size = lax.axis_size(axis)
    return lax.ppermute(value, axis, [(i, (i + by) % size) for i in range(size)])


def send_near(kv):
    return [kv] + [shift(kv, "seq", k) for k in range(1, lax.axis_size("seq"))]


def send_far(near):
    return [part[None] for part in near + [swap_cores(value) for value in near]]


def pick(value, index, axis):
    return lax.dynamic_index_in_dim(value, index, axis, keepdims=False)


def send_steps(value, axis, dim):
    size, me = lax.axis_size(axis), lax.axis_index(axis)
    terms = [pick(value, me, dim)]
    for k in range(1, size):
        terms.append(shift(pick(value, (me + k) % size, dim), axis, k))
    return terms


def add_up(terms):
    total = terms[0].astype(F32)
    for term in terms[1:]:
        total = total + term.astype(F32)
    return total


def by_core(own, other, axis):
    first = lax.axis_index("mp") == 0
    return jnp.concatenate(
        [jnp.where(first, own, other), jnp.where(first, other, own)], axis=axis
    )


def rotate_rows(values, cosine, sine_table):
    half = values.shape[0] // 2
    a, b = values[:half], values[half:]
    return jnp.concatenate([a * cosine - b * sine_table, b * cosine + a * sine_table], axis=0)


def project_kernel(
    sent, x_ref, og_ref, gain_ref, wkv_ref, wq_ref, wdo_ref, wdp_ref, cos_ref, sin_ref,
    kv_ref, nt_ref, q_ref, ga_ref, near_ref, far_ref, kept, wd, load_sems, own_sems, sends, receives,
):
    b = pl.program_id(0)
    count_s = lax.axis_size("seq")
    me_s, core = lax.axis_index("seq"), lax.axis_index("mp")
    peers = [{"seq": lax.rem(me_s + k, count_s)} for k in range(1, count_s)]
    other_core = {"mp": 1 - core}
    near, forward = [], []
    slots = iter(range(sends.shape[0]))

    def link(source, target, peer):
        slot = next(slots)
        return pltpu.make_async_remote_copy(
            src_ref=source,
            dst_ref=target,
            send_sem=sends.at[slot],
            recv_sem=receives.at[slot],
            device_id=peer,
            device_id_type=pl.DeviceIdType.MESH,
        )

    for i in range(sent):
        near.append([link(kept.at[i], near_ref.at[k, i], peers[k - 1]) for k in range(1, count_s)])
        forward.append(
            [link(kept.at[i], far_ref.at[0, i], other_core)]
            + [link(near_ref.at[k, i], far_ref.at[k, i], other_core) for k in range(1, count_s)]
        )
    own = [pltpu.make_async_copy(kept.at[i], near_ref.at[0, i], own_sems.at[i]) for i in range(sent)]
    loads = load_weights([(wdo_ref, 0, 0), (wdp_ref, 1, 0)], [wd, wd], load_sems)

    @pl.when(b == 0)
    def _():
        for copy in loads:
            copy.start()
        barrier = pltpu.get_barrier_semaphore()
        for peer in [other_core] + peers:
            pl.semaphore_signal(barrier, inc=1, device_id=peer, device_id_type=pl.DeviceIdType.MESH)
        pl.semaphore_wait(barrier, count_s)

    x = x_ref[0].astype(F32)
    inverse = lax.rsqrt(jnp.mean(x * x, axis=-1, keepdims=True) + epsilon)
    normed = (x * inverse * gain_ref[...]).astype(BF)
    lin = mxu(wkv_ref[...], normed, NT)
    tied = wkv_ref.shape[0] - RD
    cosine, sine_table = cos_ref[...], sin_ref[...]
    rope = rotate_rows(lin[tied:], cosine, sine_table)
    keys = jnp.concatenate([lin[:tied], rope], axis=0).astype(BF)
    kv_ref[0] = keys
    for i in range(sent):

        @pl.when(b == i)
        def _():
            kept[i] = keys
            for copy in near[i]:
                copy.start()
            forward[i][0].start()
            own[i].start()

    nt_ref[...] = normed.T
    lin = mxu(wq_ref[...], normed, NT)
    plain = HD - RD
    pieces = []
    for at in range(0, lin.shape[0], HD):
        pieces.append(lin[at : at + plain])
        pieces.append(rotate_rows(lin[at + plain : at + HD], cosine, sine_table))
    queries = jnp.concatenate(pieces, axis=0)
    q_ref[...] = (queries.astype(BF) * HD ** (-0.5)).astype(BF)

    @pl.when(b == 0)
    def _():
        for copy in loads:
            copy.wait()

    og = og_ref[0]
    for at in range(0, wd.shape[0], 2 * LANE):
        to = slice(at, at + 2 * LANE)
        ga_ref[:, to] = mxu(og, wd[to], NT).astype(BF)

    steps = pl.num_programs(0)
    for i in range(sent):

        @pl.when(b == steps - 1 - (3 * (sent - 1 - i) + 1) // 2)
        def _():
            for copy in near[i]:
                copy.wait()
            for copy in forward[i][1:]:
                copy.start()

    @pl.when(b == steps - 1)
    def _():
        for i in range(sent):
            own[i].wait()
            for copy in forward[i]:
                copy.wait()


def project(x, og, gain, wkv, wq, wd, cosine, sine_table, sent):
    count, own, width = x.shape
    kv_rows, rows, half = wkv.shape[0], wq.shape[0], wd[0].shape[0]
    count_s = lax.axis_size("seq")
    whole = lambda array: pl.BlockSpec(array.shape, lambda b: (0, 0))
    seq = pl.BlockSpec((1, own, width), lambda b: (b, 0, 0))
    hbm = pl.BlockSpec(memory_space=pl.ANY)
    gathered = jax.ShapeDtypeStruct((count_s, sent, kv_rows, own), BF)
    links = sent * (2 * count_s - 1)
    return pl.pallas_call(
        functools.partial(project_kernel, sent),
        grid=(count,),
        in_specs=[
            seq, seq, whole(gain), whole(wkv), whole(wq), hbm, hbm, whole(cosine), whole(cosine),
        ],
        out_specs=[
            pl.BlockSpec((1, kv_rows, own), lambda b: (b, 0, 0)),
            pl.BlockSpec((width, own), lambda b: (0, b)),
            pl.BlockSpec((rows, own), lambda b: (0, b)),
            pl.BlockSpec((own, 2 * half), lambda b: (b, 0)),
            hbm,
            hbm,
        ],
        out_shape=[
            jax.ShapeDtypeStruct((count, kv_rows, own), BF),
            jax.ShapeDtypeStruct((width, count * own), BF),
            jax.ShapeDtypeStruct((rows, count * own), BF),
            jax.ShapeDtypeStruct((count * own, 2 * half), BF),
            gathered,
            gathered,
        ],
        scratch_shapes=[
            pltpu.VMEM((sent, kv_rows, own), BF),
            pltpu.VMEM((2 * half, width), BF),
            pltpu.SemaphoreType.DMA((2 * (half // LANE),)),
            pltpu.SemaphoreType.DMA((sent,)),
            pltpu.SemaphoreType.DMA((links,)),
            pltpu.SemaphoreType.DMA((links,)),
        ],
        compiler_params=pltpu.CompilerParams(
            vmem_limit_bytes=56 * MIB, collective_id=2, has_side_effects=True
        ),
        cost_estimate=cost(3 * 10**10),
        name="project",
    )(x, og, gain, wkv, wq, *wd, cosine, sine_table)


def segment_counts(starts, first, width):
    position = first + lax.broadcasted_iota(jnp.int32, (1, width), 1)
    count = jnp.zeros((1, width), jnp.int32)
    for start in starts:
        count = count + (start <= position).astype(jnp.int32)
    return count


def query_rows(starts, first, width):
    row = lax.broadcasted_iota(jnp.int32, (16, width), 0)
    match = segment_counts(starts, first, width) == row + 1
    return jnp.where(match, 1.0, 0.0).astype(BF)


def key_rows(starts, first, width):
    row = lax.broadcasted_iota(jnp.int32, (16, width), 0)
    match = (segment_counts(starts, first, width) == row + 1) | (row >= len(starts))
    return jnp.where(match, 0.0, -BIG).astype(BF)


def first_rows(count, width):
    row = lax.broadcasted_iota(jnp.int32, (16, width), 0)
    return jnp.where(row < count, 1.0, 0.0).astype(BF)


def three_parts(row, width):
    high = row.astype(BF)
    rest = row - high.astype(F32)
    middle = rest.astype(BF)
    low = (rest - middle.astype(F32)).astype(BF)
    at = lax.broadcasted_iota(jnp.int32, (16, width), 0)
    parts = jnp.where(at == 0, high.astype(F32), 0.0)
    parts = jnp.where(at == 1, middle.astype(F32), parts)
    return jnp.where(at == 2, low.astype(F32), parts).astype(BF)


def start_chunk(starts, first, chunk):
    begin = jnp.int32(0)
    for start in starts:
        begin = jnp.where(start <= first, jnp.maximum(begin, start), begin)
    return begin // chunk


def my_chunk():
    return lax.axis_index("seq") * lax.axis_size("mp") + lax.axis_index("mp")


def place_keys(refs, kv, begin, me):
    steps = lax.axis_size("seq")
    seq, core = lax.axis_index("seq"), lax.axis_index("mp")
    places = [(ref, i) for ref in refs for i in range(ref.shape[0])]
    for at, (ref, i) in enumerate(places):
        of = core if at < steps else 1 - core
        j = lax.rem(seq - at % steps + steps, steps) * 2 + of

        @pl.when((j >= begin) & (j <= me))
        def _():
            kv[j] = ref[i, 0]


def stack_heads(value, at, heads, rows=HD):
    half = value.shape[1] // 2
    return jnp.concatenate(
        [
            value[at + h * rows : at + (h + 1) * rows, s * half : (s + 1) * half]
            for s in range(2)
            for h in range(heads)
        ],
        axis=1,
    )


def stack_queries(starts, first, half, heads):
    return jnp.concatenate(
        [query_rows(starts, first + s * half, half) for s in range(2) for _ in range(heads)], axis=1
    )


def attend_kernel(groups, heads, first, inputs, docs_ref, q_ref, *refs):
    kv_refs = refs[:inputs]
    out_ref, lse_ref, kv_ref, qa, acc, top = refs[-6:]
    b = pl.program_id(0) + first
    own = q_ref.shape[1]
    ndoc = docs_ref.shape[1]
    starts = [docs_ref[b, k] for k in range(ndoc)]
    me = my_chunk()
    begin = start_chunk(starts, me * own, own)
    half = own // 2
    begin_second = start_chunk(starts, me * own + half, own)
    place_keys(kv_refs, kv_ref, begin, me)
    wide = heads * own
    first_half = wide // 2
    tied = groups * HD
    plain = HD - RD
    q_doc = stack_queries(starts, me * own, half, heads)
    q_all = q_ref[...]
    for g in range(groups):
        qa[g, :HD] = stack_heads(q_all, g * heads * HD, heads)
        qa[g, HD : HD + 16] = q_doc
        qa[g, HD + 16 :] = jnp.zeros((LANE - HD - 16, wide), BF)
    ones = first_rows(1, own)
    zeros = jnp.zeros((LANE - HD - 16, own), BF)

    def keys_of(j, g):
        doc = key_rows(starts, j * own, own)
        block = jnp.concatenate(
            [
                kv_ref[j, g * HD : g * HD + plain],
                kv_ref[j, tied : tied + RD],
                doc,
                zeros,
            ],
            axis=0,
        )
        return block.T

    def values_of(j, g):
        return jnp.concatenate([kv_ref[j, g * HD : (g + 1) * HD], ones], axis=0)

    key_at = lax.broadcasted_iota(jnp.int32, (own, half), 0)
    query_at = lax.broadcasted_iota(jnp.int32, (own, half), 1)
    causal = jnp.concatenate(
        [key_at <= query_at + s * half for s in range(2) for _ in range(heads)], axis=1
    )

    def block(j, lanes, diagonal=False):
        def logits_of(g):
            return mxu(keys_of(j, g), qa[g, :, lanes], NN)

        following = logits_of(0)
        for g in range(groups):
            logits = following
            if g + 1 < groups:
                following = logits_of(g + 1)
            if diagonal:
                logits = jnp.where(causal, logits, masked_value)
            peak = jnp.max(logits, axis=0, keepdims=True)
            if not diagonal:
                old = top[g, :, lanes]
                peak = jnp.maximum(old, peak)
            weights = jnp.exp(logits - peak).astype(BF)
            added = mxu(values_of(j, g), weights, NN)
            if not diagonal:
                added = acc[g, :, lanes] * jnp.exp(old - peak) + added
            acc[g, :, lanes] = added
            top[g, :, lanes] = peak

    block(me, slice(0, wide), True)

    def both(i, carry):
        block(me - 1 - i, slice(0, wide))
        return carry

    def first_only(i, carry):
        block(begin_second - 1 - i, slice(0, first_half))
        return carry

    lax.fori_loop(0, me - begin_second, both, 0)
    lax.fori_loop(0, begin_second - begin, first_only, 0)
    for g in range(groups):
        total = acc[g, HD : HD + 1]
        result = acc[g, :HD] / total
        lse_ref[0, g : g + 1] = top[g] + jnp.log(total)
        for s in range(2):
            for h in range(heads):
                at, of = (g * heads + h) * HD, (s * heads + h) * half
                out_ref[at : at + HD, s * half : (s + 1) * half] = result[:, of : of + half].astype(BF)


def kv_specs(kv, kv_at):
    return [
        pl.BlockSpec((part.shape[0], 1, *part.shape[2:]), lambda b: (0, b + kv_at, 0, 0))
        for part in kv
    ]


def attend_forward(docs, q, kv, groups, heads, first, size, kv_at, into):
    kv_rows, own = kv[0].shape[2:]
    count, chunks, inputs = docs.shape[0], 2 * lax.axis_size("seq"), len(kv)
    wide = heads * own
    hbm = pl.BlockSpec(memory_space=pl.ANY)
    return pl.pallas_call(
        functools.partial(attend_kernel, groups, heads, first, inputs),
        grid=(size,),
        in_specs=[
            pl.BlockSpec(memory_space=pltpu.SMEM),
            pl.BlockSpec((q.shape[0], own), lambda b: (0, b + first)),
        ]
        + kv_specs(kv, kv_at)
        + [hbm] * len(into),
        out_specs=[
            pl.BlockSpec((q.shape[0], own), lambda b: (0, b + first)),
            pl.BlockSpec((1, groups, wide), lambda b: (b + first, 0, 0)),
        ],
        out_shape=[
            jax.ShapeDtypeStruct(q.shape, BF),
            jax.ShapeDtypeStruct((count, groups, wide), F32),
        ],
        scratch_shapes=[
            pltpu.VMEM((chunks, kv_rows, own), BF),
            pltpu.VMEM((groups, LANE, wide), BF),
            pltpu.VMEM((groups, HD + 16, wide), F32),
            pltpu.VMEM((groups, 1, wide), F32),
        ],
        input_output_aliases={2 + inputs + i: i for i in range(len(into))},
        compiler_params=params(),
        cost_estimate=cost(10**10 * size),
        name="attend",
    )(docs, q, *kv, *into)


def attend_back_kernel(
    groups, heads, first, inputs, docs_ref, q_ref, do_ref, lse_ref, delta_ref, rot_ref, *refs
):
    kv_refs = refs[:inputs]
    chunks = 2 * lax.axis_size("seq")
    dq_ref, keep_ref, give_ref, kv_ref, stage, qs, qa, ds_, da, dq = refs[-10:]
    b = pl.program_id(0) + first
    own = q_ref.shape[1]
    ndoc = docs_ref.shape[1]
    starts = [docs_ref[b, k] for k in range(ndoc)]
    me = my_chunk()
    begin = start_chunk(starts, me * own, own)
    half = own // 2
    begin_second = start_chunk(starts, me * own + half, own)
    place_keys(kv_refs, kv_ref, begin, me)
    wide = heads * own
    tied = groups * HD
    plain = HD - RD
    q_doc = stack_queries(starts, me * own, half, heads)
    q_all, do_all = q_ref[...], do_ref[...]
    pad_q = jnp.zeros((LANE - HD - 32, wide), BF)
    pad_d = jnp.zeros((LANE - HD - 16, wide), BF)
    row_at = lax.broadcasted_iota(jnp.int32, (own, own), 0)
    column_at = lax.broadcasted_iota(jnp.int32, (own, own), 1)
    identity = jnp.where(row_at == column_at, 1.0, 0.0).astype(BF)

    def turn(rows, ref):
        for h in range(0, heads, 2):
            pair = [rows[:, (h + i) * own : (h + i + 1) * own] for i in range(2)]
            turned = mxu(identity, jnp.concatenate(pair, axis=0), NT).astype(BF)
            ref[h * own : (h + 1) * own] = turned[:, :LANE]
            ref[(h + 1) * own : (h + 2) * own] = turned[:, LANE:]

    for g in range(groups):
        q_rows = stack_heads(q_all, g * heads * HD, heads)
        do_rows = stack_heads(do_all, g * heads * HD, heads)
        qs[g] = q_rows
        ds_[g] = do_rows
        lse_rows = three_parts(-lse_ref[0, g : g + 1], wide)
        delta_row = stack_heads(delta_ref[0], g * heads, heads, 1)
        delta_rows = three_parts(-delta_row, wide)
        turn(jnp.concatenate([q_rows, q_doc, lse_rows, pad_q], axis=0), qa.at[g])
        turn(jnp.concatenate([do_rows, delta_rows, pad_d], axis=0), da.at[g])
    ones = first_rows(3, own)
    pad_k = jnp.zeros((LANE - HD - 32, own), BF)
    pad_v = jnp.zeros((LANE - HD - 16, own), BF)

    seq, core = lax.axis_index("seq"), lax.axis_index("mp")
    steps = chunks // 2

    def deliver(j, value):
        k = lax.rem(j // 2 - seq + steps, steps)

        @pl.when(lax.rem(j, 2) == core)
        def _():
            keep_ref[k, 0] = value()

        @pl.when(lax.rem(j, 2) != core)
        def _():
            give_ref[k, 0] = value()

    def clear(j, carry):
        deliver(j, lambda: jnp.zeros(keep_ref.shape[2:], BF))
        return carry

    lax.fori_loop(0, begin, clear, 0)
    lax.fori_loop(me + 1, chunks, clear, 0)

    def block(j, rows, diagonal):
        doc = key_rows(starts, j * own, own)
        rope_rows = kv_ref[j, tied : tied + RD]
        rope_sum = jnp.zeros((RD, own), F32)

        def keys_of(g):
            return jnp.concatenate(
                [kv_ref[j, g * HD : g * HD + plain], rope_rows], axis=0
            )

        def products(g):
            values = kv_ref[j, g * HD : (g + 1) * HD]
            return (
                mxu(qa[g, :rows], jnp.concatenate([keys_of(g), doc, ones, pad_k], axis=0), NN),
                mxu(da[g, :rows], jnp.concatenate([values, ones, pad_v], axis=0), NN),
            )

        following = products(0)
        for g in range(groups):
            logits, slopes = following
            if g + 1 < groups:
                following = products(g + 1)
            keys = keys_of(g)
            weights = jnp.exp(logits)
            if diagonal:
                query_at = lax.broadcasted_iota(jnp.int32, (half, own), 0)
                key_at = lax.broadcasted_iota(jnp.int32, (half, own), 1)
                causal = jnp.concatenate(
                    [key_at <= query_at + s * half for s in range(2) for _ in range(heads)], axis=0
                )
                weights = jnp.where(causal, weights, 0.0)
            grads = (weights * slopes).astype(BF)
            grad_values = mxu(ds_[g, :, :rows], weights.astype(BF), NN)
            grad_keys = mxu(qs[g, :, :rows], grads, NN)
            keys_t = keys.T
            grad_queries = mxu(grads, jnp.concatenate([keys_t, keys_t], axis=1), NN)
            if diagonal:
                dq[g] = grad_queries
            else:
                dq[g, :rows] += grad_queries
            stage[g * HD : g * HD + plain] = (
                grad_values[:plain] + grad_keys[:plain]
            ).astype(BF)
            stage[g * HD + plain : (g + 1) * HD] = grad_values[plain:].astype(BF)
            rope_sum = rope_sum + grad_keys[plain:]
        stage[tied : tied + RD] = rope_sum.astype(BF)
        deliver(j, lambda: stage[...])

    block(me, wide, True)

    def both(j, carry):
        block(j, wide, False)
        return carry

    def first_only(j, carry):
        block(j, wide // 2, False)
        return carry

    lax.fori_loop(begin_second, me, both, 0)
    lax.fori_loop(begin, begin_second, first_only, 0)
    straight, ahead, behind = rot_ref[0], rot_ref[1], rot_ref[2]
    lane = lax.broadcasted_iota(jnp.int32, (half, LANE), 1)
    quarter = RD // 2
    for g in range(groups):
        for s in range(2):
            positions = slice(s * half, (s + 1) * half)
            for pair in range(heads // 2):
                at = (s * heads + 2 * pair) * half
                two = jnp.where(lane < HD, dq[g, at : at + half], dq[g, at + half : at + 2 * half])
                turned = (
                    two * straight[positions]
                    + pltpu.roll(two, LANE - quarter, 1) * ahead[positions]
                    + pltpu.roll(two, quarter, 1) * behind[positions]
                )
                to = (g * heads + 2 * pair) * HD
                dq_ref[positions, to : to + 2 * HD] = turned.astype(BF)


def attend_backward(docs, q, do, lse, delta, turns, kv, groups, heads, first, size, kv_at, into):
    kv_rows, own = kv[0].shape[2:]
    count, chunks, inputs = docs.shape[0], 2 * lax.axis_size("seq"), len(kv)
    wide = heads * own
    width = q.shape[0]
    column = pl.BlockSpec((width, own), lambda b: (0, b + first))
    hbm = pl.BlockSpec(memory_space=pl.ANY)
    return pl.pallas_call(
        functools.partial(attend_back_kernel, groups, heads, first, inputs),
        grid=(size,),
        in_specs=[
            pl.BlockSpec(memory_space=pltpu.SMEM),
            column,
            column,
            pl.BlockSpec((1, groups, wide), lambda b: (b + first, 0, 0)),
            pl.BlockSpec((1, groups * heads, own), lambda b: (b + first, 0, 0)),
            pl.BlockSpec(turns.shape, lambda b: (0, 0, 0)),
        ]
        + kv_specs(kv, kv_at)
        + [hbm] * len(into),
        out_specs=[
            pl.BlockSpec((own, width), lambda b: (b + first, 0)),
            pl.BlockSpec((chunks // 2, 1, kv_rows, own), lambda b: (0, b, 0, 0)),
            pl.BlockSpec((chunks // 2, 1, kv_rows, own), lambda b: (0, b, 0, 0)),
        ],
        out_shape=[
            jax.ShapeDtypeStruct((count * own, width), BF),
            jax.ShapeDtypeStruct((chunks // 2, size, kv_rows, own), BF),
            jax.ShapeDtypeStruct((chunks // 2, size, kv_rows, own), BF),
        ],
        scratch_shapes=[
            pltpu.VMEM((chunks, kv_rows, own), BF),
            pltpu.VMEM((kv_rows, own), BF),
            pltpu.VMEM((groups, HD, wide), BF),
            pltpu.VMEM((groups, wide, LANE), BF),
            pltpu.VMEM((groups, HD, wide), BF),
            pltpu.VMEM((groups, wide, LANE), BF),
            pltpu.VMEM((groups, wide, LANE), F32),
        ],
        input_output_aliases={6 + inputs + i: i for i in range(len(into))},
        compiler_params=params(),
        cost_estimate=cost(10**9 * size),
        name="attend_back",
    )(docs, q, do, lse, delta, turns, *kv, *into)


def join_cores(keep, give):
    received = swap_cores(give)
    return [
        (keep[k].astype(F32) + received[k].astype(F32)).astype(BF) for k in range(keep.shape[0])
    ]


def send_keys(summed):
    return [summed[0]] + [shift(summed[k], "seq", k) for k in range(1, len(summed))]


def load_weights(refs, targets, sems):
    copies = []
    slot = 0
    for (source, side, axis), target in zip(refs, targets, strict=True):
        blocks = source.shape[axis] // LANE
        for t in range(blocks):
            to = pl.ds((2 * t + side) * LANE, LANE)
            of = pl.ds(t * LANE, LANE)
            src = source.at[:, of] if axis == 1 else source.at[of]
            dst = target.at[:, to] if axis == 1 else target.at[to]
            copies.append(pltpu.make_async_copy(src, dst, sems.at[slot]))
            slot += 1
    return copies


def feed_kernel(
    x_ref, og_ref, ga_ref, o_ref, gain_ref, wo_ref, wgo_ref, wgp_ref, wuo_ref, wup_ref, wdo_ref, wdp_ref,
    out_ref, nt_ref, ogt_ref, act_ref, gg_ref, gu_ref, gh_ref, gat_ref, do_ref, delta_ref, gg2_ref,
    wo, wg, wu, wd, sems,
):
    b = pl.program_id(0)

    @pl.when(b == 0)
    def _():
        copies = [pltpu.make_async_copy(wo_ref, wo, sems.at[sems.shape[0] - 1])]
        copies += load_weights(
            [
                (wgo_ref, 0, 1), (wgp_ref, 1, 1), (wuo_ref, 0, 1), (wup_ref, 1, 1),
                (wdo_ref, 0, 0), (wdp_ref, 1, 0),
            ],
            [wg, wg, wu, wu, wd, wd],
            sems,
        )
        for copy in copies:
            copy.start()
        for copy in copies:
            copy.wait()
        gg2_ref[...] = jnp.zeros(gg2_ref.shape, F32)

    og = og_ref[0]
    heads_out = o_ref[...]
    gain = gain_ref[...]
    hidden = x_ref[0].astype(F32) + mxu(heads_out, wo[...], TN)
    inverse = lax.rsqrt(jnp.mean(hidden * hidden, axis=-1, keepdims=True) + epsilon)
    normed = (hidden * inverse * gain).astype(BF)
    nt_ref[...] = normed.T
    ogt_ref[...] = og.T
    units = wg.shape[1]
    tile = 2 * LANE
    for t in range(units // tile):
        at = slice(t * tile, (t + 1) * tile)
        gate = mxu(normed, wg[:, at], NN)
        up = mxu(normed, wu[:, at], NN)
        grad = ga_ref[:, at].astype(F32)
        sigmoid = 1.0 / (1.0 + jnp.exp(-gate))
        silu = gate * sigmoid
        act_ref[:, at] = (silu * up).astype(BF)
        gu_ref[:, at] = (grad * silu).astype(BF)
        gg_ref[:, at] = (grad * up * (sigmoid + silu * (1.0 - sigmoid))).astype(BF)
    result = mxu(act_ref[...], wd[...], NN)
    out_ref[0] = (hidden + result).astype(BF)
    grad_normed = mxu(gg_ref[...], wg[...], NT) + mxu(gu_ref[...], wu[...], NT)
    scaled = grad_normed * gain
    gg2_ref[...] += jnp.sum(grad_normed * (hidden * inverse), axis=0, keepdims=True)
    mean = jnp.mean(scaled * hidden, axis=-1, keepdims=True)
    grad_hidden = og.astype(F32) + inverse * scaled - hidden * (inverse * inverse * inverse * mean)
    gh_ref[0] = grad_hidden
    grad_attended = grad_hidden.astype(BF)
    gat_ref[...] = grad_attended.T
    grad_heads = mxu(wo[...], grad_attended, NT).astype(BF)
    do_ref[...] = grad_heads
    product = grad_heads.astype(F32) * heads_out.astype(F32)
    for h in range(product.shape[0] // HD):
        delta_ref[0, h : h + 1] = jnp.sum(product[h * HD : (h + 1) * HD], axis=0, keepdims=True)


def feed(x, og, slopes, heads_out, gain, wo, wg, wu, wd):
    count, own, width = x.shape
    hd = heads_out.shape[0]
    half = wg[0].shape[1]
    units = 2 * half
    tokens = count * own
    seq = pl.BlockSpec((1, own, width), lambda b: (b, 0, 0))
    column = lambda rows: pl.BlockSpec((rows, own), lambda b: (0, b))
    row = pl.BlockSpec((own, units), lambda b: (b, 0))
    hbm = pl.BlockSpec(memory_space=pl.ANY)
    return pl.pallas_call(
        feed_kernel,
        grid=(count,),
        in_specs=[seq, seq, row, column(hd), pl.BlockSpec((1, width), lambda b: (0, 0))] + [hbm] * 7,
        out_specs=[
            seq, column(width), column(width), row, row, row, seq, column(width), column(hd),
            pl.BlockSpec((1, hd // HD, own), lambda b: (b, 0, 0)),
            pl.BlockSpec((1, width), lambda b: (0, 0)),
        ],
        out_shape=[
            jax.ShapeDtypeStruct(x.shape, BF),
            jax.ShapeDtypeStruct((width, tokens), BF),
            jax.ShapeDtypeStruct((width, tokens), BF),
            jax.ShapeDtypeStruct((tokens, units), BF),
            jax.ShapeDtypeStruct((tokens, units), BF),
            jax.ShapeDtypeStruct((tokens, units), BF),
            jax.ShapeDtypeStruct(x.shape, F32),
            jax.ShapeDtypeStruct((width, tokens), BF),
            jax.ShapeDtypeStruct((hd, tokens), BF),
            jax.ShapeDtypeStruct((count, hd // HD, own), F32),
            jax.ShapeDtypeStruct((1, width), F32),
        ],
        scratch_shapes=[
            pltpu.VMEM((hd, width), BF),
            pltpu.VMEM((width, units), BF),
            pltpu.VMEM((width, units), BF),
            pltpu.VMEM((units, width), BF),
            pltpu.SemaphoreType.DMA((6 * (half // LANE) + 1,)),
        ],
        compiler_params=params(),
        cost_estimate=cost(2 * tokens * width * (5 * units + 2 * hd)),
        name="feed",
    )(x, og, slopes, heads_out, gain, wo, *wg, *wu, *wd)


def regroup_rows(value, split):
    if split is None:
        return value
    count_d, count_s = split
    own = value.shape[0] // (count_d * count_s)
    return jnp.concatenate(
        [
            value[(d * count_s + s) * own : (d * count_s + s + 1) * own]
            for s in range(count_s)
            for d in range(count_d)
        ],
        axis=0,
    )


def early_kernel(
    split, nt_ref, gg_ref, gu_ref, act_ref, act_next_ref, ogt_ref, gat_ref, o_ref, out_ref,
    ogt, gat, heads_out, stage, landed, load_sems, sends, receives,
):
    t = pl.program_id(0)
    core = lax.axis_index("mp")
    tiles = landed.shape[0]
    width = nt_ref.shape[0]
    tile = 2 * LANE
    pairs, head_tiles = gg_tiles(gg_ref, tiles, heads_out)
    other_core = {"mp": 1 - core}
    loads = [
        pltpu.make_async_copy(source, target, load_sems.at[i])
        for i, (source, target) in enumerate(((gat_ref, gat), (o_ref, heads_out), (ogt_ref, ogt)))
    ]

    @pl.when(t == 0)
    def _():
        for copy in loads:
            copy.start()
        barrier = pltpu.get_barrier_semaphore()
        pl.semaphore_signal(barrier, inc=1, device_id=other_core, device_id_type=pl.DeviceIdType.MESH)
        pl.semaphore_wait(barrier, 1)

    @pl.when(t == pairs)
    def _():
        loads[0].wait()
        loads[1].wait()

    @pl.when(t == pairs + head_tiles)
    def _():
        loads[2].wait()

    def send(i):
        return pltpu.make_async_remote_copy(
            src_ref=stage.at[lax.rem(i, 2)],
            dst_ref=landed.at[i],
            send_sem=sends.at[i],
            recv_sem=receives.at[i],
            device_id=other_core,
            device_id_type=pl.DeviceIdType.MESH,
        )

    def deliver(product):
        product = regroup_rows(product, split)

        @pl.when(t < tiles)
        def _():
            @pl.when(t >= 2)
            def _():
                send(t - 2).wait_send()

            stage[lax.rem(t, 2)] = product.astype(BF)
            send(t).start()

        @pl.when(t >= tiles)
        def _():
            @pl.when(t < tiles + 2)
            def _():
                send(t - 2).wait_send()

            send(t - tiles).wait_recv()
            out_ref[...] = (product + landed[t - tiles].astype(F32)).astype(BF)

    at = lax.rem(t, tiles)

    @pl.when(at < pairs)
    def _():
        deliver(mxu(nt_ref[...], jnp.concatenate([gg_ref[...], gu_ref[...]], axis=1), NN))

    @pl.when((at >= pairs) & (at < pairs + head_tiles))
    def _():
        side = jnp.where(t < tiles, 1 - core, core)
        row = pl.multiple_of((side * head_tiles + at - pairs) * tile, tile)
        deliver(mxu(gat[...], heads_out[pl.ds(row, tile)], NT))

    @pl.when(at >= pairs + head_tiles)
    def _():
        deliver(mxu(ogt[...], jnp.concatenate([act_ref[...], act_next_ref[...]], axis=1), NN))


def gg_tiles(gg_ref, tiles, heads_out):
    head_tiles = heads_out.shape[0] // (4 * LANE)
    return (2 * (tiles - head_tiles)) // 3, head_tiles


def early_grads(nt, gg, gu, act, ogt, gat, heads_out, split):
    width, tokens = nt.shape
    units = gg.shape[1]
    blocks = units // (2 * LANE)
    tile = 2 * LANE
    head_tiles = heads_out.shape[0] // (2 * tile)
    down_tiles = (blocks + 1) // 2
    tiles = blocks + head_tiles + down_tiles
    columns = units + units // 2 + heads_out.shape[0] // 2
    hbm = pl.BlockSpec(memory_space=pl.ANY)
    side = lambda t: jnp.where(t < tiles, 1, 0)

    def pair(t):
        return (0, 2 * jnp.minimum(lax.rem(t, tiles), blocks - 1) + side(t))

    def down(t, shift_by):
        at = jnp.clip(lax.rem(t, tiles) - blocks - head_tiles, 0, down_tiles - 1)
        return (0, 2 * jnp.minimum(2 * at + shift_by, blocks - 1) + side(t))

    block = lambda index: pl.BlockSpec((tokens, LANE), index)
    return pl.pallas_call(
        functools.partial(early_kernel, split),
        grid=(2 * tiles,),
        in_specs=[
            pl.BlockSpec((width, tokens), lambda t: (0, 0), pipeline_mode=pl.Buffered(1)),
            block(pair),
            block(pair),
            block(lambda t: down(t, 0)),
            block(lambda t: down(t, 1)),
            hbm,
            hbm,
            hbm,
        ],
        out_specs=pl.BlockSpec((width, tile), lambda t: (0, jnp.maximum(t - tiles, 0))),
        out_shape=jax.ShapeDtypeStruct((width, columns), BF),
        scratch_shapes=[
            pltpu.VMEM((width, tokens), BF),
            pltpu.VMEM((width, tokens), BF),
            pltpu.VMEM(heads_out.shape, BF),
            pltpu.VMEM((2, width, tile), BF),
            pltpu.VMEM((tiles, width, tile), BF),
            pltpu.SemaphoreType.DMA((3,)),
            pltpu.SemaphoreType.DMA((tiles,)),
            pltpu.SemaphoreType.DMA((tiles,)),
        ],
        compiler_params=pltpu.CompilerParams(
            vmem_limit_bytes=56 * MIB, collective_id=3, has_side_effects=True
        ),
        cost_estimate=cost(6 * 10**10),
        name="early_grads",
    )(nt, gg, gu, act, act, ogt, gat, heads_out)


def head_grads_kernel(core_ref, left_ref, right_ref, out_ref):
    out_ref[0] = mxu(left_ref[...], right_ref[...], NN).astype(BF)


def head_grads(left, right):
    rows, tokens = left.shape
    columns = right.shape[1]
    tile = 2 * LANE
    tiles = columns // tile
    part = tiles // 2
    return pl.pallas_call(
        head_grads_kernel,
        grid_spec=pltpu.PrefetchScalarGridSpec(
            num_scalar_prefetch=1,
            grid=(tiles,),
            in_specs=[
                pl.BlockSpec((rows, tokens), lambda t, core: (0, 0)),
                pl.BlockSpec((tokens, tile), lambda t, core: (0, (t + core[0] * part) % tiles)),
            ],
            out_specs=pl.BlockSpec((1, rows, tile), lambda t, core: (t // part, 0, t % part)),
        ),
        out_shape=jax.ShapeDtypeStruct((2, rows, columns // 2), BF),
        compiler_params=params(),
        cost_estimate=cost(10**8),
        name="head_grads",
    )(lax.axis_index("mp").astype(jnp.int32)[None], left, right)


def tail_kernel(
    order, x_ref, gh_ref, dq_ref, nt_ref, gain_ref, wq_ref, wkv_ref, cos_ref, sin_ref, gg2_ref,
    query_ref, near_refs, *refs,
):
    count_d, count_s = lax.axis_size("dp"), lax.axis_size("seq")
    me_d, me_s, core = lax.axis_index("dp"), lax.axis_index("seq"), lax.axis_index("mp")
    late = len(order) - len(near_refs)
    far_refs, refs = refs[:late], refs[late:]
    gi_ref, query_out, small_out = refs[:3]
    (
        key_in, query_in, query_sum, query_seq, query_part, query_dp, dw, gg1,
        small_other, small_in, small_sum, small_seq, small_part, small_dp, sends, receives,
    ) = refs[3:]
    rows = query_out.shape[0]
    step = pl.program_id(0)
    other_core = {"mp": 1 - core}
    seq_peers = [{"seq": lax.rem(me_s + k, count_s)} for k in range(1, count_s)]
    dp_peers = [{"dp": lax.rem(me_d + k, count_d)} for k in range(1, count_d)]
    peers = [other_core] + seq_peers + dp_peers
    slots = iter(range(sends.shape[0]))

    def link(source, target, peer):
        slot = next(slots)
        return pltpu.make_async_remote_copy(
            src_ref=source,
            dst_ref=target,
            send_sem=sends.at[slot],
            recv_sem=receives.at[slot],
            device_id=peer,
            device_id_type=pl.DeviceIdType.MESH,
        )

    to_seq = [lax.rem(me_s + k, count_s) for k in range(1, count_s)]
    to_dp = [lax.rem(me_d + k, count_d) for k in range(1, count_d)]
    key_copies, at = [], 0
    for far in far_refs:
        size = far.shape[1]
        key_copies.append(
            [
                link(far.at[k + 1], key_in.at[k, pl.ds(at, size)], seq_peers[k])
                for k in range(count_s - 1)
            ]
        )
        at += size
    query_core = link(query_ref.at[1], query_in, other_core)
    query_seqs = [
        link(query_sum.at[to_seq[k]], query_seq.at[k], seq_peers[k]) for k in range(count_s - 1)
    ]
    query_dps = [
        link(query_part.at[to_dp[k]], query_dp.at[k], dp_peers[k]) for k in range(count_d - 1)
    ]
    small_core = link(small_other, small_in, other_core)
    small_seqs = [
        link(small_sum.at[to_seq[k]], small_seq.at[k], seq_peers[k]) for k in range(count_s - 1)
    ]
    small_dps = [
        link(small_part.at[to_dp[k]], small_dp.at[k], dp_peers[k]) for k in range(count_d - 1)
    ]

    def start(copies):
        for copy in copies:
            copy.start()

    def by_seq(total, target):
        for s in range(count_s):
            for d in range(count_d):
                of = (d * count_s + s) * rows
                target[s, d * rows : (d + 1) * rows] = total[of : of + rows].astype(BF)

    def gather(own, copies, arrived):
        total = own.astype(F32)
        for k, copy in enumerate(copies):
            copy.wait()
            total = total + arrived[k].astype(F32)
        return total

    def by_dp(total, target):
        for d in range(count_d):
            target[d] = total[d * rows : (d + 1) * rows].astype(BF)

    @pl.when(step == 0)
    def _():
        barrier = pltpu.get_barrier_semaphore()
        for peer in peers:
            pl.semaphore_signal(barrier, inc=1, device_id=peer, device_id_type=pl.DeviceIdType.MESH)
        pl.semaphore_wait(barrier, len(peers))
        start([query_core])
        for copies in key_copies:
            start(copies)
        dw[...] = jnp.zeros(dw.shape, F32)
        gg1[...] = jnp.zeros(gg1.shape, F32)

    @pl.when(step == 1)
    def _():
        query_core.wait()
        by_seq(query_ref[0].astype(F32) + query_in[...].astype(F32), query_sum)
        start(query_seqs)

    tied = wkv_ref.shape[0] - RD

    def finish(summed):
        turned = rotate_rows(summed[tied:], cos_ref[...], -sin_ref[...])
        dkv = jnp.concatenate([summed[:tied], turned], axis=0).astype(BF)
        grad_normed = mxu(dq_ref[...], wq_ref[...], NN) + mxu(dkv, wkv_ref[...], TN)
        dw[...] += mxu(nt_ref[...], dkv, NT)
        x = x_ref[0].astype(F32)
        inverse = lax.rsqrt(jnp.mean(x * x, axis=-1, keepdims=True) + epsilon)
        scaled = grad_normed * gain_ref[...]
        gg1[...] += jnp.sum(grad_normed * (x * inverse), axis=0, keepdims=True)
        mean = jnp.mean(scaled * x, axis=-1, keepdims=True)
        gi_ref[0] = gh_ref[0] + inverse * scaled - x * (inverse * inverse * inverse * mean)

    begin = 0
    for (_, size), terms in zip(order, near_refs):

        @pl.when((step >= begin) & (step < begin + size))
        def _():
            summed = terms[0][0].astype(F32)
            for ref in terms[1:]:
                summed = summed + ref[0].astype(F32)
            finish(summed)

        begin += size

    base = begin
    for part, far in enumerate(far_refs):
        size = far.shape[1]

        @pl.when(step == begin)
        def _():
            for copy in key_copies[part]:
                copy.wait()

        @pl.when((step >= begin) & (step < begin + size))
        def _():
            at = step - base
            summed = far[0, step - begin].astype(F32)
            for k in range(count_s - 1):
                summed = summed + key_in[k, at].astype(F32)
            finish(summed)

        begin += size

    @pl.when(step == begin - 2)
    def _():
        total = gather(query_sum[me_s], query_seqs, query_seq)
        by_dp(total, query_part)
        start(query_dps)

    @pl.when(step == begin - 1)
    def _():
        width = dw.shape[0]
        pad = jnp.zeros((LANE - RD, width), F32)
        row = lax.broadcasted_iota(jnp.int32, (LANE, width), 0)
        gains = jnp.where(row == RD, gg1[...], 0.0)
        gains = jnp.where(row == RD + 1, gg2_ref[...], gains)
        weights = dw[...]
        rope = jnp.concatenate([weights[:, tied:], jnp.zeros((width, LANE - RD), F32)], axis=1)
        small = rope + gains.T
        half = tied // 2
        first, second = weights[:, :half], weights[:, half:tied]
        mine = jnp.concatenate([jnp.where(core == 0, first, second), small], axis=1)
        other = jnp.concatenate([jnp.where(core == 0, second, first), small], axis=1)
        small_other[...] = other.astype(BF)
        start([small_core])
        small_core.wait()
        by_seq(mine + small_in[...].astype(F32), small_sum)
        start(small_seqs)
        by_dp(gather(small_sum[me_s], small_seqs, small_seq), small_part)
        start(small_dps)
        query_out[...] = gather(query_part[me_d], query_dps, query_dp)
        small_out[...] = gather(small_part[me_d], small_dps, small_dp)


def tail(
    order, x, grad_hidden, dq, nt, gain, wq, wkv, cosine, sine_table, grad_gain_two, grad_query,
    near, far,
):
    count, own, width = x.shape
    count_d, count_s = lax.axis_size("dp"), lax.axis_size("seq")
    rows = width // (count_d * count_s)
    kv_rows = wkv.shape[0]
    tied = kv_rows - RD
    wide = grad_query.shape[2]
    narrow = tied // 2 + LANE
    sent = sum(part.shape[1] for part in far)

    def place(i):
        done, at = 0, i
        for first, size in order:
            at = jnp.where((i >= done) & (i < done + size), first + i - done, at)
            done += size
        return at

    seq = pl.BlockSpec((1, own, width), lambda i: (place(i), 0, 0))
    whole = lambda array: pl.BlockSpec(array.shape, lambda i: (0,) * array.ndim)
    near_specs, done = [], 0
    for (_, size), terms in zip(order, near):
        index = lambda i, done=done, size=size: (jnp.clip(i - done, 0, size - 1), 0, 0)
        near_specs += [pl.BlockSpec((1, kv_rows, own), index)] * len(terms)
        done += size
    fixed = [gain, wq, wkv, cosine, sine_table, grad_gain_two, grad_query]
    outs = [
        jax.ShapeDtypeStruct(x.shape, F32),
        jax.ShapeDtypeStruct((rows, wide), F32),
        jax.ShapeDtypeStruct((rows, narrow), F32),
    ]
    near_all = [term for terms in near for term in terms]

    def kernel(*refs):
        head, rest = refs[:11], refs[11 + len(near_all) :]
        nears = [refs[11 + i * count_s : 11 + (i + 1) * count_s] for i in range(len(near))]
        tail_kernel(order, *head, nears, *rest)

    slots = 2 * (count_d - 1) + (2 + len(far)) * (count_s - 1) + 2
    return pl.pallas_call(
        kernel,
        grid=(count,),
        in_specs=[
            seq, seq,
            pl.BlockSpec((own, dq.shape[1]), lambda i: (place(i), 0)),
            pl.BlockSpec((width, own), lambda i: (0, place(i))),
        ]
        + [whole(array) for array in fixed]
        + near_specs
        + [whole(array) for array in far],
        out_specs=[seq] + [whole(out) for out in outs[1:]],
        out_shape=outs,
        scratch_shapes=[
            pltpu.VMEM((count_s - 1, sent, kv_rows, own), BF),
            pltpu.VMEM((width, wide), BF),
            pltpu.VMEM((count_s, count_d * rows, wide), BF),
            pltpu.VMEM((count_s - 1, count_d * rows, wide), BF),
            pltpu.VMEM((count_d, rows, wide), BF),
            pltpu.VMEM((count_d - 1, rows, wide), BF),
            pltpu.VMEM((width, kv_rows), F32),
            pltpu.VMEM((1, width), F32),
            pltpu.VMEM((width, narrow), BF),
            pltpu.VMEM((width, narrow), BF),
            pltpu.VMEM((count_s, count_d * rows, narrow), BF),
            pltpu.VMEM((count_s - 1, count_d * rows, narrow), BF),
            pltpu.VMEM((count_d, rows, narrow), BF),
            pltpu.VMEM((count_d - 1, rows, narrow), BF),
            pltpu.SemaphoreType.DMA((slots,)),
            pltpu.SemaphoreType.DMA((slots,)),
        ],
        compiler_params=pltpu.CompilerParams(
            vmem_limit_bytes=56 * MIB, collective_id=1, has_side_effects=True
        ),
        cost_estimate=cost(4 * 10**10),
        name="tail",
    )(x, grad_hidden, dq, nt, *fixed, *near_all, *far)


def turn_tables(cosine, sine_table):
    plain = HD - RD
    one = jnp.ones((cosine.shape[0], plain), F32)
    none = jnp.zeros_like(one)
    quiet = jnp.zeros_like(sine_table)
    straight = jnp.concatenate([one, cosine, cosine], axis=1)
    ahead = jnp.concatenate([none, sine_table, quiet], axis=1)
    behind = jnp.concatenate([none, quiet, -sine_table], axis=1)
    tables = jnp.stack([jnp.concatenate([t, t], axis=1) for t in (straight, ahead, behind)])
    return tables * HD ** (-0.5)


def after(value, *others):
    return lax.optimization_barrier((value, *others))[0]


def on_device_fast(
    inputs, gain_one, w_query, w_tied, w_rope, w_out, gain_two, w_gate, w_up, w_down,
    doc_starts, out_grad,
):
    count, own, width = inputs.shape
    cores = lax.axis_size("mp")
    groups = cores * w_tied.shape[1] // HD
    all_heads = cores * w_query.shape[1] // HD
    heads = all_heads // groups
    mp_index = lax.axis_index("mp")
    split = (lax.axis_size("dp"), lax.axis_size("seq"))
    tied_t = w_tied.T
    tied_both = by_core(tied_t, swap_cores(tied_t), 0)
    keys_weights = jnp.concatenate([tied_both, w_rope.T], axis=0)
    query_t = w_query.T
    queries_weights = by_core(query_t, swap_cores(query_t), 0)
    down_other = swap_cores(w_down)
    gain_one_float = gain_one.astype(F32)[None]
    gain_two_float = gain_two.astype(F32)[None]
    cosine, sine_table = rope_tables(my_chunk() * own, own, RD)
    cosine_t, sine_t = cosine.T, sine_table.T
    half = count // 2
    kv, normed_t, q, slopes, kv_near, kv_far = project(
        inputs, out_grad, gain_one_float, keys_weights, queries_weights, (w_down, down_other),
        cosine_t, sine_t, half,
    )
    kv_late = send_near(kv[half:])
    out_other = swap_cores(w_out)
    gate_other, up_other = swap_cores(w_gate), swap_cores(w_up)
    span = half - half // 4
    made = attend_forward(doc_starts, q, [kv_near, kv_far], groups, heads, 0, span, 0, ())
    kv_late = send_far([after(part, *made) for part in kv_late])
    made = attend_forward(
        doc_starts, q, [kv_near, kv_far], groups, heads, span, half - span, span, made
    )
    heads_out, lse = attend_forward(doc_starts, q, kv_late, groups, heads, half, half, 0, made)
    out_both = by_core(w_out, out_other, 0)
    (
        outputs, normed_two_t, out_grad_t, active, grad_gate, grad_up, grad_hidden, grad_attended_t,
        grad_heads, delta, grad_gain_two,
    ) = feed(
        inputs, out_grad, slopes, heads_out, gain_two_float, out_both, (w_gate, gate_other),
        (w_up, up_other), (w_down, down_other),
    )
    units, head_half = w_gate.shape[1], w_out.shape[0]
    first_sum = early_grads(
        normed_two_t, grad_gate, grad_up, active, out_grad_t, grad_attended_t, heads_out, split
    )
    first_sum, grad_heads = lax.optimization_barrier((first_sum, grad_heads))
    first_sum = lax.psum_scatter(first_sum, "seq", scatter_dimension=0, tiled=True)

    turns = turn_tables(cosine, sine_table)
    quarter = half // 2
    backward = [
        (half, half, kv_late, 0),
        (quarter, half - quarter, [kv_near, kv_far], quarter),
        (0, quarter, [kv_near, kv_far], 0),
    ]
    dq, near, summed = (), [], None
    for part, (at, size, kv_part, kv_at) in enumerate(backward):
        need = []
        if part > 0:
            near.append(send_keys(summed))
            need = near[-1][:1]
        if part == 2:
            need = [first_sum, *near[0], near[1][0]]
        made_dq, keep, give = attend_backward(
            doc_starts, after(q, *need), grad_heads, lse, delta, turns, kv_part, groups, heads, at,
            size, kv_at, dq,
        )
        dq = (made_dq,)
        if part > 0:
            give = after(give, *near[-1])
        summed = join_cores(keep, give)
    first_sum = first_sum.reshape(split[0], -1, first_sum.shape[1])
    first_sum = add_up(send_steps(first_sum, "dp", 0))
    grad_query = head_grads(normed_t, dq[0])
    order = [span[:2] for span in backward]
    grad_inputs, query_sum, small_sum = tail(
        order, inputs, grad_hidden, dq[0], normed_t, gain_one_float, queries_weights, keys_weights,
        cosine_t, sine_t, grad_gain_two, grad_query, near,
        [jnp.stack(summed)],
    )
    half_tied = groups * HD // cores
    late_sum, small_sum = small_sum[:, :half_tied], small_sum[:, half_tied:]
    rows = small_sum.shape[0] // cores
    small_sum = lax.dynamic_slice_in_dim(small_sum, mp_index * rows, rows, 0)
    pairs = first_sum[:, : 2 * units].reshape(first_sum.shape[0], units // LANE, 2, LANE)
    gate_sum = pairs[:, :, 0].reshape(-1, units)
    up_sum = pairs[:, :, 1].reshape(-1, units)
    out_sum = first_sum[:, 2 * units : 2 * units + head_half]
    down_sum = first_sum[:, 2 * units + head_half :]
    return (
        outputs,
        grad_inputs,
        small_sum[:, RD],
        query_sum,
        late_sum,
        small_sum[:, :RD],
        out_sum.T,
        small_sum[:, RD + 1],
        gate_sum,
        up_sum,
        down_sum.T,
    )


def solution(mesh):
    in_specs = (
        P("dp", ("seq", "mp"), None),
        P(),
        P(None, "mp"),
        P(None, "mp"),
        P(),
        P("mp", None),
        P(),
        P(None, "mp"),
        P(None, "mp"),
        P("mp", None),
        P("dp", None),
        P("dp", ("seq", "mp"), None),
    )
    out_specs = (
        P("dp", ("seq", "mp"), None),
        P("dp", ("seq", "mp"), None),
        P(("dp", "seq", "mp")),
        P(("dp", "seq"), "mp"),
        P(("dp", "seq"), "mp"),
        P(("dp", "seq", "mp"), None),
        P("mp", ("dp", "seq")),
        P(("dp", "seq", "mp")),
        P(("dp", "seq"), "mp"),
        P(("dp", "seq"), "mp"),
        P("mp", ("dp", "seq")),
    )

    def local(inputs, *rest):
        step = on_device_fast if inputs.shape[1] % (2 * LANE) == 0 else on_device
        return step(inputs, *rest)

    return jax.shard_map(
        local, mesh=mesh, in_specs=in_specs, out_specs=out_specs, check_vma=False
    )
```

```python
import functools

import jax
import jax.numpy as jnp
from jax import lax
from jax.experimental import pallas as pl
from jax.experimental.pallas import tpu as pltpu
from jax.sharding import PartitionSpec as P

HD = 64
RD = 32


epsilon = 1e-05
rope_base = 10000.0
masked_value = -1e30


def rope_tables(offset, count, rope_width):
    position = (offset + jnp.arange(count, dtype=jnp.int32)).astype(jnp.float32)
    frequency = rope_base ** (-jnp.arange(rope_width // 2, dtype=jnp.float32) * 2.0 / rope_width)
    angles = position[:, None] * frequency[None, :]
    return (jnp.cos(angles), jnp.sin(angles))


def rotate(values, cosine, sine_table):
    half_width = values.shape[-1] // 2
    first_half = values[..., :half_width]
    second_half = values[..., half_width:]
    return jnp.concatenate(
        [
            first_half * cosine - second_half * sine_table,
            second_half * cosine + first_half * sine_table,
        ],
        axis=-1,
    )


def rotate_back(grads, cosine, sine_table):
    half_width = grads.shape[-1] // 2
    first_half = grads[..., :half_width]
    second_half = grads[..., half_width:]
    return jnp.concatenate(
        [
            first_half * cosine + second_half * sine_table,
            second_half * cosine - first_half * sine_table,
        ],
        axis=-1,
    )


def contract_rows(left, right):
    return lax.dot_general(
        left, right, (((0,), (0,)), ((), ())), preferred_element_type=jnp.float32
    )


def times_transposed(left, right):
    return lax.dot_general(
        left, right, (((1,), (1,)), ((), ())), preferred_element_type=jnp.float32
    )


def norm_back(grad_normed, values, inverse, gain):
    scaled = grad_normed * gain
    grad_gain = jnp.sum(grad_normed * values * inverse, axis=(0, 1))
    grad_values = inverse * scaled - values * inverse**3 * jnp.mean(
        scaled * values, axis=-1, keepdims=True
    )
    return (grad_values, grad_gain)


def attend(operands):
    queries, key_full, values, allowed = operands
    scores = jnp.einsum(
        "qghd,kgd->ghqk", queries, key_full, preferred_element_type=jnp.float32
    ) * HD ** (-0.5)
    masked = jnp.where(allowed[None, None], scores, masked_value)
    row_max = jnp.max(masked, axis=-1, keepdims=True)
    weights = jnp.exp(masked - row_max)
    row_total = jnp.sum(weights, axis=-1, keepdims=True)
    attention_probs = (weights / row_total).astype(jnp.bfloat16)
    combined = jnp.einsum(
        "ghqk,kgd->qghd", attention_probs, values, preferred_element_type=jnp.float32
    )
    return (combined.astype(jnp.bfloat16), row_max + jnp.log(row_total))


def attend_back(operands):
    queries, key_full, values, allowed, log_total, grad_heads = operands
    score_scale = HD ** (-0.5)
    plain_width = HD - RD
    scores = (
        jnp.einsum("qghd,kgd->ghqk", queries, key_full, preferred_element_type=jnp.float32)
        * score_scale
    )
    masked = jnp.where(allowed[None, None], scores, masked_value)
    probs_float = jnp.exp(masked - log_total)
    grad_probs = jnp.einsum(
        "qghd,kgd->ghqk", grad_heads, values, preferred_element_type=jnp.float32
    )
    row_delta = jnp.sum(probs_float * grad_probs, axis=-1, keepdims=True)
    grad_scores = (probs_float * (grad_probs - row_delta)).astype(jnp.bfloat16)
    grad_queries = (
        jnp.einsum("ghqk,kgd->qghd", grad_scores, key_full, preferred_element_type=jnp.float32)
        * score_scale
    )
    grad_keys = (
        jnp.einsum("ghqk,qghd->kgd", grad_scores, queries, preferred_element_type=jnp.float32)
        * score_scale
    )
    grad_values = jnp.einsum(
        "ghqk,qghd->kgd",
        probs_float.astype(jnp.bfloat16),
        grad_heads,
        preferred_element_type=jnp.float32,
    )
    grad_tied = grad_values + jnp.concatenate(
        [grad_keys[..., :plain_width], jnp.zeros_like(grad_keys[..., plain_width:])], axis=-1
    )
    grad_rope = jnp.sum(grad_keys[..., plain_width:], axis=1)
    return (grad_queries, grad_tied, grad_rope)


def on_device(
    inputs,
    gain_one,
    w_query,
    w_tied,
    w_rope,
    w_out,
    gain_two,
    w_gate,
    w_up,
    w_down,
    doc_starts,
    out_grad,
):
    seq_count, own_count, model_width = inputs.shape
    plain_width = HD - RD
    group_local = w_tied.shape[1] // HD
    head_local = w_query.shape[1] // HD
    seq_index = lax.axis_index("seq")
    mp_index = lax.axis_index("mp")
    gain_one_float = gain_one.astype(jnp.float32)
    gain_two_float = gain_two.astype(jnp.float32)
    inputs_float = inputs.astype(jnp.float32)
    inverse_one = lax.rsqrt(jnp.mean(inputs_float * inputs_float, axis=-1, keepdims=True) + epsilon)
    normed_one = (inputs_float * inverse_one * gain_one_float).astype(jnp.bfloat16)
    gathered_one = lax.all_gather(normed_one, "mp", axis=1, tiled=True)
    context = gathered_one.shape[1]
    token_count = seq_count * context
    flat_one = gathered_one.reshape(token_count, model_width)
    offset = seq_index * context
    cosine, sine_table = rope_tables(offset, context, RD)
    query_lin = jnp.dot(flat_one, w_query, preferred_element_type=jnp.float32).reshape(
        seq_count, context, head_local, HD
    )
    queries = jnp.concatenate(
        [
            query_lin[..., :plain_width],
            rotate(
                query_lin[..., plain_width:], cosine[None, :, None, :], sine_table[None, :, None, :]
            ),
        ],
        axis=-1,
    ).astype(jnp.bfloat16)
    queries = queries.reshape(seq_count, context, group_local, head_local // group_local, HD)
    tied_state = (
        jnp.dot(flat_one, w_tied, preferred_element_type=jnp.float32)
        .astype(jnp.bfloat16)
        .reshape(seq_count, context, group_local * HD)
    )
    rope_lin = jnp.dot(flat_one, w_rope, preferred_element_type=jnp.float32).reshape(
        seq_count, context, RD
    )
    rope_keys = rotate(rope_lin, cosine[None], sine_table[None]).astype(jnp.bfloat16)
    tied_all, rope_all = (
        lax.all_gather(tied_state, "seq", axis=1, tiled=True),
        lax.all_gather(rope_keys, "seq", axis=1, tiled=True),
    )
    length = tied_all.shape[1]
    values_all = tied_all.reshape(seq_count, length, group_local, HD)
    key_full = jnp.concatenate(
        [
            values_all[..., :plain_width],
            jnp.broadcast_to(rope_all[:, :, None, :], (seq_count, length, group_local, RD)),
        ],
        axis=-1,
    )
    key_position = jnp.arange(length, dtype=jnp.int32)
    key_segment = jnp.sum(
        (doc_starts[:, None, :] <= key_position[None, :, None]).astype(jnp.int32), axis=-1
    )
    query_segment = lax.dynamic_slice_in_dim(key_segment, offset, context, 1)
    query_position = offset + jnp.arange(context, dtype=jnp.int32)
    allowed = (query_segment[:, :, None] == key_segment[:, None, :]) & (
        query_position[:, None] >= key_position[None, :]
    )[None]
    head_outputs, log_total = lax.map(attend, (queries, key_full, values_all, allowed))
    flat_heads = head_outputs.reshape(token_count, head_local * HD)
    attended_part = jnp.dot(flat_heads, w_out, preferred_element_type=jnp.float32).reshape(
        seq_count, context, model_width
    )
    attended = lax.psum_scatter(
        attended_part.astype(jnp.bfloat16), "mp", scatter_dimension=1, tiled=True
    ).astype(jnp.float32)
    hidden = inputs_float + attended
    inverse_two = lax.rsqrt(jnp.mean(hidden * hidden, axis=-1, keepdims=True) + epsilon)
    normed_two = (hidden * inverse_two * gain_two_float).astype(jnp.bfloat16)
    gathered_two = lax.all_gather(normed_two, "mp", axis=1, tiled=True)
    flat_two = gathered_two.reshape(token_count, model_width)
    gate_values = jnp.dot(flat_two, w_gate, preferred_element_type=jnp.float32)
    up_values = jnp.dot(flat_two, w_up, preferred_element_type=jnp.float32)
    sigmoid_gate = jax.nn.sigmoid(gate_values)
    silu_gate = gate_values * sigmoid_gate
    active = (silu_gate * up_values).astype(jnp.bfloat16)
    result_part = jnp.dot(active, w_down, preferred_element_type=jnp.float32).reshape(
        seq_count, context, model_width
    )
    result = lax.psum_scatter(
        result_part.astype(jnp.bfloat16), "mp", scatter_dimension=1, tiled=True
    ).astype(jnp.float32)
    outputs = (hidden + result).astype(jnp.bfloat16)
    grad_out_all = lax.all_gather(out_grad, "mp", axis=1, tiled=True)
    flat_grad = grad_out_all.reshape(token_count, model_width)
    grad_active = times_transposed(flat_grad, w_down)
    grad_w_down = contract_rows(active, flat_grad)
    grad_gate = (
        grad_active * up_values * sigmoid_gate * (1.0 + gate_values * (1.0 - sigmoid_gate))
    ).astype(jnp.bfloat16)
    grad_up = (grad_active * silu_gate).astype(jnp.bfloat16)
    grad_w_gate = contract_rows(flat_two, grad_gate)
    grad_w_up = contract_rows(flat_two, grad_up)
    grad_two_part = (times_transposed(grad_gate, w_gate) + times_transposed(grad_up, w_up)).reshape(
        seq_count, context, model_width
    )
    grad_normed_two = lax.psum_scatter(
        grad_two_part.astype(jnp.bfloat16), "mp", scatter_dimension=1, tiled=True
    ).astype(jnp.float32)
    grad_hidden_norm, grad_gain_two = norm_back(
        grad_normed_two, hidden, inverse_two, gain_two_float
    )
    grad_hidden = out_grad.astype(jnp.float32) + grad_hidden_norm
    grad_attended_all = lax.all_gather(grad_hidden.astype(jnp.bfloat16), "mp", axis=1, tiled=True)
    flat_attended = grad_attended_all.reshape(token_count, model_width)
    grad_w_out = contract_rows(flat_heads, flat_attended)
    grad_heads = times_transposed(flat_attended, w_out).astype(jnp.bfloat16).reshape(queries.shape)
    grad_queries, grad_tied, grad_rope = lax.map(
        attend_back, (queries, key_full, values_all, allowed, log_total, grad_heads)
    )
    grad_queries = grad_queries.reshape(seq_count, context, head_local, HD)
    grad_query_lin = (
        jnp.concatenate(
            [
                grad_queries[..., :plain_width],
                rotate_back(
                    grad_queries[..., plain_width:],
                    cosine[None, :, None, :],
                    sine_table[None, :, None, :],
                ),
            ],
            axis=-1,
        )
        .astype(jnp.bfloat16)
        .reshape(token_count, head_local * HD)
    )
    tied_own, rope_context = (
        lax.psum_scatter(
            grad_tied.reshape(seq_count, length, group_local * HD).astype(jnp.bfloat16),
            "seq",
            scatter_dimension=1,
            tiled=True,
        ).astype(jnp.float32),
        lax.psum_scatter(
            grad_rope.astype(jnp.bfloat16), "seq", scatter_dimension=1, tiled=True
        ).astype(jnp.float32),
    )
    grad_tied_flat = tied_own.astype(jnp.bfloat16).reshape(token_count, group_local * HD)
    grad_one_part = (
        times_transposed(grad_query_lin, w_query) + times_transposed(grad_tied_flat, w_tied)
    ).reshape(seq_count, context, model_width)
    grad_normed_one, rope_own = (
        lax.psum_scatter(
            grad_one_part.astype(jnp.bfloat16), "mp", scatter_dimension=1, tiled=True
        ).astype(jnp.float32),
        lax.psum_scatter(
            rope_context.astype(jnp.bfloat16), "mp", scatter_dimension=1, tiled=True
        ).astype(jnp.float32),
    )
    own_offset = offset + mp_index * own_count
    cosine_own, sine_own = rope_tables(own_offset, own_count, RD)
    grad_rope_flat = (
        rotate_back(rope_own, cosine_own[None], sine_own[None])
        .astype(jnp.bfloat16)
        .reshape(seq_count * own_count, RD)
    )
    grad_normed_one = grad_normed_one + times_transposed(grad_rope_flat, w_rope).reshape(
        seq_count, own_count, model_width
    )
    grad_w_rope = contract_rows(
        normed_one.reshape(seq_count * own_count, model_width), grad_rope_flat
    )
    grad_w_query = contract_rows(flat_one, grad_query_lin)
    grad_w_tied = contract_rows(flat_one, grad_tied_flat)
    grad_inputs_norm, grad_gain_one = norm_back(
        grad_normed_one, inputs_float, inverse_one, gain_one_float
    )
    grad_inputs = grad_hidden + grad_inputs_norm
    small_sums = (
        lax.psum_scatter(grad_gain_one, ("dp", "seq", "mp"), scatter_dimension=0, tiled=True),
        lax.psum_scatter(grad_w_rope, ("dp", "seq", "mp"), scatter_dimension=0, tiled=True),
        lax.psum_scatter(grad_gain_two, ("dp", "seq", "mp"), scatter_dimension=0, tiled=True),
    )
    weight_terms = (grad_w_query, grad_w_tied, grad_w_out, grad_w_gate, grad_w_up, grad_w_down)
    weight_sums = (
        lax.psum_scatter(weight_terms[0], ("dp", "seq"), scatter_dimension=0, tiled=True),
        lax.psum_scatter(weight_terms[1], ("dp", "seq"), scatter_dimension=0, tiled=True),
        lax.psum_scatter(weight_terms[2], ("dp", "seq"), scatter_dimension=1, tiled=True),
        lax.psum_scatter(weight_terms[3], ("dp", "seq"), scatter_dimension=0, tiled=True),
        lax.psum_scatter(weight_terms[4], ("dp", "seq"), scatter_dimension=0, tiled=True),
        lax.psum_scatter(weight_terms[5], ("dp", "seq"), scatter_dimension=1, tiled=True),
    )
    return (
        outputs,
        grad_inputs,
        small_sums[0],
        weight_sums[0],
        weight_sums[1],
        small_sums[1],
        weight_sums[2],
        small_sums[2],
        weight_sums[3],
        weight_sums[4],
        weight_sums[5],
    )


BF = jnp.bfloat16
F32 = jnp.float32
NN = (((1,), (0,)), ((), ()))
NT = (((1,), (1,)), ((), ()))
TN = (((0,), (0,)), ((), ()))
BIG = 2.0**100
MIB = 1 << 20
LANE = 128


def mxu(left, right, dims):
    return lax.dot_general(left, right, dims, preferred_element_type=F32)


def params(limit=56):
    return pltpu.CompilerParams(vmem_limit_bytes=limit * MIB)


def cost(flops, moved=0):
    return pl.CostEstimate(flops=int(flops), bytes_accessed=int(moved), transcendentals=0)


def swap_cores(value):
    return lax.ppermute(value, "mp", [(0, 1), (1, 0)])


def shift(value, axis, by):
    size = lax.axis_size(axis)
    return lax.ppermute(value, axis, [(i, (i + by) % size) for i in range(size)])


def send_near(kv):
    return [kv] + [shift(kv, "seq", k) for k in range(1, lax.axis_size("seq"))]


def send_far(near):
    return [part[None] for part in near + [swap_cores(value) for value in near]]


def pick(value, index, axis):
    return lax.dynamic_index_in_dim(value, index, axis, keepdims=False)


def send_steps(value, axis, dim):
    size, me = lax.axis_size(axis), lax.axis_index(axis)
    terms = [pick(value, me, dim)]
    for k in range(1, size):
        terms.append(shift(pick(value, (me + k) % size, dim), axis, k))
    return terms


def add_up(terms):
    total = terms[0].astype(F32)
    for term in terms[1:]:
        total = total + term.astype(F32)
    return total


def by_core(own, other, axis):
    first = lax.axis_index("mp") == 0
    return jnp.concatenate(
        [jnp.where(first, own, other), jnp.where(first, other, own)], axis=axis
    )


def rotate_rows(values, cosine, sine_table):
    half = values.shape[0] // 2
    a, b = values[:half], values[half:]
    return jnp.concatenate([a * cosine - b * sine_table, b * cosine + a * sine_table], axis=0)


def project_kernel(
    sent, x_ref, og_ref, gain_ref, wqo_ref, wqp_ref, wto_ref, wtp_ref, wr_ref, wdo_ref, wdp_ref,
    cos_ref, sin_ref, kv_ref, nt_ref, q_ref, ga_ref, wq_ref, wkv_ref, near_ref, far_ref,
    kept, wd, load_sems, own_sems, sends, receives,
):
    b = pl.program_id(0)
    count_s = lax.axis_size("seq")
    me_s, core = lax.axis_index("seq"), lax.axis_index("mp")
    peers = [{"seq": lax.rem(me_s + k, count_s)} for k in range(1, count_s)]
    other_core = {"mp": 1 - core}
    near, forward = [], []
    slots = iter(range(sends.shape[0]))

    def link(source, target, peer):
        slot = next(slots)
        return pltpu.make_async_remote_copy(
            src_ref=source,
            dst_ref=target,
            send_sem=sends.at[slot],
            recv_sem=receives.at[slot],
            device_id=peer,
            device_id_type=pl.DeviceIdType.MESH,
        )

    for i in range(sent):
        near.append([link(kept.at[i], near_ref.at[k, i], peers[k - 1]) for k in range(1, count_s)])
        forward.append(
            [link(kept.at[i], far_ref.at[0, i], other_core)]
            + [link(near_ref.at[k, i], far_ref.at[k, i], other_core) for k in range(1, count_s)]
        )
    own = [pltpu.make_async_copy(kept.at[i], near_ref.at[0, i], own_sems.at[i]) for i in range(sent)]
    loads = load_weights([(wdo_ref, 0, 0), (wdp_ref, 1, 0)], [wd, wd], load_sems)

    @pl.when(b == 0)
    def _():
        for copy in loads:
            copy.start()
        barrier = pltpu.get_barrier_semaphore()
        for peer in [other_core] + peers:
            pl.semaphore_signal(barrier, inc=1, device_id=peer, device_id_type=pl.DeviceIdType.MESH)
        pl.semaphore_wait(barrier, count_s)

        def turn(source, target, at):
            size = source.shape[1]
            row = lax.broadcasted_iota(jnp.int32, (size, size), 0)
            column = lax.broadcasted_iota(jnp.int32, (size, size), 1)
            identity = jnp.where(row == column, 1.0, 0.0).astype(BF)
            target[pl.ds(at, size)] = mxu(identity, source[...], NT).astype(BF)

        for pair, target in (((wto_ref, wtp_ref), wkv_ref), ((wqo_ref, wqp_ref), wq_ref)):
            size = pair[0].shape[1]
            for side, source in enumerate(pair):
                place = jnp.where(core == side, 0, 1)
                turn(source, target, pl.multiple_of(place * size, size))
        turn(wr_ref, wkv_ref, wkv_ref.shape[0] - RD)

    x = x_ref[0].astype(F32)
    inverse = lax.rsqrt(jnp.mean(x * x, axis=-1, keepdims=True) + epsilon)
    normed = (x * inverse * gain_ref[...]).astype(BF)
    lin = mxu(wkv_ref[...], normed, NT)
    tied = wkv_ref.shape[0] - RD
    cosine, sine_table = cos_ref[...], sin_ref[...]
    rope = rotate_rows(lin[tied:], cosine, sine_table)
    keys = jnp.concatenate([lin[:tied], rope], axis=0).astype(BF)
    @pl.when(b >= sent)
    def _():
        kv_ref[0] = keys

    for i in range(sent):

        @pl.when(b == i)
        def _():
            kept[i] = keys
            for copy in near[i]:
                copy.start()
            forward[i][0].start()
            own[i].start()

    nt_ref[0] = normed.T
    lin = mxu(wq_ref[...], normed, NT)
    plain = HD - RD
    pieces = []
    for at in range(0, lin.shape[0], HD):
        pieces.append(lin[at : at + plain])
        pieces.append(rotate_rows(lin[at + plain : at + HD], cosine, sine_table))
    queries = jnp.concatenate(pieces, axis=0)
    q_ref[0] = (queries.astype(BF) * HD ** (-0.5)).astype(BF)

    @pl.when(b == 0)
    def _():
        for copy in loads:
            copy.wait()

    og = og_ref[0]
    for at in range(0, wd.shape[0], 2 * LANE):
        to = slice(at, at + 2 * LANE)
        ga_ref[:, to] = mxu(og, wd[to], NT).astype(BF)

    steps = pl.num_programs(0)
    for i in range(sent):

        @pl.when(b == steps - 1 - (3 * (sent - 1 - i) + 1) // 2)
        def _():
            for copy in near[i]:
                copy.wait()
            for copy in forward[i][1:]:
                copy.start()

    @pl.when(b == steps - 1)
    def _():
        for i in range(sent):
            own[i].wait()
            for copy in forward[i]:
                copy.wait()


def project(x, og, gain, wq, wt, wr, wd, cosine, sine_table, sent):
    count, own, width = x.shape
    rows, half = 2 * wq[0].shape[1], wd[0].shape[0]
    kv_rows = 2 * wt[0].shape[1] + wr.shape[1]
    weights = [*wq, *wt, wr]
    count_s = lax.axis_size("seq")
    whole = lambda array: pl.BlockSpec(array.shape, lambda b: (0, 0))
    seq = pl.BlockSpec((1, own, width), lambda b: (b, 0, 0))
    hbm = pl.BlockSpec(memory_space=pl.ANY)
    gathered = jax.ShapeDtypeStruct((count_s, sent, kv_rows, own), BF)
    links = sent * (2 * count_s - 1)
    return pl.pallas_call(
        functools.partial(project_kernel, sent),
        grid=(count,),
        in_specs=[
            seq, seq, whole(gain), *[whole(part) for part in weights], hbm, hbm, whole(cosine),
            whole(cosine),
        ],
        out_specs=[
            pl.BlockSpec((1, kv_rows, own), lambda b: (jnp.maximum(b - sent, 0), 0, 0)),
            pl.BlockSpec((1, width, own), lambda b: (b, 0, 0)),
            pl.BlockSpec((1, rows, own), lambda b: (b, 0, 0)),
            pl.BlockSpec((own, 2 * half), lambda b: (b, 0)),
            pl.BlockSpec((rows, width), lambda b: (0, 0)),
            pl.BlockSpec((kv_rows, width), lambda b: (0, 0)),
            hbm,
            hbm,
        ],
        out_shape=[
            jax.ShapeDtypeStruct((count - sent, kv_rows, own), BF),
            jax.ShapeDtypeStruct((count, width, own), BF),
            jax.ShapeDtypeStruct((count, rows, own), BF),
            jax.ShapeDtypeStruct((count * own, 2 * half), BF),
            jax.ShapeDtypeStruct((rows, width), BF),
            jax.ShapeDtypeStruct((kv_rows, width), BF),
            gathered,
            gathered,
        ],
        scratch_shapes=[
            pltpu.VMEM((sent, kv_rows, own), BF),
            pltpu.VMEM((2 * half, width), BF),
            pltpu.SemaphoreType.DMA((2 * (half // LANE),)),
            pltpu.SemaphoreType.DMA((sent,)),
            pltpu.SemaphoreType.DMA((links,)),
            pltpu.SemaphoreType.DMA((links,)),
        ],
        compiler_params=pltpu.CompilerParams(
            vmem_limit_bytes=56 * MIB, collective_id=2, has_side_effects=True
        ),
        cost_estimate=cost(3 * 10**10),
        name="project",
    )(x, og, gain, *weights, *wd, cosine, sine_table)


def segment_counts(starts, first, width):
    position = first + lax.broadcasted_iota(jnp.int32, (1, width), 1)
    count = jnp.zeros((1, width), jnp.int32)
    for start in starts:
        count = count + (start <= position).astype(jnp.int32)
    return count


def query_rows(starts, first, width):
    row = lax.broadcasted_iota(jnp.int32, (16, width), 0)
    match = segment_counts(starts, first, width) == row + 1
    return jnp.where(match, 1.0, 0.0).astype(BF)


def key_rows(starts, first, width):
    row = lax.broadcasted_iota(jnp.int32, (16, width), 0)
    match = (segment_counts(starts, first, width) == row + 1) | (row >= len(starts))
    return jnp.where(match, 0.0, -BIG).astype(BF)


def first_rows(count, width):
    row = lax.broadcasted_iota(jnp.int32, (16, width), 0)
    return jnp.where(row < count, 1.0, 0.0).astype(BF)


def three_parts(row, width):
    high = row.astype(BF)
    rest = row - high.astype(F32)
    middle = rest.astype(BF)
    low = (rest - middle.astype(F32)).astype(BF)
    at = lax.broadcasted_iota(jnp.int32, (16, width), 0)
    parts = jnp.where(at == 0, high.astype(F32), 0.0)
    parts = jnp.where(at == 1, middle.astype(F32), parts)
    return jnp.where(at == 2, low.astype(F32), parts).astype(BF)


def start_chunk(starts, first, chunk):
    begin = jnp.int32(0)
    for start in starts:
        begin = jnp.where(start <= first, jnp.maximum(begin, start), begin)
    return begin // chunk


def my_chunk():
    return lax.axis_index("seq") * lax.axis_size("mp") + lax.axis_index("mp")


def place_keys(refs, kv, begin, me):
    steps = lax.axis_size("seq")
    seq, core = lax.axis_index("seq"), lax.axis_index("mp")
    places = [(ref, i) for ref in refs for i in range(ref.shape[0])]
    for at, (ref, i) in enumerate(places):
        of = core if at < steps else 1 - core
        j = lax.rem(seq - at % steps + steps, steps) * 2 + of

        @pl.when((j >= begin) & (j <= me))
        def _():
            kv[j] = ref[i, 0]


def stack_heads(value, at, heads, rows=HD):
    half = value.shape[1] // 2
    return jnp.concatenate(
        [
            value[at + h * rows : at + (h + 1) * rows, s * half : (s + 1) * half]
            for s in range(2)
            for h in range(heads)
        ],
        axis=1,
    )


def stack_queries(starts, first, half, heads):
    return jnp.concatenate(
        [query_rows(starts, first + s * half, half) for s in range(2) for _ in range(heads)], axis=1
    )


def attend_kernel(groups, heads, first, inputs, docs_ref, q_ref, *refs):
    kv_refs = refs[:inputs]
    out_ref, lse_ref, kv_ref, qa, acc, top = refs[-6:]
    b = pl.program_id(0) + first
    own = q_ref.shape[2]
    ndoc = docs_ref.shape[1]
    starts = [docs_ref[b, k] for k in range(ndoc)]
    me = my_chunk()
    begin = start_chunk(starts, me * own, own)
    half = own // 2
    begin_second = start_chunk(starts, me * own + half, own)
    place_keys(kv_refs, kv_ref, begin, me)
    wide = heads * own
    first_half = wide // 2
    tied = groups * HD
    plain = HD - RD
    q_doc = stack_queries(starts, me * own, half, heads)
    q_all = q_ref[0]
    for g in range(groups):
        qa[g, :HD] = stack_heads(q_all, g * heads * HD, heads)
        qa[g, HD : HD + 16] = q_doc
        qa[g, HD + 16 :] = jnp.zeros((LANE - HD - 16, wide), BF)
    ones = first_rows(1, own)
    zeros = jnp.zeros((LANE - HD - 16, own), BF)

    def keys_of(j, g):
        doc = key_rows(starts, j * own, own)
        block = jnp.concatenate(
            [
                kv_ref[j, g * HD : g * HD + plain],
                kv_ref[j, tied : tied + RD],
                doc,
                zeros,
            ],
            axis=0,
        )
        return block.T

    def values_of(j, g):
        return jnp.concatenate([kv_ref[j, g * HD : (g + 1) * HD], ones], axis=0)

    key_at = lax.broadcasted_iota(jnp.int32, (own, half), 0)
    query_at = lax.broadcasted_iota(jnp.int32, (own, half), 1)
    causal = jnp.concatenate(
        [key_at <= query_at + s * half for s in range(2) for _ in range(heads)], axis=1
    )

    def block(j, lanes, diagonal=False):
        def logits_of(g):
            return mxu(keys_of(j, g), qa[g, :, lanes], NN)

        following = logits_of(0)
        for g in range(groups):
            logits = following
            if g + 1 < groups:
                following = logits_of(g + 1)
            if diagonal:
                logits = jnp.where(causal, logits, masked_value)
            peak = jnp.max(logits, axis=0, keepdims=True)
            if not diagonal:
                old = top[g, :, lanes]
                peak = jnp.maximum(old, peak)
            weights = jnp.exp(logits - peak).astype(BF)
            added = mxu(values_of(j, g), weights, NN)
            if not diagonal:
                added = acc[g, :, lanes] * jnp.exp(old - peak) + added
            acc[g, :, lanes] = added
            top[g, :, lanes] = peak

    block(me, slice(0, wide), True)

    def both(i, carry):
        block(me - 1 - i, slice(0, wide))
        return carry

    def first_only(i, carry):
        block(begin_second - 1 - i, slice(0, first_half))
        return carry

    lax.fori_loop(0, me - begin_second, both, 0)
    lax.fori_loop(0, begin_second - begin, first_only, 0)
    for g in range(groups):
        total = acc[g, HD : HD + 1]
        result = acc[g, :HD] / total
        lse_ref[0, g : g + 1] = top[g] + jnp.log(total)
        for s in range(2):
            for h in range(heads):
                at, of = (g * heads + h) * HD, (s * heads + h) * half
                out_ref[0, at : at + HD, s * half : (s + 1) * half] = result[:, of : of + half].astype(BF)


def kv_specs(kv, kv_at):
    return [
        pl.BlockSpec((part.shape[0], 1, *part.shape[2:]), lambda b: (0, b + kv_at, 0, 0))
        for part in kv
    ]


def attend_forward(docs, q, kv, groups, heads, first, size, kv_at, into):
    kv_rows, own = kv[0].shape[2:]
    count, chunks, inputs = docs.shape[0], 2 * lax.axis_size("seq"), len(kv)
    wide = heads * own
    hbm = pl.BlockSpec(memory_space=pl.ANY)
    return pl.pallas_call(
        functools.partial(attend_kernel, groups, heads, first, inputs),
        grid=(size,),
        in_specs=[
            pl.BlockSpec(memory_space=pltpu.SMEM),
            pl.BlockSpec((1, q.shape[1], own), lambda b: (b + first, 0, 0)),
        ]
        + kv_specs(kv, kv_at)
        + [hbm] * len(into),
        out_specs=[
            pl.BlockSpec((1, q.shape[1], own), lambda b: (b + first, 0, 0)),
            pl.BlockSpec((1, groups, wide), lambda b: (b + first, 0, 0)),
        ],
        out_shape=[
            jax.ShapeDtypeStruct(q.shape, BF),
            jax.ShapeDtypeStruct((count, groups, wide), F32),
        ],
        scratch_shapes=[
            pltpu.VMEM((chunks, kv_rows, own), BF),
            pltpu.VMEM((groups, LANE, wide), BF),
            pltpu.VMEM((groups, HD + 16, wide), F32),
            pltpu.VMEM((groups, 1, wide), F32),
        ],
        input_output_aliases={2 + inputs + i: i for i in range(len(into))},
        compiler_params=params(),
        cost_estimate=cost(10**10 * size),
        name="attend",
    )(docs, q, *kv, *into)


def attend_back_kernel(
    groups, heads, first, inputs, docs_ref, q_ref, do_ref, lse_ref, delta_ref, rot_ref, *refs
):
    kv_refs = refs[:inputs]
    chunks = 2 * lax.axis_size("seq")
    dq_ref, keep_ref, give_ref, kv_ref, stage, qs, qa, ds_, da, dq = refs[-10:]
    b = pl.program_id(0) + first
    own = q_ref.shape[2]
    ndoc = docs_ref.shape[1]
    starts = [docs_ref[b, k] for k in range(ndoc)]
    me = my_chunk()
    begin = start_chunk(starts, me * own, own)
    half = own // 2
    begin_second = start_chunk(starts, me * own + half, own)
    place_keys(kv_refs, kv_ref, begin, me)
    wide = heads * own
    tied = groups * HD
    plain = HD - RD
    q_doc = stack_queries(starts, me * own, half, heads)
    q_all, do_all = q_ref[0], do_ref[0]
    pad_q = jnp.zeros((LANE - HD - 32, wide), BF)
    pad_d = jnp.zeros((LANE - HD - 16, wide), BF)
    row_at = lax.broadcasted_iota(jnp.int32, (own, own), 0)
    column_at = lax.broadcasted_iota(jnp.int32, (own, own), 1)
    identity = jnp.where(row_at == column_at, 1.0, 0.0).astype(BF)

    def turn(rows, ref):
        for h in range(0, heads, 2):
            pair = [rows[:, (h + i) * own : (h + i + 1) * own] for i in range(2)]
            turned = mxu(identity, jnp.concatenate(pair, axis=0), NT).astype(BF)
            ref[h * own : (h + 1) * own] = turned[:, :LANE]
            ref[(h + 1) * own : (h + 2) * own] = turned[:, LANE:]

    for g in range(groups):
        q_rows = stack_heads(q_all, g * heads * HD, heads)
        do_rows = stack_heads(do_all, g * heads * HD, heads)
        qs[g] = q_rows
        ds_[g] = do_rows
        lse_rows = three_parts(-lse_ref[0, g : g + 1], wide)
        delta_row = stack_heads(delta_ref[0], g * heads, heads, 1)
        delta_rows = three_parts(-delta_row, wide)
        turn(jnp.concatenate([q_rows, q_doc, lse_rows, pad_q], axis=0), qa.at[g])
        turn(jnp.concatenate([do_rows, delta_rows, pad_d], axis=0), da.at[g])
    ones = first_rows(3, own)
    pad_k = jnp.zeros((LANE - HD - 32, own), BF)
    pad_v = jnp.zeros((LANE - HD - 16, own), BF)

    seq, core = lax.axis_index("seq"), lax.axis_index("mp")
    steps = chunks // 2

    def deliver(j, value):
        k = lax.rem(j // 2 - seq + steps, steps)

        @pl.when(lax.rem(j, 2) == core)
        def _():
            keep_ref[k, 0] = value()

        @pl.when(lax.rem(j, 2) != core)
        def _():
            give_ref[k, 0] = value()

    def clear(j, carry):
        deliver(j, lambda: jnp.zeros(keep_ref.shape[2:], BF))
        return carry

    lax.fori_loop(0, begin, clear, 0)
    lax.fori_loop(me + 1, chunks, clear, 0)

    def block(j, rows, diagonal):
        doc = key_rows(starts, j * own, own)
        rope_rows = kv_ref[j, tied : tied + RD]
        rope_sum = jnp.zeros((RD, own), F32)

        def keys_of(g):
            return jnp.concatenate(
                [kv_ref[j, g * HD : g * HD + plain], rope_rows], axis=0
            )

        def products(g):
            values = kv_ref[j, g * HD : (g + 1) * HD]
            return (
                mxu(qa[g, :rows], jnp.concatenate([keys_of(g), doc, ones, pad_k], axis=0), NN),
                mxu(da[g, :rows], jnp.concatenate([values, ones, pad_v], axis=0), NN),
            )

        following = products(0)
        for g in range(groups):
            logits, slopes = following
            if g + 1 < groups:
                following = products(g + 1)
            keys = keys_of(g)
            weights = jnp.exp(logits)
            if diagonal:
                query_at = lax.broadcasted_iota(jnp.int32, (half, own), 0)
                key_at = lax.broadcasted_iota(jnp.int32, (half, own), 1)
                causal = jnp.concatenate(
                    [key_at <= query_at + s * half for s in range(2) for _ in range(heads)], axis=0
                )
                weights = jnp.where(causal, weights, 0.0)
            grads = (weights * slopes).astype(BF)
            grad_values = mxu(ds_[g, :, :rows], weights.astype(BF), NN)
            grad_keys = mxu(qs[g, :, :rows], grads, NN)
            keys_t = keys.T
            grad_queries = mxu(grads, jnp.concatenate([keys_t, keys_t], axis=1), NN)
            if diagonal:
                dq[g] = grad_queries
            else:
                dq[g, :rows] += grad_queries
            stage[g * HD : g * HD + plain] = (
                grad_values[:plain] + grad_keys[:plain]
            ).astype(BF)
            stage[g * HD + plain : (g + 1) * HD] = grad_values[plain:].astype(BF)
            rope_sum = rope_sum + grad_keys[plain:]
        stage[tied : tied + RD] = rope_sum.astype(BF)
        deliver(j, lambda: stage[...])

    block(me, wide, True)

    def both(j, carry):
        block(j, wide, False)
        return carry

    def first_only(j, carry):
        block(j, wide // 2, False)
        return carry

    lax.fori_loop(begin_second, me, both, 0)
    lax.fori_loop(begin, begin_second, first_only, 0)
    straight, ahead, behind = rot_ref[0], rot_ref[1], rot_ref[2]
    lane = lax.broadcasted_iota(jnp.int32, (half, LANE), 1)
    quarter = RD // 2
    for g in range(groups):
        for s in range(2):
            positions = slice(s * half, (s + 1) * half)
            for pair in range(heads // 2):
                at = (s * heads + 2 * pair) * half
                two = jnp.where(lane < HD, dq[g, at : at + half], dq[g, at + half : at + 2 * half])
                turned = (
                    two * straight[positions]
                    + pltpu.roll(two, LANE - quarter, 1) * ahead[positions]
                    + pltpu.roll(two, quarter, 1) * behind[positions]
                )
                to = (g * heads + 2 * pair) * HD
                dq_ref[positions, to : to + 2 * HD] = turned.astype(BF)


def attend_backward(docs, q, do, lse, delta, turns, kv, groups, heads, first, size, kv_at, into):
    kv_rows, own = kv[0].shape[2:]
    count, chunks, inputs = docs.shape[0], 2 * lax.axis_size("seq"), len(kv)
    wide = heads * own
    width = q.shape[1]
    column = pl.BlockSpec((1, width, own), lambda b: (b + first, 0, 0))
    hbm = pl.BlockSpec(memory_space=pl.ANY)
    return pl.pallas_call(
        functools.partial(attend_back_kernel, groups, heads, first, inputs),
        grid=(size,),
        in_specs=[
            pl.BlockSpec(memory_space=pltpu.SMEM),
            column,
            column,
            pl.BlockSpec((1, groups, wide), lambda b: (b + first, 0, 0)),
            pl.BlockSpec((1, groups * heads, own), lambda b: (b + first, 0, 0)),
            pl.BlockSpec(turns.shape, lambda b: (0, 0, 0)),
        ]
        + kv_specs(kv, kv_at)
        + [hbm] * len(into),
        out_specs=[
            pl.BlockSpec((own, width), lambda b: (b + first, 0)),
            pl.BlockSpec((chunks // 2, 1, kv_rows, own), lambda b: (0, b, 0, 0)),
            pl.BlockSpec((chunks // 2, 1, kv_rows, own), lambda b: (0, b, 0, 0)),
        ],
        out_shape=[
            jax.ShapeDtypeStruct((count * own, width), BF),
            jax.ShapeDtypeStruct((chunks // 2, size, kv_rows, own), BF),
            jax.ShapeDtypeStruct((chunks // 2, size, kv_rows, own), BF),
        ],
        scratch_shapes=[
            pltpu.VMEM((chunks, kv_rows, own), BF),
            pltpu.VMEM((kv_rows, own), BF),
            pltpu.VMEM((groups, HD, wide), BF),
            pltpu.VMEM((groups, wide, LANE), BF),
            pltpu.VMEM((groups, HD, wide), BF),
            pltpu.VMEM((groups, wide, LANE), BF),
            pltpu.VMEM((groups, wide, LANE), F32),
        ],
        input_output_aliases={6 + inputs + i: i for i in range(len(into))},
        compiler_params=params(),
        cost_estimate=cost(10**9 * size),
        name="attend_back",
    )(docs, q, do, lse, delta, turns, *kv, *into)


def join_cores(keep, received):
    return [
        (keep[k].astype(F32) + received[k].astype(F32)).astype(BF) for k in range(keep.shape[0])
    ]


def send_keys(summed):
    return [summed[0]] + [shift(summed[k], "seq", k) for k in range(1, len(summed))]


def load_weights(refs, targets, sems):
    copies = []
    slot = 0
    for (source, side, axis), target in zip(refs, targets, strict=True):
        blocks = source.shape[axis] // LANE
        for t in range(blocks):
            to = pl.ds((2 * t + side) * LANE, LANE)
            of = pl.ds(t * LANE, LANE)
            src = source.at[:, of] if axis == 1 else source.at[of]
            dst = target.at[:, to] if axis == 1 else target.at[to]
            copies.append(pltpu.make_async_copy(src, dst, sems.at[slot]))
            slot += 1
    return copies


def put(ref, t, value):
    value = value.astype(BF)
    ref[2 * t], ref[2 * t + 1] = value[:, :LANE], value[:, LANE:]


def wide(ref):
    return jnp.concatenate([ref[i] for i in range(ref.shape[0])], axis=1)


def feed_kernel(
    x_ref, og_ref, ga_ref, o_ref, gain_ref, wo_ref, wgo_ref, wgp_ref, wuo_ref, wup_ref, wdo_ref, wdp_ref,
    out_ref, nt_ref, ogt_ref, act_ref, gg_ref, gu_ref, gh_ref, gat_ref, do_ref, delta_ref, gg2_ref,
    wo, wg, wu, wd, sems,
):
    b = pl.program_id(0)

    @pl.when(b == 0)
    def _():
        copies = [pltpu.make_async_copy(wo_ref, wo, sems.at[sems.shape[0] - 1])]
        copies += load_weights(
            [
                (wgo_ref, 0, 1), (wgp_ref, 1, 1), (wuo_ref, 0, 1), (wup_ref, 1, 1),
                (wdo_ref, 0, 0), (wdp_ref, 1, 0),
            ],
            [wg, wg, wu, wu, wd, wd],
            sems,
        )
        for copy in copies:
            copy.start()
        for copy in copies:
            copy.wait()
        gg2_ref[...] = jnp.zeros(gg2_ref.shape, F32)

    og = og_ref[0]
    heads_out = o_ref[0]
    gain = gain_ref[...]
    hidden = x_ref[0].astype(F32) + mxu(heads_out, wo[...], TN)
    inverse = lax.rsqrt(jnp.mean(hidden * hidden, axis=-1, keepdims=True) + epsilon)
    normed = (hidden * inverse * gain).astype(BF)
    nt_ref[0] = normed.T
    ogt_ref[0] = og.T
    units = wg.shape[1]
    tile = 2 * LANE
    for t in range(units // tile):
        at = slice(t * tile, (t + 1) * tile)
        gate = mxu(normed, wg[:, at], NN)
        up = mxu(normed, wu[:, at], NN)
        grad = ga_ref[:, at].astype(F32)
        sigmoid = 1.0 / (1.0 + jnp.exp(-gate))
        silu = gate * sigmoid
        put(act_ref, t, silu * up)
        put(gu_ref, t, grad * silu)
        put(gg_ref, t, grad * up * (sigmoid + silu * (1.0 - sigmoid)))
    result = mxu(wide(act_ref), wd[...], NN)
    out_ref[0] = (hidden + result).astype(BF)
    grad_normed = mxu(wide(gg_ref), wg[...], NT) + mxu(wide(gu_ref), wu[...], NT)
    scaled = grad_normed * gain
    gg2_ref[...] += jnp.sum(grad_normed * (hidden * inverse), axis=0, keepdims=True)
    mean = jnp.mean(scaled * hidden, axis=-1, keepdims=True)
    grad_hidden = og.astype(F32) + inverse * scaled - hidden * (inverse * inverse * inverse * mean)
    grad_attended = grad_hidden.astype(BF)
    gh_ref[0] = grad_attended
    gat_ref[0] = grad_attended.T
    grad_heads = mxu(wo[...], grad_attended, NT).astype(BF)
    do_ref[0] = grad_heads
    product = grad_heads.astype(F32) * heads_out.astype(F32)
    for h in range(product.shape[0] // HD):
        delta_ref[0, h : h + 1] = jnp.sum(product[h * HD : (h + 1) * HD], axis=0, keepdims=True)


def feed(x, og, slopes, heads_out, gain, wo, wg, wu, wd):
    count, own, width = x.shape
    hd = heads_out.shape[1]
    half = wg[0].shape[1]
    units = 2 * half
    tokens = count * own
    seq = pl.BlockSpec((1, own, width), lambda b: (b, 0, 0))
    column = lambda rows: pl.BlockSpec((1, rows, own), lambda b: (b, 0, 0))
    row = pl.BlockSpec((own, units), lambda b: (b, 0))
    blocks = pl.BlockSpec((units // LANE, own, LANE), lambda b: (0, b, 0))
    hbm = pl.BlockSpec(memory_space=pl.ANY)
    return pl.pallas_call(
        feed_kernel,
        grid=(count,),
        in_specs=[seq, seq, row, column(hd), pl.BlockSpec((1, width), lambda b: (0, 0))] + [hbm] * 7,
        out_specs=[
            seq, column(width), column(width), blocks, blocks, blocks, seq, column(width), column(hd),
            pl.BlockSpec((1, hd // HD, own), lambda b: (b, 0, 0)),
            pl.BlockSpec((1, width), lambda b: (0, 0)),
        ],
        out_shape=[
            jax.ShapeDtypeStruct(x.shape, BF),
            jax.ShapeDtypeStruct((count, width, own), BF),
            jax.ShapeDtypeStruct((count, width, own), BF),
            jax.ShapeDtypeStruct((units // LANE, tokens, LANE), BF),
            jax.ShapeDtypeStruct((units // LANE, tokens, LANE), BF),
            jax.ShapeDtypeStruct((units // LANE, tokens, LANE), BF),
            jax.ShapeDtypeStruct(x.shape, BF),
            jax.ShapeDtypeStruct((count, width, own), BF),
            jax.ShapeDtypeStruct((count, hd, own), BF),
            jax.ShapeDtypeStruct((count, hd // HD, own), F32),
            jax.ShapeDtypeStruct((1, width), F32),
        ],
        scratch_shapes=[
            pltpu.VMEM((hd, width), BF),
            pltpu.VMEM((width, units), BF),
            pltpu.VMEM((width, units), BF),
            pltpu.VMEM((units, width), BF),
            pltpu.SemaphoreType.DMA((6 * (half // LANE) + 1,)),
        ],
        compiler_params=params(),
        cost_estimate=cost(2 * tokens * width * (5 * units + 2 * hd)),
        name="feed",
    )(x, og, slopes, heads_out, gain, wo, *wg, *wu, *wd)


def regroup_rows(value, split):
    if split is None:
        return value
    count_d, count_s = split
    own = value.shape[0] // (count_d * count_s)
    return jnp.concatenate(
        [
            value[(d * count_s + s) * own : (d * count_s + s + 1) * own]
            for s in range(count_s)
            for d in range(count_d)
        ],
        axis=0,
    )


def side_by_side(source, target, sems, slot):
    count, _, own = source.shape
    return [
        pltpu.make_async_copy(
            source.at[i], target.at[:, pl.ds(i * own, own)], sems.at[slot + i]
        )
        for i in range(count)
    ]


def early_kernel(
    split, cut, nt_ref, gg_ref, gu_ref, act_ref, act_next_ref, ogt_ref, gat_ref, o_ref, out_ref,
    rest_ref, nt, ogt, gat, heads_out, stage, landed, load_sems, sends, receives,
):
    t = pl.program_id(0)
    core = lax.axis_index("mp")
    tiles = landed.shape[0]
    tile = 2 * LANE
    pairs, head_tiles = gg_tiles(gg_ref, tiles, heads_out)
    other_core = {"mp": 1 - core}
    loads = []
    for source, target in ((nt_ref, nt), (gat_ref, gat), (o_ref, heads_out), (ogt_ref, ogt)):
        loads.append(side_by_side(source, target, load_sems, len(loads) * nt_ref.shape[0]))

    @pl.when(t == 0)
    def _():
        for copies in loads:
            for copy in copies:
                copy.start()
        barrier = pltpu.get_barrier_semaphore()
        pl.semaphore_signal(barrier, inc=1, device_id=other_core, device_id_type=pl.DeviceIdType.MESH)
        pl.semaphore_wait(barrier, 1)
        for copy in loads[0]:
            copy.wait()

    @pl.when(t == pairs)
    def _():
        for copy in loads[1] + loads[2]:
            copy.wait()

    @pl.when(t == pairs + head_tiles)
    def _():
        for copy in loads[3]:
            copy.wait()

    def send(i):
        return pltpu.make_async_remote_copy(
            src_ref=stage.at[lax.rem(i, 2)],
            dst_ref=landed.at[i],
            send_sem=sends.at[i],
            recv_sem=receives.at[i],
            device_id=other_core,
            device_id_type=pl.DeviceIdType.MESH,
        )

    def deliver(product):
        product = regroup_rows(product, split)

        @pl.when(t < tiles)
        def _():
            @pl.when(t >= 2)
            def _():
                send(t - 2).wait_send()

            stage[lax.rem(t, 2)] = product.astype(BF)
            send(t).start()

        @pl.when(t >= tiles)
        def _():
            @pl.when(t < tiles + 2)
            def _():
                send(t - 2).wait_send()

            send(t - tiles).wait_recv()
            total = (product + landed[t - tiles].astype(F32)).astype(BF)

            out_ref[...] = jnp.where(t < tiles + cut, total, out_ref[...])
            rest_ref[...] = total

    at = lax.rem(t, tiles)

    @pl.when(at < pairs)
    def _():
        deliver(mxu(nt[...], jnp.concatenate([gg_ref[0], gu_ref[0]], axis=1), NN))

    @pl.when((at >= pairs) & (at < pairs + head_tiles))
    def _():
        side = jnp.where(t < tiles, 1 - core, core)
        row = pl.multiple_of((side * head_tiles + at - pairs) * tile, tile)
        deliver(mxu(gat[...], heads_out[pl.ds(row, tile)], NT))

    @pl.when(at >= pairs + head_tiles)
    def _():
        deliver(mxu(ogt[...], jnp.concatenate([act_ref[0], act_next_ref[0]], axis=1), NN))


def gg_tiles(gg_ref, tiles, heads_out):
    head_tiles = heads_out.shape[0] // (4 * LANE)
    return (2 * (tiles - head_tiles)) // 3, head_tiles


def early_grads(nt, gg, gu, act, ogt, gat, heads_out, split):
    count, width, own = nt.shape
    tokens = count * own
    units = gg.shape[0] * LANE
    blocks = units // (2 * LANE)
    tile = 2 * LANE
    hd = heads_out.shape[1]
    head_tiles = hd // (2 * tile)
    down_tiles = (blocks + 1) // 2
    tiles = blocks + head_tiles + down_tiles
    cut = tiles - 4
    rest = units + units // 2 + hd // 2 - cut * tile
    hbm = pl.BlockSpec(memory_space=pl.ANY)
    side = lambda t: jnp.where(t < tiles, 1, 0)

    def pair(t):
        return (2 * jnp.minimum(lax.rem(t, tiles), blocks - 1) + side(t), 0, 0)

    def down(t, shift_by):
        at = jnp.clip(lax.rem(t, tiles) - blocks - head_tiles, 0, down_tiles - 1)
        return (2 * jnp.minimum(2 * at + shift_by, blocks - 1) + side(t), 0, 0)

    block = lambda index: pl.BlockSpec((1, tokens, LANE), index)
    return pl.pallas_call(
        functools.partial(early_kernel, split, cut),
        grid=(2 * tiles,),
        in_specs=[
            hbm,
            block(pair),
            block(pair),
            block(lambda t: down(t, 0)),
            block(lambda t: down(t, 1)),
            hbm,
            hbm,
            hbm,
        ],
        out_specs=[
            pl.BlockSpec((width, tile), lambda t: (0, jnp.clip(t - tiles, 0, cut - 1))),
            pl.BlockSpec((width, tile), lambda t: (0, jnp.maximum(t - tiles - cut, 0))),
        ],
        out_shape=[
            jax.ShapeDtypeStruct((width, cut * tile), BF),
            jax.ShapeDtypeStruct((width, rest), BF),
        ],
        scratch_shapes=[
            pltpu.VMEM((width, tokens), BF),
            pltpu.VMEM((width, tokens), BF),
            pltpu.VMEM((width, tokens), BF),
            pltpu.VMEM((hd, tokens), BF),
            pltpu.VMEM((2, width, tile), BF),
            pltpu.VMEM((tiles, width, tile), BF),
            pltpu.SemaphoreType.DMA((4 * count,)),
            pltpu.SemaphoreType.DMA((tiles,)),
            pltpu.SemaphoreType.DMA((tiles,)),
        ],
        compiler_params=pltpu.CompilerParams(
            vmem_limit_bytes=56 * MIB, collective_id=3, has_side_effects=True
        ),
        cost_estimate=cost(6 * 10**10),
        name="early_grads",
    )(nt, gg, gu, act, act, ogt, gat, heads_out)


def tail_kernel(
    order, x_ref, dq_ref, nt_ref, gain_ref, wq_ref, wkv_ref, cos_ref, sin_ref, gg2_ref,
    nt_all_ref, dq_all_ref, early_ref, near_refs, *refs,
):
    count_d, count_s = lax.axis_size("dp"), lax.axis_size("seq")
    me_d, me_s, core = lax.axis_index("dp"), lax.axis_index("seq"), lax.axis_index("mp")
    (keep_mid, got_mid, keep_end, give_end, update_ref, query_out, small_out, early_out) = refs[:8]
    (
        key_in, sum_mid, sum_end, got_end, query_stage, query_in, query_sum, query_seq, query_part,
        query_dp, early_in, early_own, nt_all, dq_all, load_sems, dw, gg1, small_other, small_in, small_sum, small_seq, small_part,
        small_dp, sends, receives,
    ) = refs[8:]
    rows = query_out.shape[0]
    step = pl.program_id(0)
    other_core = {"mp": 1 - core}
    seq_peers = [{"seq": lax.rem(me_s + k, count_s)} for k in range(1, count_s)]
    dp_peers = [{"dp": lax.rem(me_d + k, count_d)} for k in range(1, count_d)]
    peers = [other_core] + seq_peers + dp_peers
    slots = iter(range(sends.shape[0]))

    def link(source, target, peer):
        slot = next(slots)
        return pltpu.make_async_remote_copy(
            src_ref=source,
            dst_ref=target,
            send_sem=sends.at[slot],
            recv_sem=receives.at[slot],
            device_id=peer,
            device_id_type=pl.DeviceIdType.MESH,
        )

    to_seq = [lax.rem(me_s + k, count_s) for k in range(1, count_s)]
    to_dp = [lax.rem(me_d + k, count_d) for k in range(1, count_d)]
    early_copies = [
        link(early_ref.at[to_dp[k]], early_in.at[k], dp_peers[k]) for k in range(count_d - 1)
    ]
    end_core = link(give_end, got_end, other_core)
    key_copies, at = [], 0
    for part in (sum_mid, sum_end):
        size = part.shape[1]
        key_copies.append(
            [
                link(part.at[k + 1], key_in.at[k, pl.ds(at, size)], seq_peers[k])
                for k in range(count_s - 1)
            ]
        )
        at += size
    query_core = link(query_stage, query_in, other_core)
    query_seqs = [
        link(query_sum.at[to_seq[k]], query_seq.at[k], seq_peers[k]) for k in range(count_s - 1)
    ]
    query_dps = [
        link(query_part.at[to_dp[k]], query_dp.at[k], dp_peers[k]) for k in range(count_d - 1)
    ]
    small_core = link(small_other, small_in, other_core)
    small_seqs = [
        link(small_sum.at[to_seq[k]], small_seq.at[k], seq_peers[k]) for k in range(count_s - 1)
    ]
    small_dps = [
        link(small_part.at[to_dp[k]], small_dp.at[k], dp_peers[k]) for k in range(count_d - 1)
    ]

    def start(copies):
        for copy in copies:
            copy.start()

    def by_seq(total, target):
        for s in range(count_s):
            for d in range(count_d):
                of = (d * count_s + s) * rows
                target[s, d * rows : (d + 1) * rows] = total[of : of + rows].astype(BF)

    def gather(own, copies, arrived):
        total = own.astype(F32)
        for k, copy in enumerate(copies):
            copy.wait()
            total = total + arrived[k].astype(F32)
        return total

    def by_dp(total, target):
        for d in range(count_d):
            target[d] = total[d * rows : (d + 1) * rows].astype(BF)

    loads = side_by_side(nt_all_ref, nt_all, load_sems, 2) + [
        pltpu.make_async_copy(dq_all_ref, dq_all, load_sems.at[0]),
        pltpu.make_async_copy(early_ref.at[me_d], early_own, load_sems.at[1]),
    ]

    def join(mine, got, total):
        for k in range(count_s):
            total[k] = (mine[k].astype(F32) + got[k].astype(F32)).astype(BF)

    def query_product(half):
        size = query_stage.shape[1]
        columns = pl.ds(pl.multiple_of(half * size, size), size)
        return mxu(nt_all[...], dq_all[:, columns], NN)

    @pl.when(step == 0)
    def _():
        barrier = pltpu.get_barrier_semaphore()
        for peer in peers:
            pl.semaphore_signal(barrier, inc=1, device_id=peer, device_id_type=pl.DeviceIdType.MESH)
        pl.semaphore_wait(barrier, len(peers))
        start([end_core])
        join(keep_mid, got_mid, sum_mid)
        start(key_copies[0])
        start(early_copies)
        start(loads)
        end_core.wait()
        join(keep_end, got_end, sum_end)
        start(key_copies[1])
        for load in loads:
            load.wait()
        query_stage[...] = query_product(1 - core).astype(BF)
        start([query_core])
        dw[...] = jnp.zeros(dw.shape, F32)
        gg1[...] = jnp.zeros(gg1.shape, F32)

    @pl.when(step == 1)
    def _():
        product = query_product(core)
        query_core.wait()
        by_seq(product + query_in[...].astype(F32), query_sum)
        start(query_seqs)

    tied = wkv_ref.shape[0] - RD

    def finish(summed):
        turned = rotate_rows(summed[tied:], cos_ref[...], -sin_ref[...])
        dkv = jnp.concatenate([summed[:tied], turned], axis=0).astype(BF)
        grad_normed = mxu(dq_ref[...], wq_ref[...], NN) + mxu(dkv, wkv_ref[...], TN)
        dw[...] += mxu(nt_ref[0], dkv, NT)
        x = x_ref[0].astype(F32)
        inverse = lax.rsqrt(jnp.mean(x * x, axis=-1, keepdims=True) + epsilon)
        scaled = grad_normed * gain_ref[...]
        gg1[...] += jnp.sum(grad_normed * (x * inverse), axis=0, keepdims=True)
        mean = jnp.mean(scaled * x, axis=-1, keepdims=True)
        update = inverse * scaled - x * (inverse * inverse * inverse * mean)
        update_ref[0] = update.astype(BF)

    begin = 0
    for (_, size), terms in zip(order, near_refs):

        @pl.when((step >= begin) & (step < begin + size))
        def _():
            summed = terms[0][0].astype(F32)
            for ref in terms[1:]:
                summed = summed + ref[0].astype(F32)
            finish(summed)

        begin += size

    base = begin
    for part, far in enumerate((sum_mid, sum_end)):
        size = far.shape[1]

        @pl.when(step == begin)
        def _():
            for copy in key_copies[part]:
                copy.wait()

        @pl.when((step >= begin) & (step < begin + size))
        def _():
            at = step - base
            summed = far[0, step - begin].astype(F32)
            for k in range(count_s - 1):
                summed = summed + key_in[k, at].astype(F32)
            finish(summed)

        begin += size

    @pl.when(step == begin - 2)
    def _():
        total = gather(query_sum[me_s], query_seqs, query_seq)
        by_dp(total, query_part)
        start(query_dps)

    @pl.when(step == begin - 1)
    def _():
        width = dw.shape[0]
        pad = jnp.zeros((LANE - RD, width), F32)
        row = lax.broadcasted_iota(jnp.int32, (LANE, width), 0)
        gains = jnp.where(row == RD, gg1[...], 0.0)
        gains = jnp.where(row == RD + 1, gg2_ref[...], gains)
        weights = dw[...]
        rope = jnp.concatenate([weights[:, tied:], jnp.zeros((width, LANE - RD), F32)], axis=1)
        small = rope + gains.T
        half = tied // 2
        first, second = weights[:, :half], weights[:, half:tied]
        mine = jnp.concatenate([jnp.where(core == 0, first, second), small], axis=1)
        other = jnp.concatenate([jnp.where(core == 0, second, first), small], axis=1)
        small_other[...] = other.astype(BF)
        start([small_core])
        small_core.wait()
        by_seq(mine + small_in[...].astype(F32), small_sum)
        start(small_seqs)
        by_dp(gather(small_sum[me_s], small_seqs, small_seq), small_part)
        start(small_dps)
        query_out[...] = gather(query_part[me_d], query_dps, query_dp)
        early_out[...] = gather(early_own[...], early_copies, early_in)
        small_out[...] = gather(small_part[me_d], small_dps, small_dp)


def tail(
    order, x, dq, nt, gain, wq, wkv, cosine, sine_table, grad_gain_two, early, near,
    shares,
):
    count, own, width = x.shape
    count_d, count_s = lax.axis_size("dp"), lax.axis_size("seq")
    rows = width // (count_d * count_s)
    kv_rows = wkv.shape[0]
    tied = kv_rows - RD
    wide = dq.shape[1] // 2
    narrow = tied // 2 + LANE
    middle, end = shares[0].shape, shares[2].shape
    sent = middle[1] + end[1]

    def place(i):
        done, at = 0, i
        for first, size in order:
            at = jnp.where((i >= done) & (i < done + size), first + i - done, at)
            done += size
        return at

    seq = pl.BlockSpec((1, own, width), lambda i: (place(i), 0, 0))
    whole = lambda array: pl.BlockSpec(array.shape, lambda i: (0,) * array.ndim)
    near_specs, done = [], 0
    for (_, size), terms in zip(order, near):
        index = lambda i, done=done, size=size: (jnp.clip(i - done, 0, size - 1), 0, 0)
        near_specs += [pl.BlockSpec((1, kv_rows, own), index)] * len(terms)
        done += size
    fixed = [gain, wq, wkv, cosine, sine_table, grad_gain_two]
    hbm = pl.BlockSpec(memory_space=pl.ANY)
    outs = [
        jax.ShapeDtypeStruct(x.shape, BF),
        jax.ShapeDtypeStruct((rows, wide), F32),
        jax.ShapeDtypeStruct((rows, narrow), F32),
        jax.ShapeDtypeStruct((rows, early.shape[2]), F32),
    ]
    near_all = [term for terms in near for term in terms]

    def kernel(*refs):
        head, rest = refs[:12], refs[12 + len(near_all) :]
        nears = [refs[12 + i * count_s : 12 + (i + 1) * count_s] for i in range(len(near))]
        tail_kernel(order, *head, nears, *rest)

    slots = 3 * (count_d - 1) + 4 * (count_s - 1) + 3
    return pl.pallas_call(
        kernel,
        grid=(count,),
        in_specs=[
            seq,
            pl.BlockSpec((own, dq.shape[1]), lambda i: (place(i), 0)),
            pl.BlockSpec((1, width, own), lambda i: (place(i), 0, 0)),
        ]
        + [whole(array) for array in fixed]
        + [hbm, hbm, hbm]
        + near_specs
        + [whole(array) for array in shares],
        out_specs=[seq] + [whole(out) for out in outs[1:]],
        out_shape=outs,
        scratch_shapes=[
            pltpu.VMEM((count_s - 1, sent, kv_rows, own), BF),
            pltpu.VMEM(middle, BF),
            pltpu.VMEM(end, BF),
            pltpu.VMEM(end, BF),
            pltpu.VMEM((width, wide), BF),
            pltpu.VMEM((width, wide), BF),
            pltpu.VMEM((count_s, count_d * rows, wide), BF),
            pltpu.VMEM((count_s - 1, count_d * rows, wide), BF),
            pltpu.VMEM((count_d, rows, wide), BF),
            pltpu.VMEM((count_d - 1, rows, wide), BF),
            pltpu.VMEM((count_d - 1, rows, early.shape[2]), BF),
            pltpu.VMEM((rows, early.shape[2]), BF),
            pltpu.VMEM((width, count * own), BF),
            pltpu.VMEM(dq.shape, BF),
            pltpu.SemaphoreType.DMA((2 + count,)),
            pltpu.VMEM((width, kv_rows), F32),
            pltpu.VMEM((1, width), F32),
            pltpu.VMEM((width, narrow), BF),
            pltpu.VMEM((width, narrow), BF),
            pltpu.VMEM((count_s, count_d * rows, narrow), BF),
            pltpu.VMEM((count_s - 1, count_d * rows, narrow), BF),
            pltpu.VMEM((count_d, rows, narrow), BF),
            pltpu.VMEM((count_d - 1, rows, narrow), BF),
            pltpu.SemaphoreType.DMA((slots,)),
            pltpu.SemaphoreType.DMA((slots,)),
        ],
        compiler_params=pltpu.CompilerParams(
            vmem_limit_bytes=56 * MIB, collective_id=1, has_side_effects=True
        ),
        cost_estimate=cost(10**8),
        name="tail",
    )(x, dq, nt, *fixed, nt, dq, early, *near_all, *shares)


def turn_tables(cosine, sine_table):
    plain = HD - RD
    one = jnp.ones((cosine.shape[0], plain), F32)
    none = jnp.zeros_like(one)
    quiet = jnp.zeros_like(sine_table)
    straight = jnp.concatenate([one, cosine, cosine], axis=1)
    ahead = jnp.concatenate([none, sine_table, quiet], axis=1)
    behind = jnp.concatenate([none, quiet, -sine_table], axis=1)
    tables = jnp.stack([jnp.concatenate([t, t], axis=1) for t in (straight, ahead, behind)])
    return tables * HD ** (-0.5)


def after(value, *others):
    return lax.optimization_barrier((value, *others))[0]


def on_device_fast(
    inputs, gain_one, w_query, w_tied, w_rope, w_out, gain_two, w_gate, w_up, w_down,
    doc_starts, out_grad,
):
    count, own, width = inputs.shape
    cores = lax.axis_size("mp")
    groups = cores * w_tied.shape[1] // HD
    all_heads = cores * w_query.shape[1] // HD
    heads = all_heads // groups
    mp_index = lax.axis_index("mp")
    split = (lax.axis_size("dp"), lax.axis_size("seq"))
    tied_other, query_other = swap_cores(w_tied), swap_cores(w_query)
    down_other = swap_cores(w_down)
    gain_one_float = gain_one.astype(F32)[None]
    gain_two_float = gain_two.astype(F32)[None]
    cosine, sine_table = rope_tables(my_chunk() * own, own, RD)
    cosine_t, sine_t = cosine.T, sine_table.T
    half = count // 2
    kv, normed_t, q, slopes, queries_weights, keys_weights, kv_near, kv_far = project(
        inputs, out_grad, gain_one_float, (w_query, query_other), (w_tied, tied_other), w_rope,
        (w_down, down_other), cosine_t, sine_t, half,
    )
    kv_late = send_near(kv)
    out_other = swap_cores(w_out)
    gate_other, up_other = swap_cores(w_gate), swap_cores(w_up)
    span = half - half // 4
    made = attend_forward(doc_starts, q, [kv_near, kv_far], groups, heads, 0, span, 0, ())
    kv_late = send_far([after(part, *made) for part in kv_late])
    made = attend_forward(
        doc_starts, q, [kv_near, kv_far], groups, heads, span, half - span, span, made
    )
    heads_out, lse = attend_forward(doc_starts, q, kv_late, groups, heads, half, half, 0, made)
    out_both = by_core(w_out, after(out_other, lse), 0)
    (
        outputs, normed_two_t, out_grad_t, active, grad_gate, grad_up, grad_hidden, grad_attended_t,
        grad_heads, delta, grad_gain_two,
    ) = feed(
        inputs, out_grad, slopes, heads_out, gain_two_float, out_both, (w_gate, gate_other),
        (w_up, up_other), (w_down, down_other),
    )
    units, head_half = w_gate.shape[1], w_out.shape[0]
    first_sum, rest_sum = early_grads(
        normed_two_t, grad_gate, grad_up, active, out_grad_t, grad_attended_t, heads_out, split
    )
    first_sum, rest_sum, grad_heads = lax.optimization_barrier((first_sum, rest_sum, grad_heads))
    first_sum = lax.psum_scatter(first_sum, "seq", scatter_dimension=0, tiled=True)

    turns = turn_tables(cosine, sine_table)
    quarter = half // 2
    backward = [
        (half, half, kv_late, 0),
        (quarter, half - quarter, [kv_near, kv_far], quarter),
        (0, quarter, [kv_near, kv_far], 0),
    ]
    rest_sum = rest_sum.reshape(split[1], split[0], -1, rest_sum.shape[1])
    rest_sum = add_up(send_steps(rest_sum, "dp", 1)).astype(BF)
    rest_terms = send_steps(rest_sum, "seq", 0)
    dq, near, shares = (), [], []
    for part, (at, size, kv_part, kv_at) in enumerate(backward):
        need = near[0][:1] if part == 2 else []
        made_dq, keep, give = attend_backward(
            doc_starts, after(q, *need), grad_heads, lse, delta, turns, kv_part, groups, heads, at,
            size, kv_at, dq,
        )
        dq = (made_dq,)
        if part == 0:
            first_shares = (keep, swap_cores(after(give, rest_sum)))
        if part == 1:
            give = after(give, *rest_terms)
            near.append(send_keys(join_cores(*first_shares)))
            shares = [keep, swap_cores(give)]
        if part == 2:
            shares += [keep, give]
    early = first_sum.reshape(split[0], -1, first_sum.shape[1])
    order = [span[:2] for span in backward]
    update, query_sum, small_sum, first_sum = tail(
        order, inputs, dq[0], normed_t, gain_one_float, queries_weights, keys_weights,
        cosine_t, sine_t, grad_gain_two, early, near,
        shares,
    )
    grad_inputs = grad_hidden.astype(F32) + update.astype(F32)
    half_tied = groups * HD // cores
    late_sum, small_sum = small_sum[:, :half_tied], small_sum[:, half_tied:]
    rows = small_sum.shape[0] // cores
    small_sum = lax.dynamic_slice_in_dim(small_sum, mp_index * rows, rows, 0)
    pairs = first_sum[:, : 2 * units].reshape(first_sum.shape[0], units // LANE, 2, LANE)
    gate_sum = pairs[:, :, 0].reshape(-1, units)
    up_sum = pairs[:, :, 1].reshape(-1, units)
    out_sum = first_sum[:, 2 * units : 2 * units + head_half]
    down_sum = jnp.concatenate([first_sum[:, 2 * units + head_half :], add_up(rest_terms)], axis=1)
    return (
        outputs,
        grad_inputs,
        small_sum[:, RD],
        query_sum,
        late_sum,
        small_sum[:, :RD],
        out_sum.T,
        small_sum[:, RD + 1],
        gate_sum,
        up_sum,
        down_sum.T,
    )


def solution(mesh):
    in_specs = (
        P("dp", ("seq", "mp"), None),
        P(),
        P(None, "mp"),
        P(None, "mp"),
        P(),
        P("mp", None),
        P(),
        P(None, "mp"),
        P(None, "mp"),
        P("mp", None),
        P("dp", None),
        P("dp", ("seq", "mp"), None),
    )
    out_specs = (
        P("dp", ("seq", "mp"), None),
        P("dp", ("seq", "mp"), None),
        P(("dp", "seq", "mp")),
        P(("dp", "seq"), "mp"),
        P(("dp", "seq"), "mp"),
        P(("dp", "seq", "mp"), None),
        P("mp", ("dp", "seq")),
        P(("dp", "seq", "mp")),
        P(("dp", "seq"), "mp"),
        P(("dp", "seq"), "mp"),
        P("mp", ("dp", "seq")),
    )

    def local(inputs, *rest):
        step = on_device_fast if inputs.shape[1] % (2 * LANE) == 0 else on_device
        return step(inputs, *rest)

    return jax.shard_map(
        local, mesh=mesh, in_specs=in_specs, out_specs=out_specs, check_vma=False
    )
```

```python
import functools

import jax
import jax.numpy as jnp
from jax import lax
from jax.experimental import pallas as pl
from jax.experimental.pallas import tpu as pltpu
from jax.sharding import PartitionSpec as P

HD = 64
RD = 32


epsilon = 1e-05
rope_base = 10000.0
masked_value = -1e30


def rope_tables(offset, count, rope_width):
    position = (offset + jnp.arange(count, dtype=jnp.int32)).astype(jnp.float32)
    frequency = rope_base ** (-jnp.arange(rope_width // 2, dtype=jnp.float32) * 2.0 / rope_width)
    angles = position[:, None] * frequency[None, :]
    return (jnp.cos(angles), jnp.sin(angles))


def rotate(values, cosine, sine_table):
    half_width = values.shape[-1] // 2
    first_half = values[..., :half_width]
    second_half = values[..., half_width:]
    return jnp.concatenate(
        [
            first_half * cosine - second_half * sine_table,
            second_half * cosine + first_half * sine_table,
        ],
        axis=-1,
    )


def rotate_back(grads, cosine, sine_table):
    half_width = grads.shape[-1] // 2
    first_half = grads[..., :half_width]
    second_half = grads[..., half_width:]
    return jnp.concatenate(
        [
            first_half * cosine + second_half * sine_table,
            second_half * cosine - first_half * sine_table,
        ],
        axis=-1,
    )


def contract_rows(left, right):
    return lax.dot_general(
        left, right, (((0,), (0,)), ((), ())), preferred_element_type=jnp.float32
    )


def times_transposed(left, right):
    return lax.dot_general(
        left, right, (((1,), (1,)), ((), ())), preferred_element_type=jnp.float32
    )


def norm_back(grad_normed, values, inverse, gain):
    scaled = grad_normed * gain
    grad_gain = jnp.sum(grad_normed * values * inverse, axis=(0, 1))
    grad_values = inverse * scaled - values * inverse**3 * jnp.mean(
        scaled * values, axis=-1, keepdims=True
    )
    return (grad_values, grad_gain)


def attend(operands):
    queries, key_full, values, allowed = operands
    scores = jnp.einsum(
        "qghd,kgd->ghqk", queries, key_full, preferred_element_type=jnp.float32
    ) * HD ** (-0.5)
    masked = jnp.where(allowed[None, None], scores, masked_value)
    row_max = jnp.max(masked, axis=-1, keepdims=True)
    weights = jnp.exp(masked - row_max)
    row_total = jnp.sum(weights, axis=-1, keepdims=True)
    attention_probs = (weights / row_total).astype(jnp.bfloat16)
    combined = jnp.einsum(
        "ghqk,kgd->qghd", attention_probs, values, preferred_element_type=jnp.float32
    )
    return (combined.astype(jnp.bfloat16), row_max + jnp.log(row_total))


def attend_back(operands):
    queries, key_full, values, allowed, log_total, grad_heads = operands
    score_scale = HD ** (-0.5)
    plain_width = HD - RD
    scores = (
        jnp.einsum("qghd,kgd->ghqk", queries, key_full, preferred_element_type=jnp.float32)
        * score_scale
    )
    masked = jnp.where(allowed[None, None], scores, masked_value)
    probs_float = jnp.exp(masked - log_total)
    grad_probs = jnp.einsum(
        "qghd,kgd->ghqk", grad_heads, values, preferred_element_type=jnp.float32
    )
    row_delta = jnp.sum(probs_float * grad_probs, axis=-1, keepdims=True)
    grad_scores = (probs_float * (grad_probs - row_delta)).astype(jnp.bfloat16)
    grad_queries = (
        jnp.einsum("ghqk,kgd->qghd", grad_scores, key_full, preferred_element_type=jnp.float32)
        * score_scale
    )
    grad_keys = (
        jnp.einsum("ghqk,qghd->kgd", grad_scores, queries, preferred_element_type=jnp.float32)
        * score_scale
    )
    grad_values = jnp.einsum(
        "ghqk,qghd->kgd",
        probs_float.astype(jnp.bfloat16),
        grad_heads,
        preferred_element_type=jnp.float32,
    )
    grad_tied = grad_values + jnp.concatenate(
        [grad_keys[..., :plain_width], jnp.zeros_like(grad_keys[..., plain_width:])], axis=-1
    )
    grad_rope = jnp.sum(grad_keys[..., plain_width:], axis=1)
    return (grad_queries, grad_tied, grad_rope)


def on_device(
    inputs,
    gain_one,
    w_query,
    w_tied,
    w_rope,
    w_out,
    gain_two,
    w_gate,
    w_up,
    w_down,
    doc_starts,
    out_grad,
):
    seq_count, own_count, model_width = inputs.shape
    plain_width = HD - RD
    group_local = w_tied.shape[1] // HD
    head_local = w_query.shape[1] // HD
    seq_index = lax.axis_index("seq")
    mp_index = lax.axis_index("mp")
    gain_one_float = gain_one.astype(jnp.float32)
    gain_two_float = gain_two.astype(jnp.float32)
    inputs_float = inputs.astype(jnp.float32)
    inverse_one = lax.rsqrt(jnp.mean(inputs_float * inputs_float, axis=-1, keepdims=True) + epsilon)
    normed_one = (inputs_float * inverse_one * gain_one_float).astype(jnp.bfloat16)
    gathered_one = lax.all_gather(normed_one, "mp", axis=1, tiled=True)
    context = gathered_one.shape[1]
    token_count = seq_count * context
    flat_one = gathered_one.reshape(token_count, model_width)
    offset = seq_index * context
    cosine, sine_table = rope_tables(offset, context, RD)
    query_lin = jnp.dot(flat_one, w_query, preferred_element_type=jnp.float32).reshape(
        seq_count, context, head_local, HD
    )
    queries = jnp.concatenate(
        [
            query_lin[..., :plain_width],
            rotate(
                query_lin[..., plain_width:], cosine[None, :, None, :], sine_table[None, :, None, :]
            ),
        ],
        axis=-1,
    ).astype(jnp.bfloat16)
    queries = queries.reshape(seq_count, context, group_local, head_local // group_local, HD)
    tied_state = (
        jnp.dot(flat_one, w_tied, preferred_element_type=jnp.float32)
        .astype(jnp.bfloat16)
        .reshape(seq_count, context, group_local * HD)
    )
    rope_lin = jnp.dot(flat_one, w_rope, preferred_element_type=jnp.float32).reshape(
        seq_count, context, RD
    )
    rope_keys = rotate(rope_lin, cosine[None], sine_table[None]).astype(jnp.bfloat16)
    tied_all, rope_all = (
        lax.all_gather(tied_state, "seq", axis=1, tiled=True),
        lax.all_gather(rope_keys, "seq", axis=1, tiled=True),
    )
    length = tied_all.shape[1]
    values_all = tied_all.reshape(seq_count, length, group_local, HD)
    key_full = jnp.concatenate(
        [
            values_all[..., :plain_width],
            jnp.broadcast_to(rope_all[:, :, None, :], (seq_count, length, group_local, RD)),
        ],
        axis=-1,
    )
    key_position = jnp.arange(length, dtype=jnp.int32)
    key_segment = jnp.sum(
        (doc_starts[:, None, :] <= key_position[None, :, None]).astype(jnp.int32), axis=-1
    )
    query_segment = lax.dynamic_slice_in_dim(key_segment, offset, context, 1)
    query_position = offset + jnp.arange(context, dtype=jnp.int32)
    allowed = (query_segment[:, :, None] == key_segment[:, None, :]) & (
        query_position[:, None] >= key_position[None, :]
    )[None]
    head_outputs, log_total = lax.map(attend, (queries, key_full, values_all, allowed))
    flat_heads = head_outputs.reshape(token_count, head_local * HD)
    attended_part = jnp.dot(flat_heads, w_out, preferred_element_type=jnp.float32).reshape(
        seq_count, context, model_width
    )
    attended = lax.psum_scatter(
        attended_part.astype(jnp.bfloat16), "mp", scatter_dimension=1, tiled=True
    ).astype(jnp.float32)
    hidden = inputs_float + attended
    inverse_two = lax.rsqrt(jnp.mean(hidden * hidden, axis=-1, keepdims=True) + epsilon)
    normed_two = (hidden * inverse_two * gain_two_float).astype(jnp.bfloat16)
    gathered_two = lax.all_gather(normed_two, "mp", axis=1, tiled=True)
    flat_two = gathered_two.reshape(token_count, model_width)
    gate_values = jnp.dot(flat_two, w_gate, preferred_element_type=jnp.float32)
    up_values = jnp.dot(flat_two, w_up, preferred_element_type=jnp.float32)
    sigmoid_gate = jax.nn.sigmoid(gate_values)
    silu_gate = gate_values * sigmoid_gate
    active = (silu_gate * up_values).astype(jnp.bfloat16)
    result_part = jnp.dot(active, w_down, preferred_element_type=jnp.float32).reshape(
        seq_count, context, model_width
    )
    result = lax.psum_scatter(
        result_part.astype(jnp.bfloat16), "mp", scatter_dimension=1, tiled=True
    ).astype(jnp.float32)
    outputs = (hidden + result).astype(jnp.bfloat16)
    grad_out_all = lax.all_gather(out_grad, "mp", axis=1, tiled=True)
    flat_grad = grad_out_all.reshape(token_count, model_width)
    grad_active = times_transposed(flat_grad, w_down)
    grad_w_down = contract_rows(active, flat_grad)
    grad_gate = (
        grad_active * up_values * sigmoid_gate * (1.0 + gate_values * (1.0 - sigmoid_gate))
    ).astype(jnp.bfloat16)
    grad_up = (grad_active * silu_gate).astype(jnp.bfloat16)
    grad_w_gate = contract_rows(flat_two, grad_gate)
    grad_w_up = contract_rows(flat_two, grad_up)
    grad_two_part = (times_transposed(grad_gate, w_gate) + times_transposed(grad_up, w_up)).reshape(
        seq_count, context, model_width
    )
    grad_normed_two = lax.psum_scatter(
        grad_two_part.astype(jnp.bfloat16), "mp", scatter_dimension=1, tiled=True
    ).astype(jnp.float32)
    grad_hidden_norm, grad_gain_two = norm_back(
        grad_normed_two, hidden, inverse_two, gain_two_float
    )
    grad_hidden = out_grad.astype(jnp.float32) + grad_hidden_norm
    grad_attended_all = lax.all_gather(grad_hidden.astype(jnp.bfloat16), "mp", axis=1, tiled=True)
    flat_attended = grad_attended_all.reshape(token_count, model_width)
    grad_w_out = contract_rows(flat_heads, flat_attended)
    grad_heads = times_transposed(flat_attended, w_out).astype(jnp.bfloat16).reshape(queries.shape)
    grad_queries, grad_tied, grad_rope = lax.map(
        attend_back, (queries, key_full, values_all, allowed, log_total, grad_heads)
    )
    grad_queries = grad_queries.reshape(seq_count, context, head_local, HD)
    grad_query_lin = (
        jnp.concatenate(
            [
                grad_queries[..., :plain_width],
                rotate_back(
                    grad_queries[..., plain_width:],
                    cosine[None, :, None, :],
                    sine_table[None, :, None, :],
                ),
            ],
            axis=-1,
        )
        .astype(jnp.bfloat16)
        .reshape(token_count, head_local * HD)
    )
    tied_own, rope_context = (
        lax.psum_scatter(
            grad_tied.reshape(seq_count, length, group_local * HD).astype(jnp.bfloat16),
            "seq",
            scatter_dimension=1,
            tiled=True,
        ).astype(jnp.float32),
        lax.psum_scatter(
            grad_rope.astype(jnp.bfloat16), "seq", scatter_dimension=1, tiled=True
        ).astype(jnp.float32),
    )
    grad_tied_flat = tied_own.astype(jnp.bfloat16).reshape(token_count, group_local * HD)
    grad_one_part = (
        times_transposed(grad_query_lin, w_query) + times_transposed(grad_tied_flat, w_tied)
    ).reshape(seq_count, context, model_width)
    grad_normed_one, rope_own = (
        lax.psum_scatter(
            grad_one_part.astype(jnp.bfloat16), "mp", scatter_dimension=1, tiled=True
        ).astype(jnp.float32),
        lax.psum_scatter(
            rope_context.astype(jnp.bfloat16), "mp", scatter_dimension=1, tiled=True
        ).astype(jnp.float32),
    )
    own_offset = offset + mp_index * own_count
    cosine_own, sine_own = rope_tables(own_offset, own_count, RD)
    grad_rope_flat = (
        rotate_back(rope_own, cosine_own[None], sine_own[None])
        .astype(jnp.bfloat16)
        .reshape(seq_count * own_count, RD)
    )
    grad_normed_one = grad_normed_one + times_transposed(grad_rope_flat, w_rope).reshape(
        seq_count, own_count, model_width
    )
    grad_w_rope = contract_rows(
        normed_one.reshape(seq_count * own_count, model_width), grad_rope_flat
    )
    grad_w_query = contract_rows(flat_one, grad_query_lin)
    grad_w_tied = contract_rows(flat_one, grad_tied_flat)
    grad_inputs_norm, grad_gain_one = norm_back(
        grad_normed_one, inputs_float, inverse_one, gain_one_float
    )
    grad_inputs = grad_hidden + grad_inputs_norm
    small_sums = (
        lax.psum_scatter(grad_gain_one, ("dp", "seq", "mp"), scatter_dimension=0, tiled=True),
        lax.psum_scatter(grad_w_rope, ("dp", "seq", "mp"), scatter_dimension=0, tiled=True),
        lax.psum_scatter(grad_gain_two, ("dp", "seq", "mp"), scatter_dimension=0, tiled=True),
    )
    weight_terms = (grad_w_query, grad_w_tied, grad_w_out, grad_w_gate, grad_w_up, grad_w_down)
    weight_sums = (
        lax.psum_scatter(weight_terms[0], ("dp", "seq"), scatter_dimension=0, tiled=True),
        lax.psum_scatter(weight_terms[1], ("dp", "seq"), scatter_dimension=0, tiled=True),
        lax.psum_scatter(weight_terms[2], ("dp", "seq"), scatter_dimension=1, tiled=True),
        lax.psum_scatter(weight_terms[3], ("dp", "seq"), scatter_dimension=0, tiled=True),
        lax.psum_scatter(weight_terms[4], ("dp", "seq"), scatter_dimension=0, tiled=True),
        lax.psum_scatter(weight_terms[5], ("dp", "seq"), scatter_dimension=1, tiled=True),
    )
    return (
        outputs,
        grad_inputs,
        small_sums[0],
        weight_sums[0],
        weight_sums[1],
        small_sums[1],
        weight_sums[2],
        small_sums[2],
        weight_sums[3],
        weight_sums[4],
        weight_sums[5],
    )


BF = jnp.bfloat16
F32 = jnp.float32
NN = (((1,), (0,)), ((), ()))
NT = (((1,), (1,)), ((), ()))
TN = (((0,), (0,)), ((), ()))
BIG = 2.0**100
MIB = 1 << 20
LANE = 128


def mxu(left, right, dims):
    return lax.dot_general(left, right, dims, preferred_element_type=F32)


def params(limit=56):
    return pltpu.CompilerParams(vmem_limit_bytes=limit * MIB)


def cost(flops, moved=0):
    return pl.CostEstimate(flops=int(flops), bytes_accessed=int(moved), transcendentals=0)


def swap_cores(value):
    return lax.ppermute(value, "mp", [(0, 1), (1, 0)])


def shift(value, axis, by):
    size = lax.axis_size(axis)
    return lax.ppermute(value, axis, [(i, (i + by) % size) for i in range(size)])


def send_near(kv):
    return [kv] + [shift(kv, "seq", k) for k in range(1, lax.axis_size("seq"))]


def send_far(near):
    return [part[None] for part in near + [swap_cores(value) for value in near]]


def pick(value, index, axis):
    return lax.dynamic_index_in_dim(value, index, axis, keepdims=False)


def send_steps(value, axis, dim):
    size, me = lax.axis_size(axis), lax.axis_index(axis)
    terms = [pick(value, me, dim)]
    for k in range(1, size):
        terms.append(shift(pick(value, (me + k) % size, dim), axis, k))
    return terms


def add_up(terms):
    total = terms[0].astype(F32)
    for term in terms[1:]:
        total = total + term.astype(F32)
    return total


def by_core(own, other, axis):
    first = lax.axis_index("mp") == 0
    return jnp.concatenate(
        [jnp.where(first, own, other), jnp.where(first, other, own)], axis=axis
    )


def rotate_rows(values, cosine, sine_table):
    half = values.shape[0] // 2
    a, b = values[:half], values[half:]
    return jnp.concatenate([a * cosine - b * sine_table, b * cosine + a * sine_table], axis=0)


def project_kernel(
    sent, x_ref, og_ref, gain_ref, wqo_ref, wqp_ref, wto_ref, wtp_ref, wr_ref, wdo_ref, wdp_ref,
    cos_ref, sin_ref, kv_ref, nt_ref, q_ref, ga_ref, wq_ref, wkv_ref, near_ref, far_ref,
    kept, wd, load_sems, own_sems, sends, receives,
):
    b = pl.program_id(0)
    count_s = lax.axis_size("seq")
    me_s, core = lax.axis_index("seq"), lax.axis_index("mp")
    peers = [{"seq": lax.rem(me_s + k, count_s)} for k in range(1, count_s)]
    other_core = {"mp": 1 - core}
    near, forward = [], []
    slots = iter(range(sends.shape[0]))

    def link(source, target, peer):
        slot = next(slots)
        return pltpu.make_async_remote_copy(
            src_ref=source,
            dst_ref=target,
            send_sem=sends.at[slot],
            recv_sem=receives.at[slot],
            device_id=peer,
            device_id_type=pl.DeviceIdType.MESH,
        )

    for i in range(sent):
        near.append([link(kept.at[i], near_ref.at[k, i], peers[k - 1]) for k in range(1, count_s)])
        forward.append(
            [link(kept.at[i], far_ref.at[0, i], other_core)]
            + [link(near_ref.at[k, i], far_ref.at[k, i], other_core) for k in range(1, count_s)]
        )
    own = [pltpu.make_async_copy(kept.at[i], near_ref.at[0, i], own_sems.at[i]) for i in range(sent)]
    loads = load_weights([(wdo_ref, 0, 0), (wdp_ref, 1, 0)], [wd, wd], load_sems)

    @pl.when(b == 0)
    def _():
        for copy in loads:
            copy.start()
        barrier = pltpu.get_barrier_semaphore()
        for peer in [other_core] + peers:
            pl.semaphore_signal(barrier, inc=1, device_id=peer, device_id_type=pl.DeviceIdType.MESH)
        pl.semaphore_wait(barrier, count_s)

        def turn(source, target, at):
            size = source.shape[1]
            row = lax.broadcasted_iota(jnp.int32, (size, size), 0)
            column = lax.broadcasted_iota(jnp.int32, (size, size), 1)
            identity = jnp.where(row == column, 1.0, 0.0).astype(BF)
            target[pl.ds(at, size)] = mxu(identity, source[...], NT).astype(BF)

        for pair, target in (((wto_ref, wtp_ref), wkv_ref), ((wqo_ref, wqp_ref), wq_ref)):
            size = pair[0].shape[1]
            for side, source in enumerate(pair):
                place = jnp.where(core == side, 0, 1)
                turn(source, target, pl.multiple_of(place * size, size))
        turn(wr_ref, wkv_ref, wkv_ref.shape[0] - RD)
        for copy in loads:
            copy.wait()

    x = x_ref[0].astype(F32)
    inverse = lax.rsqrt(jnp.mean(x * x, axis=-1, keepdims=True) + epsilon)
    normed = (x * inverse * gain_ref[...]).astype(BF)
    lin = mxu(wkv_ref[...], normed, NT)
    tied = wkv_ref.shape[0] - RD
    cosine, sine_table = cos_ref[...], sin_ref[...]
    rope = rotate_rows(lin[tied:], cosine, sine_table)
    keys = jnp.concatenate([lin[:tied], rope], axis=0).astype(BF)
    @pl.when(b >= sent)
    def _():
        kv_ref[0] = keys

    for i in range(sent):

        @pl.when(b == i)
        def _():
            kept[i] = keys
            for copy in near[i]:
                copy.start()
            forward[i][0].start()
            own[i].start()

    nt_ref[0] = normed.T
    lin = mxu(wq_ref[...], normed, NT)
    plain = HD - RD
    pieces = []
    for at in range(0, lin.shape[0], HD):
        pieces.append(lin[at : at + plain])
        pieces.append(rotate_rows(lin[at + plain : at + HD], cosine, sine_table))
    queries = jnp.concatenate(pieces, axis=0)
    q_ref[0] = (queries.astype(BF) * HD ** (-0.5)).astype(BF)

    og = og_ref[0]
    for at in range(0, wd.shape[0], 2 * LANE):
        to = slice(at, at + 2 * LANE)
        ga_ref[:, to] = mxu(og, wd[to], NT).astype(BF)

    steps = pl.num_programs(0)
    for i in range(sent):

        @pl.when(b == steps - sent + i)
        def _():
            for copy in near[i]:
                copy.wait()
            for copy in forward[i][1:]:
                copy.start()

    @pl.when(b == steps - 1)
    def _():
        for i in range(sent):
            own[i].wait()
            for copy in forward[i]:
                copy.wait()


def project(x, og, gain, wq, wt, wr, wd, cosine, sine_table, sent):
    count, own, width = x.shape
    rows, half = 2 * wq[0].shape[1], wd[0].shape[0]
    kv_rows = 2 * wt[0].shape[1] + wr.shape[1]
    weights = [*wq, *wt, wr]
    count_s = lax.axis_size("seq")
    whole = lambda array: pl.BlockSpec(array.shape, lambda b: (0, 0))
    seq = pl.BlockSpec((1, own, width), lambda b: (b, 0, 0))
    hbm = pl.BlockSpec(memory_space=pl.ANY)
    gathered = jax.ShapeDtypeStruct((count_s, sent, kv_rows, own), BF)
    links = sent * (2 * count_s - 1)
    return pl.pallas_call(
        functools.partial(project_kernel, sent),
        grid=(count,),
        in_specs=[
            seq, seq, whole(gain), *[whole(part) for part in weights], hbm, hbm, whole(cosine),
            whole(cosine),
        ],
        out_specs=[
            pl.BlockSpec((1, kv_rows, own), lambda b: (jnp.maximum(b - sent, 0), 0, 0)),
            pl.BlockSpec((1, width, own), lambda b: (b, 0, 0)),
            pl.BlockSpec((1, rows, own), lambda b: (b, 0, 0)),
            pl.BlockSpec((own, 2 * half), lambda b: (b, 0)),
            pl.BlockSpec((rows, width), lambda b: (0, 0)),
            pl.BlockSpec((kv_rows, width), lambda b: (0, 0)),
            hbm,
            hbm,
        ],
        out_shape=[
            jax.ShapeDtypeStruct((count - sent, kv_rows, own), BF),
            jax.ShapeDtypeStruct((count, width, own), BF),
            jax.ShapeDtypeStruct((count, rows, own), BF),
            jax.ShapeDtypeStruct((count * own, 2 * half), BF),
            jax.ShapeDtypeStruct((rows, width), BF),
            jax.ShapeDtypeStruct((kv_rows, width), BF),
            gathered,
            gathered,
        ],
        scratch_shapes=[
            pltpu.VMEM((sent, kv_rows, own), BF),
            pltpu.VMEM((2 * half, width), BF),
            pltpu.SemaphoreType.DMA((2 * (half // LANE),)),
            pltpu.SemaphoreType.DMA((sent,)),
            pltpu.SemaphoreType.DMA((links,)),
            pltpu.SemaphoreType.DMA((links,)),
        ],
        compiler_params=pltpu.CompilerParams(
            vmem_limit_bytes=56 * MIB, collective_id=2, has_side_effects=True
        ),
        cost_estimate=cost(3 * 10**10),
        name="project",
    )(x, og, gain, *weights, *wd, cosine, sine_table)


def segment_counts(starts, first, width):
    position = first + lax.broadcasted_iota(jnp.int32, (1, width), 1)
    count = jnp.zeros((1, width), jnp.int32)
    for start in starts:
        count = count + (start <= position).astype(jnp.int32)
    return count


def query_rows(starts, first, width):
    row = lax.broadcasted_iota(jnp.int32, (16, width), 0)
    match = segment_counts(starts, first, width) == row + 1
    return jnp.where(match, 1.0, 0.0).astype(BF)


def key_rows(starts, first, width):
    row = lax.broadcasted_iota(jnp.int32, (16, width), 0)
    match = (segment_counts(starts, first, width) == row + 1) | (row >= len(starts))
    return jnp.where(match, 0.0, -BIG).astype(BF)


def first_rows(count, width):
    row = lax.broadcasted_iota(jnp.int32, (16, width), 0)
    return jnp.where(row < count, 1.0, 0.0).astype(BF)


def three_parts(row, width):
    high = row.astype(BF)
    rest = row - high.astype(F32)
    middle = rest.astype(BF)
    low = (rest - middle.astype(F32)).astype(BF)
    at = lax.broadcasted_iota(jnp.int32, (16, width), 0)
    parts = jnp.where(at == 0, high.astype(F32), 0.0)
    parts = jnp.where(at == 1, middle.astype(F32), parts)
    return jnp.where(at == 2, low.astype(F32), parts).astype(BF)


def start_chunk(starts, first, chunk):
    begin = jnp.int32(0)
    for start in starts:
        begin = jnp.where(start <= first, jnp.maximum(begin, start), begin)
    return begin // chunk


def my_chunk():
    return lax.axis_index("seq") * lax.axis_size("mp") + lax.axis_index("mp")


def place_keys(refs, kv, begin, me):
    steps = lax.axis_size("seq")
    seq, core = lax.axis_index("seq"), lax.axis_index("mp")
    places = [(ref, i) for ref in refs for i in range(ref.shape[0])]
    for at, (ref, i) in enumerate(places):
        of = core if at < steps else 1 - core
        j = lax.rem(seq - at % steps + steps, steps) * 2 + of

        @pl.when((j >= begin) & (j <= me))
        def _():
            kv[j] = ref[i, 0]


def stack_heads(value, at, heads, rows=HD):
    half = value.shape[1] // 2
    return jnp.concatenate(
        [
            value[at + h * rows : at + (h + 1) * rows, s * half : (s + 1) * half]
            for s in range(2)
            for h in range(heads)
        ],
        axis=1,
    )


def stack_queries(starts, first, half, heads):
    return jnp.concatenate(
        [query_rows(starts, first + s * half, half) for s in range(2) for _ in range(heads)], axis=1
    )


def attend_kernel(groups, heads, first, inputs, docs_ref, q_ref, *refs):
    kv_refs = refs[:inputs]
    out_ref, lse_ref, kv_ref, qa, acc, top = refs[-6:]
    b = pl.program_id(0) + first
    own = q_ref.shape[2]
    ndoc = docs_ref.shape[1]
    starts = [docs_ref[b, k] for k in range(ndoc)]
    me = my_chunk()
    begin = start_chunk(starts, me * own, own)
    half = own // 2
    begin_second = start_chunk(starts, me * own + half, own)
    place_keys(kv_refs, kv_ref, begin, me)
    wide = heads * own
    first_half = wide // 2
    tied = groups * HD
    plain = HD - RD
    q_doc = stack_queries(starts, me * own, half, heads)
    q_all = q_ref[0]
    for g in range(groups):
        qa[g, :HD] = stack_heads(q_all, g * heads * HD, heads)
        qa[g, HD : HD + 16] = q_doc
        qa[g, HD + 16 :] = jnp.zeros((LANE - HD - 16, wide), BF)
    ones = first_rows(1, own)
    zeros = jnp.zeros((LANE - HD - 16, own), BF)

    def keys_of(j, g):
        doc = key_rows(starts, j * own, own)
        block = jnp.concatenate(
            [
                kv_ref[j, g * HD : g * HD + plain],
                kv_ref[j, tied : tied + RD],
                doc,
                zeros,
            ],
            axis=0,
        )
        return block.T

    def values_of(j, g):
        return jnp.concatenate([kv_ref[j, g * HD : (g + 1) * HD], ones], axis=0)

    key_at = lax.broadcasted_iota(jnp.int32, (own, half), 0)
    query_at = lax.broadcasted_iota(jnp.int32, (own, half), 1)
    causal = jnp.concatenate(
        [key_at <= query_at + s * half for s in range(2) for _ in range(heads)], axis=1
    )

    def block(j, lanes, diagonal=False):
        def logits_of(g):
            return mxu(keys_of(j, g), qa[g, :, lanes], NN)

        following = logits_of(0)
        for g in range(groups):
            logits = following
            if g + 1 < groups:
                following = logits_of(g + 1)
            if diagonal:
                logits = jnp.where(causal, logits, masked_value)
            peak = jnp.max(logits, axis=0, keepdims=True)
            if not diagonal:
                old = top[g, :, lanes]
                peak = jnp.maximum(old, peak)
            weights = jnp.exp(logits - peak).astype(BF)
            added = mxu(values_of(j, g), weights, NN)
            if not diagonal:
                added = acc[g, :, lanes] * jnp.exp(old - peak) + added
            acc[g, :, lanes] = added
            top[g, :, lanes] = peak

    block(me, slice(0, wide), True)

    def both(i, carry):
        block(me - 1 - i, slice(0, wide))
        return carry

    def first_only(i, carry):
        block(begin_second - 1 - i, slice(0, first_half))
        return carry

    lax.fori_loop(0, me - begin_second, both, 0)
    lax.fori_loop(0, begin_second - begin, first_only, 0)
    for g in range(groups):
        total = acc[g, HD : HD + 1]
        result = acc[g, :HD] / total
        lse_ref[0, g : g + 1] = top[g] + jnp.log(total)
        for s in range(2):
            for h in range(heads):
                at, of = (g * heads + h) * HD, (s * heads + h) * half
                out_ref[0, at : at + HD, s * half : (s + 1) * half] = result[:, of : of + half].astype(BF)


def kv_specs(kv, kv_at):
    return [
        pl.BlockSpec((part.shape[0], 1, *part.shape[2:]), lambda b: (0, b + kv_at, 0, 0))
        for part in kv
    ]


def attend_forward(docs, q, kv, groups, heads, first, size, kv_at, into):
    kv_rows, own = kv[0].shape[2:]
    count, chunks, inputs = docs.shape[0], 2 * lax.axis_size("seq"), len(kv)
    wide = heads * own
    hbm = pl.BlockSpec(memory_space=pl.ANY)
    return pl.pallas_call(
        functools.partial(attend_kernel, groups, heads, first, inputs),
        grid=(size,),
        in_specs=[
            pl.BlockSpec(memory_space=pltpu.SMEM),
            pl.BlockSpec((1, q.shape[1], own), lambda b: (b + first, 0, 0)),
        ]
        + kv_specs(kv, kv_at)
        + [hbm] * len(into),
        out_specs=[
            pl.BlockSpec((1, q.shape[1], own), lambda b: (b + first, 0, 0)),
            pl.BlockSpec((1, groups, wide), lambda b: (b + first, 0, 0)),
        ],
        out_shape=[
            jax.ShapeDtypeStruct(q.shape, BF),
            jax.ShapeDtypeStruct((count, groups, wide), F32),
        ],
        scratch_shapes=[
            pltpu.VMEM((chunks, kv_rows, own), BF),
            pltpu.VMEM((groups, LANE, wide), BF),
            pltpu.VMEM((groups, HD + 16, wide), F32),
            pltpu.VMEM((groups, 1, wide), F32),
        ],
        input_output_aliases={2 + inputs + i: i for i in range(len(into))},
        compiler_params=params(),
        cost_estimate=cost(10**10 * size),
        name="attend",
    )(docs, q, *kv, *into)


def attend_back_kernel(
    groups, heads, first, inputs, docs_ref, q_ref, do_ref, lse_ref, delta_ref, rot_ref, *refs
):
    kv_refs = refs[:inputs]
    chunks = 2 * lax.axis_size("seq")
    dq_ref, keep_ref, give_ref, kv_ref, stage, qs, qa, ds_, da, dq = refs[-10:]
    b = pl.program_id(0) + first
    own = q_ref.shape[2]
    ndoc = docs_ref.shape[1]
    starts = [docs_ref[b, k] for k in range(ndoc)]
    me = my_chunk()
    begin = start_chunk(starts, me * own, own)
    half = own // 2
    begin_second = start_chunk(starts, me * own + half, own)
    place_keys(kv_refs, kv_ref, begin, me)
    wide = heads * own
    tied = groups * HD
    plain = HD - RD
    q_doc = stack_queries(starts, me * own, half, heads)
    q_all, do_all = q_ref[0], do_ref[0]
    pad_q = jnp.zeros((LANE - HD - 32, wide), BF)
    pad_d = jnp.zeros((LANE - HD - 16, wide), BF)
    row_at = lax.broadcasted_iota(jnp.int32, (own, own), 0)
    column_at = lax.broadcasted_iota(jnp.int32, (own, own), 1)
    identity = jnp.where(row_at == column_at, 1.0, 0.0).astype(BF)

    def turn(rows, ref):
        for h in range(0, heads, 2):
            pair = [rows[:, (h + i) * own : (h + i + 1) * own] for i in range(2)]
            turned = mxu(identity, jnp.concatenate(pair, axis=0), NT).astype(BF)
            ref[h * own : (h + 1) * own] = turned[:, :LANE]
            ref[(h + 1) * own : (h + 2) * own] = turned[:, LANE:]

    for g in range(groups):
        q_rows = stack_heads(q_all, g * heads * HD, heads)
        do_rows = stack_heads(do_all, g * heads * HD, heads)
        qs[g] = q_rows
        ds_[g] = do_rows
        lse_rows = three_parts(-lse_ref[0, g : g + 1], wide)
        delta_row = stack_heads(delta_ref[0], g * heads, heads, 1)
        delta_rows = three_parts(-delta_row, wide)
        turn(jnp.concatenate([q_rows, q_doc, lse_rows, pad_q], axis=0), qa.at[g])
        turn(jnp.concatenate([do_rows, delta_rows, pad_d], axis=0), da.at[g])
    ones = first_rows(3, own)
    pad_k = jnp.zeros((LANE - HD - 32, own), BF)
    pad_v = jnp.zeros((LANE - HD - 16, own), BF)

    seq, core = lax.axis_index("seq"), lax.axis_index("mp")
    steps = chunks // 2

    def deliver(j, value):
        k = lax.rem(j // 2 - seq + steps, steps)

        @pl.when(lax.rem(j, 2) == core)
        def _():
            keep_ref[k, 0] = value()

        @pl.when(lax.rem(j, 2) != core)
        def _():
            give_ref[k, 0] = value()

    def clear(j, carry):
        deliver(j, lambda: jnp.zeros(keep_ref.shape[2:], BF))
        return carry

    lax.fori_loop(0, begin, clear, 0)
    lax.fori_loop(me + 1, chunks, clear, 0)

    def block(j, rows, diagonal):
        doc = key_rows(starts, j * own, own)
        rope_rows = kv_ref[j, tied : tied + RD]
        rope_sum = jnp.zeros((RD, own), F32)

        def keys_of(g):
            return jnp.concatenate(
                [kv_ref[j, g * HD : g * HD + plain], rope_rows], axis=0
            )

        def products(g):
            values = kv_ref[j, g * HD : (g + 1) * HD]
            return (
                mxu(qa[g, :rows], jnp.concatenate([keys_of(g), doc, ones, pad_k], axis=0), NN),
                mxu(da[g, :rows], jnp.concatenate([values, ones, pad_v], axis=0), NN),
            )

        following = products(0)
        for g in range(groups):
            logits, slopes = following
            if g + 1 < groups:
                following = products(g + 1)
            keys = keys_of(g)
            weights = jnp.exp(logits)
            if diagonal:
                query_at = lax.broadcasted_iota(jnp.int32, (half, own), 0)
                key_at = lax.broadcasted_iota(jnp.int32, (half, own), 1)
                causal = jnp.concatenate(
                    [key_at <= query_at + s * half for s in range(2) for _ in range(heads)], axis=0
                )
                weights = jnp.where(causal, weights, 0.0)
            grads = (weights * slopes).astype(BF)
            grad_values = mxu(ds_[g, :, :rows], weights.astype(BF), NN)
            grad_keys = mxu(qs[g, :, :rows], grads, NN)
            keys_t = keys.T
            grad_queries = mxu(grads, jnp.concatenate([keys_t, keys_t], axis=1), NN)
            if diagonal:
                dq[g] = grad_queries
            else:
                dq[g, :rows] += grad_queries
            stage[g * HD : g * HD + plain] = (
                grad_values[:plain] + grad_keys[:plain]
            ).astype(BF)
            stage[g * HD + plain : (g + 1) * HD] = grad_values[plain:].astype(BF)
            rope_sum = rope_sum + grad_keys[plain:]
        stage[tied : tied + RD] = rope_sum.astype(BF)
        deliver(j, lambda: stage[...])

    block(me, wide, True)

    def both(j, carry):
        block(j, wide, False)
        return carry

    def first_only(j, carry):
        block(j, wide // 2, False)
        return carry

    lax.fori_loop(begin_second, me, both, 0)
    lax.fori_loop(begin, begin_second, first_only, 0)
    straight, ahead, behind = rot_ref[0], rot_ref[1], rot_ref[2]
    lane = lax.broadcasted_iota(jnp.int32, (half, LANE), 1)
    quarter = RD // 2
    for g in range(groups):
        for s in range(2):
            positions = slice(s * half, (s + 1) * half)
            for pair in range(heads // 2):
                at = (s * heads + 2 * pair) * half
                two = jnp.where(lane < HD, dq[g, at : at + half], dq[g, at + half : at + 2 * half])
                turned = (
                    two * straight[positions]
                    + pltpu.roll(two, LANE - quarter, 1) * ahead[positions]
                    + pltpu.roll(two, quarter, 1) * behind[positions]
                )
                to = (g * heads + 2 * pair) * HD
                dq_ref[positions, to : to + 2 * HD] = turned.astype(BF)


def attend_backward(docs, q, do, lse, delta, turns, kv, groups, heads, first, size, kv_at, into):
    kv_rows, own = kv[0].shape[2:]
    count, chunks, inputs = docs.shape[0], 2 * lax.axis_size("seq"), len(kv)
    wide = heads * own
    width = q.shape[1]
    column = pl.BlockSpec((1, width, own), lambda b: (b + first, 0, 0))
    hbm = pl.BlockSpec(memory_space=pl.ANY)
    return pl.pallas_call(
        functools.partial(attend_back_kernel, groups, heads, first, inputs),
        grid=(size,),
        in_specs=[
            pl.BlockSpec(memory_space=pltpu.SMEM),
            column,
            column,
            pl.BlockSpec((1, groups, wide), lambda b: (b + first, 0, 0)),
            pl.BlockSpec((1, groups * heads, own), lambda b: (b + first, 0, 0)),
            pl.BlockSpec(turns.shape, lambda b: (0, 0, 0)),
        ]
        + kv_specs(kv, kv_at)
        + [hbm] * len(into),
        out_specs=[
            pl.BlockSpec((own, width), lambda b: (b + first, 0)),
            pl.BlockSpec((chunks // 2, 1, kv_rows, own), lambda b: (0, b, 0, 0)),
            pl.BlockSpec((chunks // 2, 1, kv_rows, own), lambda b: (0, b, 0, 0)),
        ],
        out_shape=[
            jax.ShapeDtypeStruct((count * own, width), BF),
            jax.ShapeDtypeStruct((chunks // 2, size, kv_rows, own), BF),
            jax.ShapeDtypeStruct((chunks // 2, size, kv_rows, own), BF),
        ],
        scratch_shapes=[
            pltpu.VMEM((chunks, kv_rows, own), BF),
            pltpu.VMEM((kv_rows, own), BF),
            pltpu.VMEM((groups, HD, wide), BF),
            pltpu.VMEM((groups, wide, LANE), BF),
            pltpu.VMEM((groups, HD, wide), BF),
            pltpu.VMEM((groups, wide, LANE), BF),
            pltpu.VMEM((groups, wide, LANE), F32),
        ],
        input_output_aliases={6 + inputs + i: i for i in range(len(into))},
        compiler_params=params(),
        cost_estimate=cost(10**9 * size),
        name="attend_back",
    )(docs, q, do, lse, delta, turns, *kv, *into)


def join_cores(keep, received):
    return [
        (keep[k].astype(F32) + received[k].astype(F32)).astype(BF) for k in range(keep.shape[0])
    ]


def send_keys(summed):
    return [summed[0]] + [shift(summed[k], "seq", k) for k in range(1, len(summed))]


def load_weights(refs, targets, sems):
    copies = []
    slot = 0
    for (source, side, axis), target in zip(refs, targets, strict=True):
        blocks = source.shape[axis] // LANE
        for t in range(blocks):
            to = pl.ds((2 * t + side) * LANE, LANE)
            of = pl.ds(t * LANE, LANE)
            src = source.at[:, of] if axis == 1 else source.at[of]
            dst = target.at[:, to] if axis == 1 else target.at[to]
            copies.append(pltpu.make_async_copy(src, dst, sems.at[slot]))
            slot += 1
    return copies


def put(ref, t, value):
    value = value.astype(BF)
    ref[2 * t], ref[2 * t + 1] = value[:, :LANE], value[:, LANE:]


def wide(ref):
    return jnp.concatenate([ref[i] for i in range(ref.shape[0])], axis=1)


def feed_kernel(
    x_ref, og_ref, ga_ref, o_ref, gain_ref, wo_ref, wgo_ref, wgp_ref, wuo_ref, wup_ref, wdo_ref, wdp_ref,
    out_ref, nt_ref, ogt_ref, act_ref, gg_ref, gu_ref, gh_ref, gat_ref, do_ref, delta_ref, gg2_ref,
    wo, wg, wu, wd, sems,
):
    b = pl.program_id(0)

    @pl.when(b == 0)
    def _():
        copies = [pltpu.make_async_copy(wo_ref, wo, sems.at[sems.shape[0] - 1])]
        copies += load_weights(
            [
                (wgo_ref, 0, 1), (wgp_ref, 1, 1), (wuo_ref, 0, 1), (wup_ref, 1, 1),
                (wdo_ref, 0, 0), (wdp_ref, 1, 0),
            ],
            [wg, wg, wu, wu, wd, wd],
            sems,
        )
        for copy in copies:
            copy.start()
        for copy in copies:
            copy.wait()
        gg2_ref[...] = jnp.zeros(gg2_ref.shape, F32)

    og = og_ref[0]
    heads_out = o_ref[0]
    gain = gain_ref[...]
    hidden = x_ref[0].astype(F32) + mxu(heads_out, wo[...], TN)
    inverse = lax.rsqrt(jnp.mean(hidden * hidden, axis=-1, keepdims=True) + epsilon)
    normed = (hidden * inverse * gain).astype(BF)
    nt_ref[0] = normed.T
    ogt_ref[0] = og.T
    units = wg.shape[1]
    tile = 2 * LANE
    for t in range(units // tile):
        at = slice(t * tile, (t + 1) * tile)
        gate = mxu(normed, wg[:, at], NN)
        up = mxu(normed, wu[:, at], NN)
        grad = ga_ref[:, at].astype(F32)
        sigmoid = 1.0 / (1.0 + jnp.exp(-gate))
        silu = gate * sigmoid
        put(act_ref, t, silu * up)
        put(gu_ref, t, grad * silu)
        put(gg_ref, t, grad * up * (sigmoid + silu * (1.0 - sigmoid)))
    result = mxu(wide(act_ref), wd[...], NN)
    out_ref[0] = (hidden + result).astype(BF)
    grad_normed = mxu(wide(gg_ref), wg[...], NT) + mxu(wide(gu_ref), wu[...], NT)
    scaled = grad_normed * gain
    gg2_ref[...] += jnp.sum(grad_normed * (hidden * inverse), axis=0, keepdims=True)
    mean = jnp.mean(scaled * hidden, axis=-1, keepdims=True)
    grad_hidden = og.astype(F32) + inverse * scaled - hidden * (inverse * inverse * inverse * mean)
    grad_attended = grad_hidden.astype(BF)
    gh_ref[0] = grad_attended
    gat_ref[0] = grad_attended.T
    grad_heads = mxu(wo[...], grad_attended, NT).astype(BF)
    do_ref[0] = grad_heads
    product = grad_heads.astype(F32) * heads_out.astype(F32)
    for h in range(product.shape[0] // HD):
        delta_ref[0, h : h + 1] = jnp.sum(product[h * HD : (h + 1) * HD], axis=0, keepdims=True)


def feed(x, og, slopes, heads_out, gain, wo, wg, wu, wd):
    count, own, width = x.shape
    hd = heads_out.shape[1]
    half = wg[0].shape[1]
    units = 2 * half
    tokens = count * own
    seq = pl.BlockSpec((1, own, width), lambda b: (b, 0, 0))
    column = lambda rows: pl.BlockSpec((1, rows, own), lambda b: (b, 0, 0))
    row = pl.BlockSpec((own, units), lambda b: (b, 0))
    blocks = pl.BlockSpec((units // LANE, own, LANE), lambda b: (0, b, 0))
    hbm = pl.BlockSpec(memory_space=pl.ANY)
    return pl.pallas_call(
        feed_kernel,
        grid=(count,),
        in_specs=[seq, seq, row, column(hd), pl.BlockSpec((1, width), lambda b: (0, 0))] + [hbm] * 7,
        out_specs=[
            seq, column(width), column(width), blocks, blocks, blocks, seq, column(width), column(hd),
            pl.BlockSpec((1, hd // HD, own), lambda b: (b, 0, 0)),
            pl.BlockSpec((1, width), lambda b: (0, 0)),
        ],
        out_shape=[
            jax.ShapeDtypeStruct(x.shape, BF),
            jax.ShapeDtypeStruct((count, width, own), BF),
            jax.ShapeDtypeStruct((count, width, own), BF),
            jax.ShapeDtypeStruct((units // LANE, tokens, LANE), BF),
            jax.ShapeDtypeStruct((units // LANE, tokens, LANE), BF),
            jax.ShapeDtypeStruct((units // LANE, tokens, LANE), BF),
            jax.ShapeDtypeStruct(x.shape, BF),
            jax.ShapeDtypeStruct((count, width, own), BF),
            jax.ShapeDtypeStruct((count, hd, own), BF),
            jax.ShapeDtypeStruct((count, hd // HD, own), F32),
            jax.ShapeDtypeStruct((1, width), F32),
        ],
        scratch_shapes=[
            pltpu.VMEM((hd, width), BF),
            pltpu.VMEM((width, units), BF),
            pltpu.VMEM((width, units), BF),
            pltpu.VMEM((units, width), BF),
            pltpu.SemaphoreType.DMA((6 * (half // LANE) + 1,)),
        ],
        compiler_params=params(),
        cost_estimate=cost(2 * tokens * width * (5 * units + 2 * hd)),
        name="feed",
    )(x, og, slopes, heads_out, gain, wo, *wg, *wu, *wd)


def regroup_rows(value, split):
    if split is None:
        return value
    count_d, count_s = split
    own = value.shape[0] // (count_d * count_s)
    return jnp.concatenate(
        [
            value[(d * count_s + s) * own : (d * count_s + s + 1) * own]
            for s in range(count_s)
            for d in range(count_d)
        ],
        axis=0,
    )


def side_by_side(source, target, sems, slot):
    count, _, own = source.shape
    return [
        pltpu.make_async_copy(
            source.at[i], target.at[:, pl.ds(i * own, own)], sems.at[slot + i]
        )
        for i in range(count)
    ]


def early_kernel(
    split, cut, nt_ref, gg_ref, gu_ref, act_ref, act_next_ref, ogt_ref, gat_ref, o_ref, out_ref,
    rest_ref, nt, ogt, gat, heads_out, stage, landed, load_sems, sends, receives,
):
    t = pl.program_id(0)
    core = lax.axis_index("mp")
    tiles = landed.shape[0]
    tile = 2 * LANE
    pairs, head_tiles = gg_tiles(gg_ref, tiles, heads_out)
    other_core = {"mp": 1 - core}
    loads = []
    for source, target in ((nt_ref, nt), (gat_ref, gat), (o_ref, heads_out), (ogt_ref, ogt)):
        loads.append(side_by_side(source, target, load_sems, len(loads) * nt_ref.shape[0]))

    @pl.when(t == 0)
    def _():
        for copies in loads:
            for copy in copies:
                copy.start()
        barrier = pltpu.get_barrier_semaphore()
        pl.semaphore_signal(barrier, inc=1, device_id=other_core, device_id_type=pl.DeviceIdType.MESH)
        pl.semaphore_wait(barrier, 1)
        for copy in loads[0]:
            copy.wait()

    @pl.when(t == pairs)
    def _():
        for copy in loads[1] + loads[2]:
            copy.wait()

    @pl.when(t == pairs + head_tiles)
    def _():
        for copy in loads[3]:
            copy.wait()

    def send(i):
        return pltpu.make_async_remote_copy(
            src_ref=stage.at[lax.rem(i, 2)],
            dst_ref=landed.at[i],
            send_sem=sends.at[i],
            recv_sem=receives.at[i],
            device_id=other_core,
            device_id_type=pl.DeviceIdType.MESH,
        )

    def deliver(product):
        @pl.when(t < tiles)
        def _():
            @pl.when(t >= 2)
            def _():
                send(t - 2).wait_send()

            stage[lax.rem(t, 2)] = regroup_rows(product(), split).astype(BF)
            send(t).start()

        @pl.when(t >= tiles)
        def _():
            @pl.when(t < tiles + 2)
            def _():
                send(t - 2).wait_send()

            send(t - tiles).wait_recv()
            total = regroup_rows(product(), split) + landed[t - tiles].astype(F32)
            total = total.astype(BF)
            out_ref[...] = jnp.where(t < tiles + cut, total, out_ref[...])
            rest_ref[...] = total

    at = lax.rem(t, tiles)

    @pl.when(at < pairs)
    def _():
        deliver(lambda: mxu(nt[...], jnp.concatenate([gg_ref[0], gu_ref[0]], axis=1), NN))

    @pl.when((at >= pairs) & (at < pairs + head_tiles))
    def _():
        side = jnp.where(t < tiles, 1 - core, core)
        row = pl.multiple_of((side * head_tiles + at - pairs) * tile, tile)
        deliver(lambda: mxu(gat[...], heads_out[pl.ds(row, tile)], NT))

    @pl.when(at >= pairs + head_tiles)
    def _():
        deliver(
            lambda: mxu(ogt[...], jnp.concatenate([act_ref[0], act_next_ref[0]], axis=1), NN)
        )


def gg_tiles(gg_ref, tiles, heads_out):
    head_tiles = heads_out.shape[0] // (4 * LANE)
    return (2 * (tiles - head_tiles)) // 3, head_tiles


def early_grads(nt, gg, gu, act, ogt, gat, heads_out, split):
    count, width, own = nt.shape
    tokens = count * own
    units = gg.shape[0] * LANE
    blocks = units // (2 * LANE)
    tile = 2 * LANE
    hd = heads_out.shape[1]
    head_tiles = hd // (2 * tile)
    down_tiles = (blocks + 1) // 2
    tiles = blocks + head_tiles + down_tiles
    cut = tiles - 4
    rest = units + units // 2 + hd // 2 - cut * tile
    hbm = pl.BlockSpec(memory_space=pl.ANY)
    side = lambda t: jnp.where(t < tiles, 1, 0)

    def pair(t):
        return (2 * jnp.minimum(lax.rem(t, tiles), blocks - 1) + side(t), 0, 0)

    def down(t, shift_by):
        at = jnp.clip(lax.rem(t, tiles) - blocks - head_tiles, 0, down_tiles - 1)
        return (2 * jnp.minimum(2 * at + shift_by, blocks - 1) + side(t), 0, 0)

    block = lambda index: pl.BlockSpec((1, tokens, LANE), index)
    return pl.pallas_call(
        functools.partial(early_kernel, split, cut),
        grid=(2 * tiles,),
        in_specs=[
            hbm,
            block(pair),
            block(pair),
            block(lambda t: down(t, 0)),
            block(lambda t: down(t, 1)),
            hbm,
            hbm,
            hbm,
        ],
        out_specs=[
            pl.BlockSpec((width, tile), lambda t: (0, jnp.clip(t - tiles, 0, cut - 1))),
            pl.BlockSpec((width, tile), lambda t: (0, jnp.maximum(t - tiles - cut, 0))),
        ],
        out_shape=[
            jax.ShapeDtypeStruct((width, cut * tile), BF),
            jax.ShapeDtypeStruct((width, rest), BF),
        ],
        scratch_shapes=[
            pltpu.VMEM((width, tokens), BF),
            pltpu.VMEM((width, tokens), BF),
            pltpu.VMEM((width, tokens), BF),
            pltpu.VMEM((hd, tokens), BF),
            pltpu.VMEM((2, width, tile), BF),
            pltpu.VMEM((tiles, width, tile), BF),
            pltpu.SemaphoreType.DMA((4 * count,)),
            pltpu.SemaphoreType.DMA((tiles,)),
            pltpu.SemaphoreType.DMA((tiles,)),
        ],
        compiler_params=pltpu.CompilerParams(
            vmem_limit_bytes=56 * MIB, collective_id=3, has_side_effects=True
        ),
        cost_estimate=cost(6 * 10**10),
        name="early_grads",
    )(nt, gg, gu, act, act, ogt, gat, heads_out)


def tail_kernel(
    order, x_ref, dq_ref, nt_ref, gain_ref, wq_ref, wkv_ref, cos_ref, sin_ref, gg2_ref,
    nt_all_ref, dq_all_ref, early_ref, near_refs, *refs,
):
    count_d, count_s = lax.axis_size("dp"), lax.axis_size("seq")
    me_d, me_s, core = lax.axis_index("dp"), lax.axis_index("seq"), lax.axis_index("mp")
    (keep_mid, got_mid, keep_end, give_end, update_ref, query_out, small_out, early_out) = refs[:8]
    (
        key_in, sum_mid, sum_end, got_end, query_stage, query_in, query_sum, query_seq, query_part,
        query_dp, early_in, early_own, nt_all, dq_all, load_sems, dw, gg1, small_other, small_in, small_sum, small_seq, small_part,
        small_dp, sends, receives,
    ) = refs[8:]
    rows = query_out.shape[0]
    step = pl.program_id(0)
    other_core = {"mp": 1 - core}
    seq_peers = [{"seq": lax.rem(me_s + k, count_s)} for k in range(1, count_s)]
    dp_peers = [{"dp": lax.rem(me_d + k, count_d)} for k in range(1, count_d)]
    peers = [other_core] + seq_peers + dp_peers
    slots = iter(range(sends.shape[0]))

    def link(source, target, peer):
        slot = next(slots)
        return pltpu.make_async_remote_copy(
            src_ref=source,
            dst_ref=target,
            send_sem=sends.at[slot],
            recv_sem=receives.at[slot],
            device_id=peer,
            device_id_type=pl.DeviceIdType.MESH,
        )

    to_seq = [lax.rem(me_s + k, count_s) for k in range(1, count_s)]
    to_dp = [lax.rem(me_d + k, count_d) for k in range(1, count_d)]
    early_copies = [
        link(early_ref.at[to_dp[k]], early_in.at[k], dp_peers[k]) for k in range(count_d - 1)
    ]
    end_core = link(give_end, got_end, other_core)
    key_copies, at = [], 0
    for part in (sum_mid, sum_end):
        size = part.shape[1]
        key_copies.append(
            [
                link(part.at[k + 1], key_in.at[k, pl.ds(at, size)], seq_peers[k])
                for k in range(count_s - 1)
            ]
        )
        at += size
    query_core = link(query_stage, query_in, other_core)
    query_seqs = [
        link(query_sum.at[to_seq[k]], query_seq.at[k], seq_peers[k]) for k in range(count_s - 1)
    ]
    query_dps = [
        link(query_part.at[to_dp[k]], query_dp.at[k], dp_peers[k]) for k in range(count_d - 1)
    ]
    small_core = link(small_other, small_in, other_core)
    small_seqs = [
        link(small_sum.at[to_seq[k]], small_seq.at[k], seq_peers[k]) for k in range(count_s - 1)
    ]
    small_dps = [
        link(small_part.at[to_dp[k]], small_dp.at[k], dp_peers[k]) for k in range(count_d - 1)
    ]

    def start(copies):
        for copy in copies:
            copy.start()

    def by_seq(total, target):
        for s in range(count_s):
            for d in range(count_d):
                of = (d * count_s + s) * rows
                target[s, d * rows : (d + 1) * rows] = total[of : of + rows].astype(BF)

    def gather(own, copies, arrived):
        total = own.astype(F32)
        for k, copy in enumerate(copies):
            copy.wait()
            total = total + arrived[k].astype(F32)
        return total

    def by_dp(total, target):
        for d in range(count_d):
            target[d] = total[d * rows : (d + 1) * rows].astype(BF)

    loads = side_by_side(nt_all_ref, nt_all, load_sems, 2) + [
        pltpu.make_async_copy(dq_all_ref, dq_all, load_sems.at[0]),
        pltpu.make_async_copy(early_ref.at[me_d], early_own, load_sems.at[1]),
    ]

    def join(mine, got, total):
        for k in range(count_s):
            total[k] = (mine[k].astype(F32) + got[k].astype(F32)).astype(BF)

    def query_product(half):
        size = query_stage.shape[1]
        columns = pl.ds(pl.multiple_of(half * size, size), size)
        return mxu(nt_all[...], dq_all[:, columns], NN)

    @pl.when(step == 0)
    def _():
        barrier = pltpu.get_barrier_semaphore()
        for peer in peers:
            pl.semaphore_signal(barrier, inc=1, device_id=peer, device_id_type=pl.DeviceIdType.MESH)
        pl.semaphore_wait(barrier, len(peers))
        start([end_core])
        join(keep_mid, got_mid, sum_mid)
        start(key_copies[0])
        start(early_copies)
        start(loads)
        end_core.wait()
        join(keep_end, got_end, sum_end)
        start(key_copies[1])
        for load in loads:
            load.wait()
        query_stage[...] = query_product(1 - core).astype(BF)
        start([query_core])
        dw[...] = jnp.zeros(dw.shape, F32)
        gg1[...] = jnp.zeros(gg1.shape, F32)

    @pl.when(step == 1)
    def _():
        product = query_product(core)
        query_core.wait()
        by_seq(product + query_in[...].astype(F32), query_sum)
        start(query_seqs)

    tied = wkv_ref.shape[0] - RD

    def finish(summed):
        turned = rotate_rows(summed[tied:], cos_ref[...], -sin_ref[...])
        dkv = jnp.concatenate([summed[:tied], turned], axis=0).astype(BF)
        grad_normed = mxu(dq_ref[...], wq_ref[...], NN) + mxu(dkv, wkv_ref[...], TN)
        dw[...] += mxu(nt_ref[0], dkv, NT)
        x = x_ref[0].astype(F32)
        inverse = lax.rsqrt(jnp.mean(x * x, axis=-1, keepdims=True) + epsilon)
        scaled = grad_normed * gain_ref[...]
        gg1[...] += jnp.sum(grad_normed * (x * inverse), axis=0, keepdims=True)
        mean = jnp.mean(scaled * x, axis=-1, keepdims=True)
        update = inverse * scaled - x * (inverse * inverse * inverse * mean)
        update_ref[0] = update.astype(BF)

    begin = 0
    for (_, size), terms in zip(order, near_refs):

        @pl.when((step >= begin) & (step < begin + size))
        def _():
            summed = terms[0][0].astype(F32)
            for ref in terms[1:]:
                summed = summed + ref[0].astype(F32)
            finish(summed)

        begin += size

    base = begin
    for part, far in enumerate((sum_mid, sum_end)):
        size = far.shape[1]

        @pl.when(step == begin)
        def _():
            for copy in key_copies[part]:
                copy.wait()

        @pl.when((step >= begin) & (step < begin + size))
        def _():
            at = step - base
            summed = far[0, step - begin].astype(F32)
            for k in range(count_s - 1):
                summed = summed + key_in[k, at].astype(F32)
            finish(summed)

        begin += size

    @pl.when(step == begin - 2)
    def _():
        total = gather(query_sum[me_s], query_seqs, query_seq)
        by_dp(total, query_part)
        start(query_dps)

    @pl.when(step == begin - 1)
    def _():
        width = dw.shape[0]
        pad = jnp.zeros((LANE - RD, width), F32)
        row = lax.broadcasted_iota(jnp.int32, (LANE, width), 0)
        gains = jnp.where(row == RD, gg1[...], 0.0)
        gains = jnp.where(row == RD + 1, gg2_ref[...], gains)
        weights = dw[...]
        rope = jnp.concatenate([weights[:, tied:], jnp.zeros((width, LANE - RD), F32)], axis=1)
        small = rope + gains.T
        half = tied // 2
        first, second = weights[:, :half], weights[:, half:tied]
        mine = jnp.concatenate([jnp.where(core == 0, first, second), small], axis=1)
        other = jnp.concatenate([jnp.where(core == 0, second, first), small], axis=1)
        small_other[...] = other.astype(BF)
        start([small_core])
        small_core.wait()
        by_seq(mine + small_in[...].astype(F32), small_sum)
        start(small_seqs)
        by_dp(gather(small_sum[me_s], small_seqs, small_seq), small_part)
        start(small_dps)
        query_out[...] = gather(query_part[me_d], query_dps, query_dp)
        early_out[...] = gather(early_own[...], early_copies, early_in)
        small_out[...] = gather(small_part[me_d], small_dps, small_dp)


def tail(
    order, x, dq, nt, gain, wq, wkv, cosine, sine_table, grad_gain_two, early, near,
    shares,
):
    count, own, width = x.shape
    count_d, count_s = lax.axis_size("dp"), lax.axis_size("seq")
    rows = width // (count_d * count_s)
    kv_rows = wkv.shape[0]
    tied = kv_rows - RD
    wide = dq.shape[1] // 2
    narrow = tied // 2 + LANE
    middle, end = shares[0].shape, shares[2].shape
    sent = middle[1] + end[1]

    def place(i):
        done, at = 0, i
        for first, size in order:
            at = jnp.where((i >= done) & (i < done + size), first + i - done, at)
            done += size
        return at

    seq = pl.BlockSpec((1, own, width), lambda i: (place(i), 0, 0))
    whole = lambda array: pl.BlockSpec(array.shape, lambda i: (0,) * array.ndim)
    near_specs, done = [], 0
    for (_, size), terms in zip(order, near):
        index = lambda i, done=done, size=size: (jnp.clip(i - done, 0, size - 1), 0, 0)
        near_specs += [pl.BlockSpec((1, kv_rows, own), index)] * len(terms)
        done += size
    fixed = [gain, wq, wkv, cosine, sine_table, grad_gain_two]
    hbm = pl.BlockSpec(memory_space=pl.ANY)
    outs = [
        jax.ShapeDtypeStruct(x.shape, BF),
        jax.ShapeDtypeStruct((rows, wide), F32),
        jax.ShapeDtypeStruct((rows, narrow), F32),
        jax.ShapeDtypeStruct((rows, early.shape[2]), F32),
    ]
    near_all = [term for terms in near for term in terms]

    def kernel(*refs):
        head, rest = refs[:12], refs[12 + len(near_all) :]
        nears = [refs[12 + i * count_s : 12 + (i + 1) * count_s] for i in range(len(near))]
        tail_kernel(order, *head, nears, *rest)

    slots = 3 * (count_d - 1) + 4 * (count_s - 1) + 3
    return pl.pallas_call(
        kernel,
        grid=(count,),
        in_specs=[
            seq,
            pl.BlockSpec((own, dq.shape[1]), lambda i: (place(i), 0)),
            pl.BlockSpec((1, width, own), lambda i: (place(i), 0, 0)),
        ]
        + [whole(array) for array in fixed]
        + [hbm, hbm, hbm]
        + near_specs
        + [whole(array) for array in shares],
        out_specs=[seq] + [whole(out) for out in outs[1:]],
        out_shape=outs,
        scratch_shapes=[
            pltpu.VMEM((count_s - 1, sent, kv_rows, own), BF),
            pltpu.VMEM(middle, BF),
            pltpu.VMEM(end, BF),
            pltpu.VMEM(end, BF),
            pltpu.VMEM((width, wide), BF),
            pltpu.VMEM((width, wide), BF),
            pltpu.VMEM((count_s, count_d * rows, wide), BF),
            pltpu.VMEM((count_s - 1, count_d * rows, wide), BF),
            pltpu.VMEM((count_d, rows, wide), BF),
            pltpu.VMEM((count_d - 1, rows, wide), BF),
            pltpu.VMEM((count_d - 1, rows, early.shape[2]), BF),
            pltpu.VMEM((rows, early.shape[2]), BF),
            pltpu.VMEM((width, count * own), BF),
            pltpu.VMEM(dq.shape, BF),
            pltpu.SemaphoreType.DMA((2 + count,)),
            pltpu.VMEM((width, kv_rows), F32),
            pltpu.VMEM((1, width), F32),
            pltpu.VMEM((width, narrow), BF),
            pltpu.VMEM((width, narrow), BF),
            pltpu.VMEM((count_s, count_d * rows, narrow), BF),
            pltpu.VMEM((count_s - 1, count_d * rows, narrow), BF),
            pltpu.VMEM((count_d, rows, narrow), BF),
            pltpu.VMEM((count_d - 1, rows, narrow), BF),
            pltpu.SemaphoreType.DMA((slots,)),
            pltpu.SemaphoreType.DMA((slots,)),
        ],
        compiler_params=pltpu.CompilerParams(
            vmem_limit_bytes=56 * MIB, collective_id=1, has_side_effects=True
        ),
        cost_estimate=cost(10**8),
        name="tail",
    )(x, dq, nt, *fixed, nt, dq, early, *near_all, *shares)


def turn_tables(cosine, sine_table):
    plain = HD - RD
    one = jnp.ones((cosine.shape[0], plain), F32)
    none = jnp.zeros_like(one)
    quiet = jnp.zeros_like(sine_table)
    straight = jnp.concatenate([one, cosine, cosine], axis=1)
    ahead = jnp.concatenate([none, sine_table, quiet], axis=1)
    behind = jnp.concatenate([none, quiet, -sine_table], axis=1)
    tables = jnp.stack([jnp.concatenate([t, t], axis=1) for t in (straight, ahead, behind)])
    return tables * HD ** (-0.5)


def after(value, *others):
    return lax.optimization_barrier((value, *others))[0]


def on_device_fast(
    inputs, gain_one, w_query, w_tied, w_rope, w_out, gain_two, w_gate, w_up, w_down,
    doc_starts, out_grad,
):
    count, own, width = inputs.shape
    cores = lax.axis_size("mp")
    groups = cores * w_tied.shape[1] // HD
    all_heads = cores * w_query.shape[1] // HD
    heads = all_heads // groups
    mp_index = lax.axis_index("mp")
    split = (lax.axis_size("dp"), lax.axis_size("seq"))
    tied_other, query_other = swap_cores(w_tied), swap_cores(w_query)
    down_other = swap_cores(w_down)
    gain_one_float = gain_one.astype(F32)[None]
    gain_two_float = gain_two.astype(F32)[None]
    cosine, sine_table = rope_tables(my_chunk() * own, own, RD)
    cosine_t, sine_t = cosine.T, sine_table.T
    half = count // 2
    kv, normed_t, q, slopes, queries_weights, keys_weights, kv_near, kv_far = project(
        inputs, out_grad, gain_one_float, (w_query, query_other), (w_tied, tied_other), w_rope,
        (w_down, down_other), cosine_t, sine_t, half,
    )
    kv_late = send_near(kv)
    out_other = swap_cores(after(w_out, kv))
    gate_other, up_other = swap_cores(after(w_gate, kv)), swap_cores(after(w_up, kv))
    span = half - half // 4
    made = attend_forward(doc_starts, q, [kv_near, kv_far], groups, heads, 0, span, 0, ())
    kv_late = send_far([after(part, *made) for part in kv_late])
    made = attend_forward(
        doc_starts, q, [kv_near, kv_far], groups, heads, span, half - span, span, made
    )
    heads_out, lse = attend_forward(doc_starts, q, kv_late, groups, heads, half, half, 0, made)
    out_both = by_core(w_out, after(out_other, lse), 0)
    (
        outputs, normed_two_t, out_grad_t, active, grad_gate, grad_up, grad_hidden, grad_attended_t,
        grad_heads, delta, grad_gain_two,
    ) = feed(
        inputs, out_grad, slopes, heads_out, gain_two_float, out_both, (w_gate, gate_other),
        (w_up, up_other), (w_down, down_other),
    )
    units, head_half = w_gate.shape[1], w_out.shape[0]
    first_sum, rest_sum = early_grads(
        normed_two_t, grad_gate, grad_up, active, out_grad_t, grad_attended_t, heads_out, split
    )
    first_sum, rest_sum, grad_heads = lax.optimization_barrier((first_sum, rest_sum, grad_heads))
    first_sum = lax.psum_scatter(first_sum, "seq", scatter_dimension=0, tiled=True)

    turns = turn_tables(cosine, sine_table)
    quarter = half // 2
    backward = [
        (half, half, kv_late, 0),
        (quarter, half - quarter, [kv_near, kv_far], quarter),
        (0, quarter, [kv_near, kv_far], 0),
    ]
    rest_sum = rest_sum.reshape(split[1], split[0], -1, rest_sum.shape[1])
    rest_sum = add_up(send_steps(rest_sum, "dp", 1)).astype(BF)
    rest_terms = send_steps(rest_sum, "seq", 0)
    dq, near, shares = (), [], []
    for part, (at, size, kv_part, kv_at) in enumerate(backward):
        need = near[0][:1] if part == 2 else []
        made_dq, keep, give = attend_backward(
            doc_starts, after(q, *need), grad_heads, lse, delta, turns, kv_part, groups, heads, at,
            size, kv_at, dq,
        )
        dq = (made_dq,)
        if part == 0:
            first_shares = (keep, swap_cores(after(give, rest_sum)))
        if part == 1:
            give = after(give, *rest_terms)
            near.append(send_keys(join_cores(*first_shares)))
            shares = [keep, swap_cores(give)]
        if part == 2:
            shares += [keep, give]
    early = first_sum.reshape(split[0], -1, first_sum.shape[1])
    order = [span[:2] for span in backward]
    update, query_sum, small_sum, first_sum = tail(
        order, inputs, dq[0], normed_t, gain_one_float, queries_weights, keys_weights,
        cosine_t, sine_t, grad_gain_two, early, near,
        shares,
    )
    grad_inputs = grad_hidden.astype(F32) + update.astype(F32)
    half_tied = groups * HD // cores
    late_sum, small_sum = small_sum[:, :half_tied], small_sum[:, half_tied:]
    rows = small_sum.shape[0] // cores
    small_sum = lax.dynamic_slice_in_dim(small_sum, mp_index * rows, rows, 0)
    pairs = first_sum[:, : 2 * units].reshape(first_sum.shape[0], units // LANE, 2, LANE)
    gate_sum = pairs[:, :, 0].reshape(-1, units)
    up_sum = pairs[:, :, 1].reshape(-1, units)
    out_sum = first_sum[:, 2 * units : 2 * units + head_half]
    down_sum = jnp.concatenate([first_sum[:, 2 * units + head_half :], add_up(rest_terms)], axis=1)
    return (
        outputs,
        grad_inputs,
        small_sum[:, RD],
        query_sum,
        late_sum,
        small_sum[:, :RD],
        out_sum.T,
        small_sum[:, RD + 1],
        gate_sum,
        up_sum,
        down_sum.T,
    )


def solution(mesh):
    in_specs = (
        P("dp", ("seq", "mp"), None),
        P(),
        P(None, "mp"),
        P(None, "mp"),
        P(),
        P("mp", None),
        P(),
        P(None, "mp"),
        P(None, "mp"),
        P("mp", None),
        P("dp", None),
        P("dp", ("seq", "mp"), None),
    )
    out_specs = (
        P("dp", ("seq", "mp"), None),
        P("dp", ("seq", "mp"), None),
        P(("dp", "seq", "mp")),
        P(("dp", "seq"), "mp"),
        P(("dp", "seq"), "mp"),
        P(("dp", "seq", "mp"), None),
        P("mp", ("dp", "seq")),
        P(("dp", "seq", "mp")),
        P(("dp", "seq"), "mp"),
        P(("dp", "seq"), "mp"),
        P("mp", ("dp", "seq")),
    )

    def local(inputs, *rest):
        step = on_device_fast if inputs.shape[1] % (2 * LANE) == 0 else on_device
        return step(inputs, *rest)

    return jax.shard_map(
        local, mesh=mesh, in_specs=in_specs, out_specs=out_specs, check_vma=False
    )
```

```python
import functools

import jax
import jax.numpy as jnp
from jax import lax
from jax.experimental import pallas as pl
from jax.experimental.pallas import tpu as pltpu
from jax.sharding import PartitionSpec as P

HD = 64
RD = 32


epsilon = 1e-05
rope_base = 10000.0
masked_value = -1e30


def rope_tables(offset, count, rope_width):
    position = (offset + jnp.arange(count, dtype=jnp.int32)).astype(jnp.float32)
    frequency = rope_base ** (-jnp.arange(rope_width // 2, dtype=jnp.float32) * 2.0 / rope_width)
    angles = position[:, None] * frequency[None, :]
    return (jnp.cos(angles), jnp.sin(angles))


def rotate(values, cosine, sine_table):
    half_width = values.shape[-1] // 2
    first_half = values[..., :half_width]
    second_half = values[..., half_width:]
    return jnp.concatenate(
        [
            first_half * cosine - second_half * sine_table,
            second_half * cosine + first_half * sine_table,
        ],
        axis=-1,
    )


def rotate_back(grads, cosine, sine_table):
    half_width = grads.shape[-1] // 2
    first_half = grads[..., :half_width]
    second_half = grads[..., half_width:]
    return jnp.concatenate(
        [
            first_half * cosine + second_half * sine_table,
            second_half * cosine - first_half * sine_table,
        ],
        axis=-1,
    )


def contract_rows(left, right):
    return lax.dot_general(
        left, right, (((0,), (0,)), ((), ())), preferred_element_type=jnp.float32
    )


def times_transposed(left, right):
    return lax.dot_general(
        left, right, (((1,), (1,)), ((), ())), preferred_element_type=jnp.float32
    )


def norm_back(grad_normed, values, inverse, gain):
    scaled = grad_normed * gain
    grad_gain = jnp.sum(grad_normed * values * inverse, axis=(0, 1))
    grad_values = inverse * scaled - values * inverse**3 * jnp.mean(
        scaled * values, axis=-1, keepdims=True
    )
    return (grad_values, grad_gain)


def attend(operands):
    queries, key_full, values, allowed = operands
    scores = jnp.einsum(
        "qghd,kgd->ghqk", queries, key_full, preferred_element_type=jnp.float32
    ) * HD ** (-0.5)
    masked = jnp.where(allowed[None, None], scores, masked_value)
    row_max = jnp.max(masked, axis=-1, keepdims=True)
    weights = jnp.exp(masked - row_max)
    row_total = jnp.sum(weights, axis=-1, keepdims=True)
    attention_probs = (weights / row_total).astype(jnp.bfloat16)
    combined = jnp.einsum(
        "ghqk,kgd->qghd", attention_probs, values, preferred_element_type=jnp.float32
    )
    return (combined.astype(jnp.bfloat16), row_max + jnp.log(row_total))


def attend_back(operands):
    queries, key_full, values, allowed, log_total, grad_heads = operands
    score_scale = HD ** (-0.5)
    plain_width = HD - RD
    scores = (
        jnp.einsum("qghd,kgd->ghqk", queries, key_full, preferred_element_type=jnp.float32)
        * score_scale
    )
    masked = jnp.where(allowed[None, None], scores, masked_value)
    probs_float = jnp.exp(masked - log_total)
    grad_probs = jnp.einsum(
        "qghd,kgd->ghqk", grad_heads, values, preferred_element_type=jnp.float32
    )
    row_delta = jnp.sum(probs_float * grad_probs, axis=-1, keepdims=True)
    grad_scores = (probs_float * (grad_probs - row_delta)).astype(jnp.bfloat16)
    grad_queries = (
        jnp.einsum("ghqk,kgd->qghd", grad_scores, key_full, preferred_element_type=jnp.float32)
        * score_scale
    )
    grad_keys = (
        jnp.einsum("ghqk,qghd->kgd", grad_scores, queries, preferred_element_type=jnp.float32)
        * score_scale
    )
    grad_values = jnp.einsum(
        "ghqk,qghd->kgd",
        probs_float.astype(jnp.bfloat16),
        grad_heads,
        preferred_element_type=jnp.float32,
    )
    grad_tied = grad_values + jnp.concatenate(
        [grad_keys[..., :plain_width], jnp.zeros_like(grad_keys[..., plain_width:])], axis=-1
    )
    grad_rope = jnp.sum(grad_keys[..., plain_width:], axis=1)
    return (grad_queries, grad_tied, grad_rope)


def on_device(
    inputs,
    gain_one,
    w_query,
    w_tied,
    w_rope,
    w_out,
    gain_two,
    w_gate,
    w_up,
    w_down,
    doc_starts,
    out_grad,
):
    seq_count, own_count, model_width = inputs.shape
    plain_width = HD - RD
    group_local = w_tied.shape[1] // HD
    head_local = w_query.shape[1] // HD
    seq_index = lax.axis_index("seq")
    mp_index = lax.axis_index("mp")
    gain_one_float = gain_one.astype(jnp.float32)
    gain_two_float = gain_two.astype(jnp.float32)
    inputs_float = inputs.astype(jnp.float32)
    inverse_one = lax.rsqrt(jnp.mean(inputs_float * inputs_float, axis=-1, keepdims=True) + epsilon)
    normed_one = (inputs_float * inverse_one * gain_one_float).astype(jnp.bfloat16)
    gathered_one = lax.all_gather(normed_one, "mp", axis=1, tiled=True)
    context = gathered_one.shape[1]
    token_count = seq_count * context
    flat_one = gathered_one.reshape(token_count, model_width)
    offset = seq_index * context
    cosine, sine_table = rope_tables(offset, context, RD)
    query_lin = jnp.dot(flat_one, w_query, preferred_element_type=jnp.float32).reshape(
        seq_count, context, head_local, HD
    )
    queries = jnp.concatenate(
        [
            query_lin[..., :plain_width],
            rotate(
                query_lin[..., plain_width:], cosine[None, :, None, :], sine_table[None, :, None, :]
            ),
        ],
        axis=-1,
    ).astype(jnp.bfloat16)
    queries = queries.reshape(seq_count, context, group_local, head_local // group_local, HD)
    tied_state = (
        jnp.dot(flat_one, w_tied, preferred_element_type=jnp.float32)
        .astype(jnp.bfloat16)
        .reshape(seq_count, context, group_local * HD)
    )
    rope_lin = jnp.dot(flat_one, w_rope, preferred_element_type=jnp.float32).reshape(
        seq_count, context, RD
    )
    rope_keys = rotate(rope_lin, cosine[None], sine_table[None]).astype(jnp.bfloat16)
    tied_all, rope_all = (
        lax.all_gather(tied_state, "seq", axis=1, tiled=True),
        lax.all_gather(rope_keys, "seq", axis=1, tiled=True),
    )
    length = tied_all.shape[1]
    values_all = tied_all.reshape(seq_count, length, group_local, HD)
    key_full = jnp.concatenate(
        [
            values_all[..., :plain_width],
            jnp.broadcast_to(rope_all[:, :, None, :], (seq_count, length, group_local, RD)),
        ],
        axis=-1,
    )
    key_position = jnp.arange(length, dtype=jnp.int32)
    key_segment = jnp.sum(
        (doc_starts[:, None, :] <= key_position[None, :, None]).astype(jnp.int32), axis=-1
    )
    query_segment = lax.dynamic_slice_in_dim(key_segment, offset, context, 1)
    query_position = offset + jnp.arange(context, dtype=jnp.int32)
    allowed = (query_segment[:, :, None] == key_segment[:, None, :]) & (
        query_position[:, None] >= key_position[None, :]
    )[None]
    head_outputs, log_total = lax.map(attend, (queries, key_full, values_all, allowed))
    flat_heads = head_outputs.reshape(token_count, head_local * HD)
    attended_part = jnp.dot(flat_heads, w_out, preferred_element_type=jnp.float32).reshape(
        seq_count, context, model_width
    )
    attended = lax.psum_scatter(
        attended_part.astype(jnp.bfloat16), "mp", scatter_dimension=1, tiled=True
    ).astype(jnp.float32)
    hidden = inputs_float + attended
    inverse_two = lax.rsqrt(jnp.mean(hidden * hidden, axis=-1, keepdims=True) + epsilon)
    normed_two = (hidden * inverse_two * gain_two_float).astype(jnp.bfloat16)
    gathered_two = lax.all_gather(normed_two, "mp", axis=1, tiled=True)
    flat_two = gathered_two.reshape(token_count, model_width)
    gate_values = jnp.dot(flat_two, w_gate, preferred_element_type=jnp.float32)
    up_values = jnp.dot(flat_two, w_up, preferred_element_type=jnp.float32)
    sigmoid_gate = jax.nn.sigmoid(gate_values)
    silu_gate = gate_values * sigmoid_gate
    active = (silu_gate * up_values).astype(jnp.bfloat16)
    result_part = jnp.dot(active, w_down, preferred_element_type=jnp.float32).reshape(
        seq_count, context, model_width
    )
    result = lax.psum_scatter(
        result_part.astype(jnp.bfloat16), "mp", scatter_dimension=1, tiled=True
    ).astype(jnp.float32)
    outputs = (hidden + result).astype(jnp.bfloat16)
    grad_out_all = lax.all_gather(out_grad, "mp", axis=1, tiled=True)
    flat_grad = grad_out_all.reshape(token_count, model_width)
    grad_active = times_transposed(flat_grad, w_down)
    grad_w_down = contract_rows(active, flat_grad)
    grad_gate = (
        grad_active * up_values * sigmoid_gate * (1.0 + gate_values * (1.0 - sigmoid_gate))
    ).astype(jnp.bfloat16)
    grad_up = (grad_active * silu_gate).astype(jnp.bfloat16)
    grad_w_gate = contract_rows(flat_two, grad_gate)
    grad_w_up = contract_rows(flat_two, grad_up)
    grad_two_part = (times_transposed(grad_gate, w_gate) + times_transposed(grad_up, w_up)).reshape(
        seq_count, context, model_width
    )
    grad_normed_two = lax.psum_scatter(
        grad_two_part.astype(jnp.bfloat16), "mp", scatter_dimension=1, tiled=True
    ).astype(jnp.float32)
    grad_hidden_norm, grad_gain_two = norm_back(
        grad_normed_two, hidden, inverse_two, gain_two_float
    )
    grad_hidden = out_grad.astype(jnp.float32) + grad_hidden_norm
    grad_attended_all = lax.all_gather(grad_hidden.astype(jnp.bfloat16), "mp", axis=1, tiled=True)
    flat_attended = grad_attended_all.reshape(token_count, model_width)
    grad_w_out = contract_rows(flat_heads, flat_attended)
    grad_heads = times_transposed(flat_attended, w_out).astype(jnp.bfloat16).reshape(queries.shape)
    grad_queries, grad_tied, grad_rope = lax.map(
        attend_back, (queries, key_full, values_all, allowed, log_total, grad_heads)
    )
    grad_queries = grad_queries.reshape(seq_count, context, head_local, HD)
    grad_query_lin = (
        jnp.concatenate(
            [
                grad_queries[..., :plain_width],
                rotate_back(
                    grad_queries[..., plain_width:],
                    cosine[None, :, None, :],
                    sine_table[None, :, None, :],
                ),
            ],
            axis=-1,
        )
        .astype(jnp.bfloat16)
        .reshape(token_count, head_local * HD)
    )
    tied_own, rope_context = (
        lax.psum_scatter(
            grad_tied.reshape(seq_count, length, group_local * HD).astype(jnp.bfloat16),
            "seq",
            scatter_dimension=1,
            tiled=True,
        ).astype(jnp.float32),
        lax.psum_scatter(
            grad_rope.astype(jnp.bfloat16), "seq", scatter_dimension=1, tiled=True
        ).astype(jnp.float32),
    )
    grad_tied_flat = tied_own.astype(jnp.bfloat16).reshape(token_count, group_local * HD)
    grad_one_part = (
        times_transposed(grad_query_lin, w_query) + times_transposed(grad_tied_flat, w_tied)
    ).reshape(seq_count, context, model_width)
    grad_normed_one, rope_own = (
        lax.psum_scatter(
            grad_one_part.astype(jnp.bfloat16), "mp", scatter_dimension=1, tiled=True
        ).astype(jnp.float32),
        lax.psum_scatter(
            rope_context.astype(jnp.bfloat16), "mp", scatter_dimension=1, tiled=True
        ).astype(jnp.float32),
    )
    own_offset = offset + mp_index * own_count
    cosine_own, sine_own = rope_tables(own_offset, own_count, RD)
    grad_rope_flat = (
        rotate_back(rope_own, cosine_own[None], sine_own[None])
        .astype(jnp.bfloat16)
        .reshape(seq_count * own_count, RD)
    )
    grad_normed_one = grad_normed_one + times_transposed(grad_rope_flat, w_rope).reshape(
        seq_count, own_count, model_width
    )
    grad_w_rope = contract_rows(
        normed_one.reshape(seq_count * own_count, model_width), grad_rope_flat
    )
    grad_w_query = contract_rows(flat_one, grad_query_lin)
    grad_w_tied = contract_rows(flat_one, grad_tied_flat)
    grad_inputs_norm, grad_gain_one = norm_back(
        grad_normed_one, inputs_float, inverse_one, gain_one_float
    )
    grad_inputs = grad_hidden + grad_inputs_norm
    small_sums = (
        lax.psum_scatter(grad_gain_one, ("dp", "seq", "mp"), scatter_dimension=0, tiled=True),
        lax.psum_scatter(grad_w_rope, ("dp", "seq", "mp"), scatter_dimension=0, tiled=True),
        lax.psum_scatter(grad_gain_two, ("dp", "seq", "mp"), scatter_dimension=0, tiled=True),
    )
    weight_terms = (grad_w_query, grad_w_tied, grad_w_out, grad_w_gate, grad_w_up, grad_w_down)
    weight_sums = (
        lax.psum_scatter(weight_terms[0], ("dp", "seq"), scatter_dimension=0, tiled=True),
        lax.psum_scatter(weight_terms[1], ("dp", "seq"), scatter_dimension=0, tiled=True),
        lax.psum_scatter(weight_terms[2], ("dp", "seq"), scatter_dimension=1, tiled=True),
        lax.psum_scatter(weight_terms[3], ("dp", "seq"), scatter_dimension=0, tiled=True),
        lax.psum_scatter(weight_terms[4], ("dp", "seq"), scatter_dimension=0, tiled=True),
        lax.psum_scatter(weight_terms[5], ("dp", "seq"), scatter_dimension=1, tiled=True),
    )
    return (
        outputs,
        grad_inputs,
        small_sums[0],
        weight_sums[0],
        weight_sums[1],
        small_sums[1],
        weight_sums[2],
        small_sums[2],
        weight_sums[3],
        weight_sums[4],
        weight_sums[5],
    )


BF = jnp.bfloat16
F32 = jnp.float32
NN = (((1,), (0,)), ((), ()))
NT = (((1,), (1,)), ((), ()))
TN = (((0,), (0,)), ((), ()))
BIG = 2.0**100
MIB = 1 << 20
LANE = 128


def mxu(left, right, dims):
    return lax.dot_general(left, right, dims, preferred_element_type=F32)


def params(limit=56):
    return pltpu.CompilerParams(vmem_limit_bytes=limit * MIB)


def cost(flops, moved=0):
    return pl.CostEstimate(flops=int(flops), bytes_accessed=int(moved), transcendentals=0)


def swap_cores(value):
    return lax.ppermute(value, "mp", [(0, 1), (1, 0)])


def shift(value, axis, by):
    size = lax.axis_size(axis)
    return lax.ppermute(value, axis, [(i, (i + by) % size) for i in range(size)])


def send_near(kv):
    return [kv] + [shift(kv, "seq", k) for k in range(1, lax.axis_size("seq"))]


def send_far(near):
    return [part[None] for part in near + [swap_cores(value) for value in near]]


def pick(value, index, axis):
    return lax.dynamic_index_in_dim(value, index, axis, keepdims=False)


def send_steps(value, axis, dim):
    size, me = lax.axis_size(axis), lax.axis_index(axis)
    terms = [pick(value, me, dim)]
    for k in range(1, size):
        terms.append(shift(pick(value, (me + k) % size, dim), axis, k))
    return terms


def add_up(terms):
    total = terms[0].astype(F32)
    for term in terms[1:]:
        total = total + term.astype(F32)
    return total


def by_core(own, other, axis):
    first = lax.axis_index("mp") == 0
    return jnp.concatenate(
        [jnp.where(first, own, other), jnp.where(first, other, own)], axis=axis
    )


def rotate_rows(values, cosine, sine_table):
    half = values.shape[0] // 2
    a, b = values[:half], values[half:]
    return jnp.concatenate([a * cosine - b * sine_table, b * cosine + a * sine_table], axis=0)


def project_kernel(
    sent, x_ref, og_ref, gain_ref, wqo_ref, wqp_ref, wto_ref, wtp_ref, wr_ref, wdo_ref, wdp_ref,
    cos_ref, sin_ref, kv_ref, nt_ref, q_ref, ga_ref, wq_ref, wkv_ref, near_ref, far_ref,
    kept, wd, load_sems, own_sems, sends, receives,
):
    b = pl.program_id(0)
    count_s = lax.axis_size("seq")
    me_s, core = lax.axis_index("seq"), lax.axis_index("mp")
    peers = [{"seq": lax.rem(me_s + k, count_s)} for k in range(1, count_s)]
    other_core = {"mp": 1 - core}
    near, forward = [], []
    slots = iter(range(sends.shape[0]))

    def link(source, target, peer):
        slot = next(slots)
        return pltpu.make_async_remote_copy(
            src_ref=source,
            dst_ref=target,
            send_sem=sends.at[slot],
            recv_sem=receives.at[slot],
            device_id=peer,
            device_id_type=pl.DeviceIdType.MESH,
        )

    for i in range(sent):
        near.append([link(kept.at[i], near_ref.at[k, i], peers[k - 1]) for k in range(1, count_s)])
        forward.append(
            [link(kept.at[i], far_ref.at[0, i], other_core)]
            + [link(near_ref.at[k, i], far_ref.at[k, i], other_core) for k in range(1, count_s)]
        )
    own = [pltpu.make_async_copy(kept.at[i], near_ref.at[0, i], own_sems.at[i]) for i in range(sent)]
    loads = load_weights([(wdo_ref, 0, 0), (wdp_ref, 1, 0)], [wd, wd], load_sems)

    @pl.when(b == 0)
    def _():
        for copy in loads:
            copy.start()
        barrier = pltpu.get_barrier_semaphore()
        for peer in [other_core] + peers:
            pl.semaphore_signal(barrier, inc=1, device_id=peer, device_id_type=pl.DeviceIdType.MESH)
        pl.semaphore_wait(barrier, count_s)

        def turn(source, target, at):
            size = source.shape[1]
            row = lax.broadcasted_iota(jnp.int32, (size, size), 0)
            column = lax.broadcasted_iota(jnp.int32, (size, size), 1)
            identity = jnp.where(row == column, 1.0, 0.0).astype(BF)
            target[pl.ds(at, size)] = mxu(identity, source[...], NT).astype(BF)

        for pair, target in (((wto_ref, wtp_ref), wkv_ref), ((wqo_ref, wqp_ref), wq_ref)):
            size = pair[0].shape[1]
            for side, source in enumerate(pair):
                place = jnp.where(core == side, 0, 1)
                turn(source, target, pl.multiple_of(place * size, size))
        turn(wr_ref, wkv_ref, wkv_ref.shape[0] - RD)
        for copy in loads:
            copy.wait()

    x = x_ref[0].astype(F32)
    inverse = lax.rsqrt(jnp.mean(x * x, axis=-1, keepdims=True) + epsilon)
    normed = (x * inverse * gain_ref[...]).astype(BF)
    lin = mxu(wkv_ref[...], normed, NT)
    tied = wkv_ref.shape[0] - RD
    cosine, sine_table = cos_ref[...], sin_ref[...]
    rope = rotate_rows(lin[tied:], cosine, sine_table)
    keys = jnp.concatenate([lin[:tied], rope], axis=0).astype(BF)
    @pl.when(b >= sent)
    def _():
        kv_ref[0] = keys

    for i in range(sent):

        @pl.when(b == i)
        def _():
            kept[i] = keys
            for copy in near[i]:
                copy.start()
            forward[i][0].start()
            own[i].start()

    nt_ref[0] = normed.T
    lin = mxu(wq_ref[...], normed, NT)
    plain = HD - RD
    pieces = []
    for at in range(0, lin.shape[0], HD):
        pieces.append(lin[at : at + plain])
        pieces.append(rotate_rows(lin[at + plain : at + HD], cosine, sine_table))
    queries = jnp.concatenate(pieces, axis=0)
    q_ref[0] = (queries.astype(BF) * HD ** (-0.5)).astype(BF)

    og = og_ref[0]
    for at in range(0, wd.shape[0], 2 * LANE):
        to = slice(at, at + 2 * LANE)
        ga_ref[:, to] = mxu(og, wd[to], NT).astype(BF)

    steps = pl.num_programs(0)
    for i in range(sent):

        @pl.when(b == steps - sent + i)
        def _():
            for copy in near[i]:
                copy.wait()
            for copy in forward[i][1:]:
                copy.start()

    @pl.when(b == steps - 1)
    def _():
        for i in range(sent):
            own[i].wait()
            for copy in forward[i]:
                copy.wait()


def project(x, og, gain, wq, wt, wr, wd, cosine, sine_table, sent):
    count, own, width = x.shape
    rows, half = 2 * wq[0].shape[1], wd[0].shape[0]
    kv_rows = 2 * wt[0].shape[1] + wr.shape[1]
    weights = [*wq, *wt, wr]
    count_s = lax.axis_size("seq")
    whole = lambda array: pl.BlockSpec(array.shape, lambda b: (0, 0))
    seq = pl.BlockSpec((1, own, width), lambda b: (b, 0, 0))
    hbm = pl.BlockSpec(memory_space=pl.ANY)
    gathered = jax.ShapeDtypeStruct((count_s, sent, kv_rows, own), BF)
    links = sent * (2 * count_s - 1)
    return pl.pallas_call(
        functools.partial(project_kernel, sent),
        grid=(count,),
        in_specs=[
            seq, seq, whole(gain), *[whole(part) for part in weights], hbm, hbm, whole(cosine),
            whole(cosine),
        ],
        out_specs=[
            pl.BlockSpec((1, kv_rows, own), lambda b: (jnp.maximum(b - sent, 0), 0, 0)),
            pl.BlockSpec((1, width, own), lambda b: (b, 0, 0)),
            pl.BlockSpec((1, rows, own), lambda b: (b, 0, 0)),
            pl.BlockSpec((own, 2 * half), lambda b: (b, 0)),
            pl.BlockSpec((rows, width), lambda b: (0, 0)),
            pl.BlockSpec((kv_rows, width), lambda b: (0, 0)),
            hbm,
            hbm,
        ],
        out_shape=[
            jax.ShapeDtypeStruct((count - sent, kv_rows, own), BF),
            jax.ShapeDtypeStruct((count, width, own), BF),
            jax.ShapeDtypeStruct((count, rows, own), BF),
            jax.ShapeDtypeStruct((count * own, 2 * half), BF),
            jax.ShapeDtypeStruct((rows, width), BF),
            jax.ShapeDtypeStruct((kv_rows, width), BF),
            gathered,
            gathered,
        ],
        scratch_shapes=[
            pltpu.VMEM((sent, kv_rows, own), BF),
            pltpu.VMEM((2 * half, width), BF),
            pltpu.SemaphoreType.DMA((2 * (half // LANE),)),
            pltpu.SemaphoreType.DMA((sent,)),
            pltpu.SemaphoreType.DMA((links,)),
            pltpu.SemaphoreType.DMA((links,)),
        ],
        compiler_params=pltpu.CompilerParams(
            vmem_limit_bytes=56 * MIB, collective_id=2, has_side_effects=True
        ),
        cost_estimate=cost(3 * 10**10),
        name="project",
    )(x, og, gain, *weights, *wd, cosine, sine_table)


def segment_counts(starts, first, width):
    position = first + lax.broadcasted_iota(jnp.int32, (1, width), 1)
    count = jnp.zeros((1, width), jnp.int32)
    for start in starts:
        count = count + (start <= position).astype(jnp.int32)
    return count


def query_rows(starts, first, width):
    row = lax.broadcasted_iota(jnp.int32, (16, width), 0)
    match = segment_counts(starts, first, width) == row + 1
    return jnp.where(match, 1.0, 0.0).astype(BF)


def key_rows(starts, first, width):
    row = lax.broadcasted_iota(jnp.int32, (16, width), 0)
    match = (segment_counts(starts, first, width) == row + 1) | (row >= len(starts))
    return jnp.where(match, 0.0, -BIG).astype(BF)


def first_rows(count, width):
    row = lax.broadcasted_iota(jnp.int32, (16, width), 0)
    return jnp.where(row < count, 1.0, 0.0).astype(BF)


def three_parts(row, width):
    high = row.astype(BF)
    rest = row - high.astype(F32)
    middle = rest.astype(BF)
    low = (rest - middle.astype(F32)).astype(BF)
    at = lax.broadcasted_iota(jnp.int32, (16, width), 0)
    parts = jnp.where(at == 0, high.astype(F32), 0.0)
    parts = jnp.where(at == 1, middle.astype(F32), parts)
    return jnp.where(at == 2, low.astype(F32), parts).astype(BF)


def start_chunk(starts, first, chunk):
    begin = jnp.int32(0)
    for start in starts:
        begin = jnp.where(start <= first, jnp.maximum(begin, start), begin)
    return begin // chunk


def my_chunk():
    return lax.axis_index("seq") * lax.axis_size("mp") + lax.axis_index("mp")


def place_keys(refs, kv, begin, me):
    steps = lax.axis_size("seq")
    seq, core = lax.axis_index("seq"), lax.axis_index("mp")
    places = [(ref, i) for ref in refs for i in range(ref.shape[0])]
    for at, (ref, i) in enumerate(places):
        of = core if at < steps else 1 - core
        j = lax.rem(seq - at % steps + steps, steps) * 2 + of

        @pl.when((j >= begin) & (j <= me))
        def _():
            kv[j] = ref[i, 0]


def stack_heads(value, at, heads, rows=HD):
    half = value.shape[1] // 2
    return jnp.concatenate(
        [
            value[at + h * rows : at + (h + 1) * rows, s * half : (s + 1) * half]
            for s in range(2)
            for h in range(heads)
        ],
        axis=1,
    )


def stack_queries(starts, first, half, heads):
    return jnp.concatenate(
        [query_rows(starts, first + s * half, half) for s in range(2) for _ in range(heads)], axis=1
    )


def attend_kernel(groups, heads, first, inputs, docs_ref, q_ref, *refs):
    kv_refs = refs[:inputs]
    out_ref, lse_ref, kv_ref, qa, acc, top = refs[-6:]
    b = pl.program_id(0) + first
    own = q_ref.shape[2]
    ndoc = docs_ref.shape[1]
    starts = [docs_ref[b, k] for k in range(ndoc)]
    me = my_chunk()
    begin = start_chunk(starts, me * own, own)
    half = own // 2
    begin_second = start_chunk(starts, me * own + half, own)
    place_keys(kv_refs, kv_ref, begin, me)
    wide = heads * own
    first_half = wide // 2
    tied = groups * HD
    plain = HD - RD
    q_doc = stack_queries(starts, me * own, half, heads)
    q_all = q_ref[0]
    for g in range(groups):
        qa[g, :HD] = stack_heads(q_all, g * heads * HD, heads)
        qa[g, HD : HD + 16] = q_doc
        qa[g, HD + 16 :] = jnp.zeros((LANE - HD - 16, wide), BF)
    ones = first_rows(1, own)
    zeros = jnp.zeros((LANE - HD - 16, own), BF)

    def keys_of(j, g):
        doc = key_rows(starts, j * own, own)
        block = jnp.concatenate(
            [
                kv_ref[j, g * HD : g * HD + plain],
                kv_ref[j, tied : tied + RD],
                doc,
                zeros,
            ],
            axis=0,
        )
        return block.T

    def values_of(j, g):
        return jnp.concatenate([kv_ref[j, g * HD : (g + 1) * HD], ones], axis=0)

    key_at = lax.broadcasted_iota(jnp.int32, (own, half), 0)
    query_at = lax.broadcasted_iota(jnp.int32, (own, half), 1)
    causal = jnp.concatenate(
        [key_at <= query_at + s * half for s in range(2) for _ in range(heads)], axis=1
    )

    def block(j, lanes, diagonal=False):
        def logits_of(g):
            return mxu(keys_of(j, g), qa[g, :, lanes], NN)

        following = logits_of(0)
        for g in range(groups):
            logits = following
            if g + 1 < groups:
                following = logits_of(g + 1)
            if diagonal:
                logits = jnp.where(causal, logits, masked_value)
            peak = jnp.max(logits, axis=0, keepdims=True)
            if not diagonal:
                old = top[g, :, lanes]
                peak = jnp.maximum(old, peak)
            weights = jnp.exp(logits - peak).astype(BF)
            added = mxu(values_of(j, g), weights, NN)
            if not diagonal:
                added = acc[g, :, lanes] * jnp.exp(old - peak) + added
            acc[g, :, lanes] = added
            top[g, :, lanes] = peak

    block(me, slice(0, wide), True)

    def both(i, carry):
        block(me - 1 - i, slice(0, wide))
        return carry

    def first_only(i, carry):
        block(begin_second - 1 - i, slice(0, first_half))
        return carry

    lax.fori_loop(0, me - begin_second, both, 0)
    lax.fori_loop(0, begin_second - begin, first_only, 0)
    for g in range(groups):
        total = acc[g, HD : HD + 1]
        result = acc[g, :HD] / total
        lse_ref[0, g : g + 1] = top[g] + jnp.log(total)
        for s in range(2):
            for h in range(heads):
                at, of = (g * heads + h) * HD, (s * heads + h) * half
                out_ref[0, at : at + HD, s * half : (s + 1) * half] = result[:, of : of + half].astype(BF)


def kv_specs(kv, kv_at):
    return [
        pl.BlockSpec((part.shape[0], 1, *part.shape[2:]), lambda b: (0, b + kv_at, 0, 0))
        for part in kv
    ]


def attend_forward(docs, q, kv, groups, heads, first, size, kv_at, into):
    kv_rows, own = kv[0].shape[2:]
    count, chunks, inputs = docs.shape[0], 2 * lax.axis_size("seq"), len(kv)
    wide = heads * own
    hbm = pl.BlockSpec(memory_space=pl.ANY)
    return pl.pallas_call(
        functools.partial(attend_kernel, groups, heads, first, inputs),
        grid=(size,),
        in_specs=[
            pl.BlockSpec(memory_space=pltpu.SMEM),
            pl.BlockSpec((1, q.shape[1], own), lambda b: (b + first, 0, 0)),
        ]
        + kv_specs(kv, kv_at)
        + [hbm] * len(into),
        out_specs=[
            pl.BlockSpec((1, q.shape[1], own), lambda b: (b + first, 0, 0)),
            pl.BlockSpec((1, groups, wide), lambda b: (b + first, 0, 0)),
        ],
        out_shape=[
            jax.ShapeDtypeStruct(q.shape, BF),
            jax.ShapeDtypeStruct((count, groups, wide), F32),
        ],
        scratch_shapes=[
            pltpu.VMEM((chunks, kv_rows, own), BF),
            pltpu.VMEM((groups, LANE, wide), BF),
            pltpu.VMEM((groups, HD + 16, wide), F32),
            pltpu.VMEM((groups, 1, wide), F32),
        ],
        input_output_aliases={2 + inputs + i: i for i in range(len(into))},
        compiler_params=params(),
        cost_estimate=cost(10**10 * size),
        name="attend",
    )(docs, q, *kv, *into)


def attend_back_kernel(
    groups, heads, first, inputs, docs_ref, q_ref, do_ref, lse_ref, delta_ref, rot_ref, *refs
):
    kv_refs = refs[:inputs]
    chunks = 2 * lax.axis_size("seq")
    dq_ref, keep_ref, give_ref, kv_ref, stage, qs, qa, ds_, da, dq = refs[-10:]
    b = pl.program_id(0) + first
    own = q_ref.shape[2]
    ndoc = docs_ref.shape[1]
    starts = [docs_ref[b, k] for k in range(ndoc)]
    me = my_chunk()
    begin = start_chunk(starts, me * own, own)
    half = own // 2
    begin_second = start_chunk(starts, me * own + half, own)
    place_keys(kv_refs, kv_ref, begin, me)
    wide = heads * own
    tied = groups * HD
    plain = HD - RD
    q_doc = stack_queries(starts, me * own, half, heads)
    q_all, do_all = q_ref[0], do_ref[0]
    pad_q = jnp.zeros((LANE - HD - 32, wide), BF)
    pad_d = jnp.zeros((LANE - HD - 16, wide), BF)
    row_at = lax.broadcasted_iota(jnp.int32, (own, own), 0)
    column_at = lax.broadcasted_iota(jnp.int32, (own, own), 1)
    identity = jnp.where(row_at == column_at, 1.0, 0.0).astype(BF)

    def turn(rows, ref):
        for h in range(0, heads, 2):
            pair = [rows[:, (h + i) * own : (h + i + 1) * own] for i in range(2)]
            turned = mxu(identity, jnp.concatenate(pair, axis=0), NT).astype(BF)
            ref[h * own : (h + 1) * own] = turned[:, :LANE]
            ref[(h + 1) * own : (h + 2) * own] = turned[:, LANE:]

    for g in range(groups):
        q_rows = stack_heads(q_all, g * heads * HD, heads)
        do_rows = stack_heads(do_all, g * heads * HD, heads)
        qs[g] = q_rows
        ds_[g] = do_rows
        lse_rows = three_parts(-lse_ref[0, g : g + 1], wide)
        delta_row = stack_heads(delta_ref[0], g * heads, heads, 1)
        delta_rows = three_parts(-delta_row, wide)
        turn(jnp.concatenate([q_rows, q_doc, lse_rows, pad_q], axis=0), qa.at[g])
        turn(jnp.concatenate([do_rows, delta_rows, pad_d], axis=0), da.at[g])
    ones = first_rows(3, own)
    pad_k = jnp.zeros((LANE - HD - 32, own), BF)
    pad_v = jnp.zeros((LANE - HD - 16, own), BF)

    seq, core = lax.axis_index("seq"), lax.axis_index("mp")
    steps = chunks // 2

    def deliver(j, value):
        k = lax.rem(j // 2 - seq + steps, steps)

        @pl.when(lax.rem(j, 2) == core)
        def _():
            keep_ref[k, 0] = value()

        @pl.when(lax.rem(j, 2) != core)
        def _():
            give_ref[k, 0] = value()

    def clear(j, carry):
        deliver(j, lambda: jnp.zeros(keep_ref.shape[2:], BF))
        return carry

    lax.fori_loop(0, begin, clear, 0)
    lax.fori_loop(me + 1, chunks, clear, 0)

    def block(j, rows, diagonal):
        doc = key_rows(starts, j * own, own)
        rope_rows = kv_ref[j, tied : tied + RD]
        rope_sum = jnp.zeros((RD, own), F32)

        def keys_of(g):
            return jnp.concatenate(
                [kv_ref[j, g * HD : g * HD + plain], rope_rows], axis=0
            )

        def products(g):
            values = kv_ref[j, g * HD : (g + 1) * HD]
            return (
                mxu(qa[g, :rows], jnp.concatenate([keys_of(g), doc, ones, pad_k], axis=0), NN),
                mxu(da[g, :rows], jnp.concatenate([values, ones, pad_v], axis=0), NN),
            )

        following = products(0)
        for g in range(groups):
            logits, slopes = following
            if g + 1 < groups:
                following = products(g + 1)
            keys = keys_of(g)
            weights = jnp.exp(logits)
            if diagonal:
                query_at = lax.broadcasted_iota(jnp.int32, (half, own), 0)
                key_at = lax.broadcasted_iota(jnp.int32, (half, own), 1)
                causal = jnp.concatenate(
                    [key_at <= query_at + s * half for s in range(2) for _ in range(heads)], axis=0
                )
                weights = jnp.where(causal, weights, 0.0)
            grads = (weights * slopes).astype(BF)
            grad_values = mxu(ds_[g, :, :rows], weights.astype(BF), NN)
            grad_keys = mxu(qs[g, :, :rows], grads, NN)
            keys_t = keys.T
            grad_queries = mxu(grads, jnp.concatenate([keys_t, keys_t], axis=1), NN)
            if diagonal:
                dq[g] = grad_queries
            else:
                dq[g, :rows] += grad_queries
            stage[g * HD : g * HD + plain] = (
                grad_values[:plain] + grad_keys[:plain]
            ).astype(BF)
            stage[g * HD + plain : (g + 1) * HD] = grad_values[plain:].astype(BF)
            rope_sum = rope_sum + grad_keys[plain:]
        stage[tied : tied + RD] = rope_sum.astype(BF)
        deliver(j, lambda: stage[...])

    block(me, wide, True)

    def both(j, carry):
        block(j, wide, False)
        return carry

    def first_only(j, carry):
        block(j, wide // 2, False)
        return carry

    lax.fori_loop(begin_second, me, both, 0)
    lax.fori_loop(begin, begin_second, first_only, 0)
    straight, ahead, behind = rot_ref[0], rot_ref[1], rot_ref[2]
    lane = lax.broadcasted_iota(jnp.int32, (half, LANE), 1)
    quarter = RD // 2
    for g in range(groups):
        for s in range(2):
            positions = slice(s * half, (s + 1) * half)
            for pair in range(heads // 2):
                at = (s * heads + 2 * pair) * half
                two = jnp.where(lane < HD, dq[g, at : at + half], dq[g, at + half : at + 2 * half])
                turned = (
                    two * straight[positions]
                    + pltpu.roll(two, LANE - quarter, 1) * ahead[positions]
                    + pltpu.roll(two, quarter, 1) * behind[positions]
                )
                to = (g * heads + 2 * pair) * HD
                dq_ref[positions, to : to + 2 * HD] = turned.astype(BF)


def attend_backward(docs, q, do, lse, delta, turns, kv, groups, heads, first, size, kv_at, into):
    kv_rows, own = kv[0].shape[2:]
    count, chunks, inputs = docs.shape[0], 2 * lax.axis_size("seq"), len(kv)
    wide = heads * own
    width = q.shape[1]
    column = pl.BlockSpec((1, width, own), lambda b: (b + first, 0, 0))
    hbm = pl.BlockSpec(memory_space=pl.ANY)
    return pl.pallas_call(
        functools.partial(attend_back_kernel, groups, heads, first, inputs),
        grid=(size,),
        in_specs=[
            pl.BlockSpec(memory_space=pltpu.SMEM),
            column,
            column,
            pl.BlockSpec((1, groups, wide), lambda b: (b + first, 0, 0)),
            pl.BlockSpec((1, groups * heads, own), lambda b: (b + first, 0, 0)),
            pl.BlockSpec(turns.shape, lambda b: (0, 0, 0)),
        ]
        + kv_specs(kv, kv_at)
        + [hbm] * len(into),
        out_specs=[
            pl.BlockSpec((own, width), lambda b: (b + first, 0)),
            pl.BlockSpec((chunks // 2, 1, kv_rows, own), lambda b: (0, b, 0, 0)),
            pl.BlockSpec((chunks // 2, 1, kv_rows, own), lambda b: (0, b, 0, 0)),
        ],
        out_shape=[
            jax.ShapeDtypeStruct((count * own, width), BF),
            jax.ShapeDtypeStruct((chunks // 2, size, kv_rows, own), BF),
            jax.ShapeDtypeStruct((chunks // 2, size, kv_rows, own), BF),
        ],
        scratch_shapes=[
            pltpu.VMEM((chunks, kv_rows, own), BF),
            pltpu.VMEM((kv_rows, own), BF),
            pltpu.VMEM((groups, HD, wide), BF),
            pltpu.VMEM((groups, wide, LANE), BF),
            pltpu.VMEM((groups, HD, wide), BF),
            pltpu.VMEM((groups, wide, LANE), BF),
            pltpu.VMEM((groups, wide, LANE), F32),
        ],
        input_output_aliases={6 + inputs + i: i for i in range(len(into))},
        compiler_params=params(),
        cost_estimate=cost(10**9 * size),
        name="attend_back",
    )(docs, q, do, lse, delta, turns, *kv, *into)


def join_cores(keep, received):
    return [
        (keep[k].astype(F32) + received[k].astype(F32)).astype(BF) for k in range(keep.shape[0])
    ]


def send_keys(summed):
    return [summed[0]] + [shift(summed[k], "seq", k) for k in range(1, len(summed))]


def load_weights(refs, targets, sems):
    copies = []
    slot = 0
    for (source, side, axis), target in zip(refs, targets, strict=True):
        blocks = source.shape[axis] // LANE
        for t in range(blocks):
            to = pl.ds((2 * t + side) * LANE, LANE)
            of = pl.ds(t * LANE, LANE)
            src = source.at[:, of] if axis == 1 else source.at[of]
            dst = target.at[:, to] if axis == 1 else target.at[to]
            copies.append(pltpu.make_async_copy(src, dst, sems.at[slot]))
            slot += 1
    return copies


def put(ref, t, value):
    value = value.astype(BF)
    ref[2 * t], ref[2 * t + 1] = value[:, :LANE], value[:, LANE:]


def wide(ref):
    return jnp.concatenate([ref[i] for i in range(ref.shape[0])], axis=1)


def feed_kernel(
    x_ref, og_ref, ga_ref, o_ref, gain_ref, wo_ref, wgo_ref, wgp_ref, wuo_ref, wup_ref, wdo_ref, wdp_ref,
    out_ref, nt_ref, ogt_ref, act_ref, gg_ref, gu_ref, gh_ref, gat_ref, do_ref, delta_ref, gg2_ref,
    wo, wg, wu, wd, sems,
):
    b = pl.program_id(0)

    @pl.when(b == 0)
    def _():
        copies = [pltpu.make_async_copy(wo_ref, wo, sems.at[sems.shape[0] - 1])]
        copies += load_weights(
            [
                (wgo_ref, 0, 1), (wgp_ref, 1, 1), (wuo_ref, 0, 1), (wup_ref, 1, 1),
                (wdo_ref, 0, 0), (wdp_ref, 1, 0),
            ],
            [wg, wg, wu, wu, wd, wd],
            sems,
        )
        for copy in copies:
            copy.start()
        for copy in copies:
            copy.wait()
        gg2_ref[...] = jnp.zeros(gg2_ref.shape, F32)

    og = og_ref[0]
    heads_out = o_ref[0]
    gain = gain_ref[...]
    hidden = x_ref[0].astype(F32) + mxu(heads_out, wo[...], TN)
    inverse = lax.rsqrt(jnp.mean(hidden * hidden, axis=-1, keepdims=True) + epsilon)
    normed = (hidden * inverse * gain).astype(BF)
    nt_ref[0] = normed.T
    ogt_ref[0] = og.T
    units = wg.shape[1]
    tile = 2 * LANE
    for t in range(units // tile):
        at = slice(t * tile, (t + 1) * tile)
        gate = mxu(normed, wg[:, at], NN)
        up = mxu(normed, wu[:, at], NN)
        grad = ga_ref[:, at].astype(F32)
        sigmoid = 1.0 / (1.0 + jnp.exp(-gate))
        silu = gate * sigmoid
        put(act_ref, t, silu * up)
        put(gu_ref, t, grad * silu)
        put(gg_ref, t, grad * up * (sigmoid + silu * (1.0 - sigmoid)))
    result = mxu(wide(act_ref), wd[...], NN)
    out_ref[0] = (hidden + result).astype(BF)
    grad_normed = mxu(wide(gg_ref), wg[...], NT) + mxu(wide(gu_ref), wu[...], NT)
    scaled = grad_normed * gain
    gg2_ref[...] += jnp.sum(grad_normed * (hidden * inverse), axis=0, keepdims=True)
    mean = jnp.mean(scaled * hidden, axis=-1, keepdims=True)
    grad_hidden = og.astype(F32) + inverse * scaled - hidden * (inverse * inverse * inverse * mean)
    grad_attended = grad_hidden.astype(BF)
    gh_ref[0] = grad_attended
    gat_ref[0] = grad_attended.T
    grad_heads = mxu(wo[...], grad_attended, NT).astype(BF)
    do_ref[0] = grad_heads
    product = grad_heads.astype(F32) * heads_out.astype(F32)
    for h in range(product.shape[0] // HD):
        delta_ref[0, h : h + 1] = jnp.sum(product[h * HD : (h + 1) * HD], axis=0, keepdims=True)


def feed(x, og, slopes, heads_out, gain, wo, wg, wu, wd):
    count, own, width = x.shape
    hd = heads_out.shape[1]
    half = wg[0].shape[1]
    units = 2 * half
    tokens = count * own
    seq = pl.BlockSpec((1, own, width), lambda b: (b, 0, 0))
    column = lambda rows: pl.BlockSpec((1, rows, own), lambda b: (b, 0, 0))
    row = pl.BlockSpec((own, units), lambda b: (b, 0))
    blocks = pl.BlockSpec((units // LANE, own, LANE), lambda b: (0, b, 0))
    hbm = pl.BlockSpec(memory_space=pl.ANY)
    return pl.pallas_call(
        feed_kernel,
        grid=(count,),
        in_specs=[seq, seq, row, column(hd), pl.BlockSpec((1, width), lambda b: (0, 0))] + [hbm] * 7,
        out_specs=[
            seq, column(width), column(width), blocks, blocks, blocks, seq, column(width), column(hd),
            pl.BlockSpec((1, hd // HD, own), lambda b: (b, 0, 0)),
            pl.BlockSpec((1, width), lambda b: (0, 0)),
        ],
        out_shape=[
            jax.ShapeDtypeStruct(x.shape, BF),
            jax.ShapeDtypeStruct((count, width, own), BF),
            jax.ShapeDtypeStruct((count, width, own), BF),
            jax.ShapeDtypeStruct((units // LANE, tokens, LANE), BF),
            jax.ShapeDtypeStruct((units // LANE, tokens, LANE), BF),
            jax.ShapeDtypeStruct((units // LANE, tokens, LANE), BF),
            jax.ShapeDtypeStruct(x.shape, BF),
            jax.ShapeDtypeStruct((count, width, own), BF),
            jax.ShapeDtypeStruct((count, hd, own), BF),
            jax.ShapeDtypeStruct((count, hd // HD, own), F32),
            jax.ShapeDtypeStruct((1, width), F32),
        ],
        scratch_shapes=[
            pltpu.VMEM((hd, width), BF),
            pltpu.VMEM((width, units), BF),
            pltpu.VMEM((width, units), BF),
            pltpu.VMEM((units, width), BF),
            pltpu.SemaphoreType.DMA((6 * (half // LANE) + 1,)),
        ],
        compiler_params=params(),
        cost_estimate=cost(2 * tokens * width * (5 * units + 2 * hd)),
        name="feed",
    )(x, og, slopes, heads_out, gain, wo, *wg, *wu, *wd)


def regroup_rows(value, split):
    if split is None:
        return value
    count_d, count_s = split
    own = value.shape[0] // (count_d * count_s)
    return jnp.concatenate(
        [
            value[(d * count_s + s) * own : (d * count_s + s + 1) * own]
            for s in range(count_s)
            for d in range(count_d)
        ],
        axis=0,
    )


def side_by_side(source, target, sems, slot):
    count, _, own = source.shape
    return [
        pltpu.make_async_copy(
            source.at[i], target.at[:, pl.ds(i * own, own)], sems.at[slot + i]
        )
        for i in range(count)
    ]


def early_kernel(
    split, cut, nt_ref, gg_ref, gu_ref, act_ref, act_next_ref, ogt_ref, gat_ref, o_ref, out_ref,
    rest_ref, nt, ogt, gat, heads_out, stage, landed, load_sems, sends, receives,
):
    t = pl.program_id(0)
    core = lax.axis_index("mp")
    tiles = landed.shape[0]
    tile = 2 * LANE
    pairs, head_tiles = gg_tiles(gg_ref, tiles, heads_out)
    other_core = {"mp": 1 - core}
    loads = []
    for source, target in ((nt_ref, nt), (gat_ref, gat), (o_ref, heads_out), (ogt_ref, ogt)):
        loads.append(side_by_side(source, target, load_sems, len(loads) * nt_ref.shape[0]))

    @pl.when(t == 0)
    def _():
        for copies in loads:
            for copy in copies:
                copy.start()
        barrier = pltpu.get_barrier_semaphore()
        pl.semaphore_signal(barrier, inc=1, device_id=other_core, device_id_type=pl.DeviceIdType.MESH)
        pl.semaphore_wait(barrier, 1)
        for copy in loads[0]:
            copy.wait()

    @pl.when(t == pairs)
    def _():
        for copy in loads[1] + loads[2]:
            copy.wait()

    @pl.when(t == pairs + head_tiles)
    def _():
        for copy in loads[3]:
            copy.wait()

    def send(i):
        return pltpu.make_async_remote_copy(
            src_ref=stage.at[lax.rem(i, 2)],
            dst_ref=landed.at[i],
            send_sem=sends.at[i],
            recv_sem=receives.at[i],
            device_id=other_core,
            device_id_type=pl.DeviceIdType.MESH,
        )

    def deliver(product):
        @pl.when(t < tiles)
        def _():
            @pl.when(t >= 2)
            def _():
                send(t - 2).wait_send()

            stage[lax.rem(t, 2)] = regroup_rows(product(), split).astype(BF)
            send(t).start()

        @pl.when(t >= tiles)
        def _():
            @pl.when(t < tiles + 2)
            def _():
                send(t - 2).wait_send()

            send(t - tiles).wait_recv()
            total = regroup_rows(product(), split) + landed[t - tiles].astype(F32)
            total = total.astype(BF)
            out_ref[...] = jnp.where(t < tiles + cut, total, out_ref[...])
            rest_ref[...] = total

    at = lax.rem(t, tiles)

    @pl.when(at < pairs)
    def _():
        deliver(lambda: mxu(nt[...], jnp.concatenate([gg_ref[0], gu_ref[0]], axis=1), NN))

    @pl.when((at >= pairs) & (at < pairs + head_tiles))
    def _():
        side = jnp.where(t < tiles, 1 - core, core)
        row = pl.multiple_of((side * head_tiles + at - pairs) * tile, tile)
        deliver(lambda: mxu(gat[...], heads_out[pl.ds(row, tile)], NT))

    @pl.when(at >= pairs + head_tiles)
    def _():
        deliver(
            lambda: mxu(ogt[...], jnp.concatenate([act_ref[0], act_next_ref[0]], axis=1), NN)
        )


def gg_tiles(gg_ref, tiles, heads_out):
    head_tiles = heads_out.shape[0] // (4 * LANE)
    return (2 * (tiles - head_tiles)) // 3, head_tiles


def early_grads(nt, gg, gu, act, ogt, gat, heads_out, split):
    count, width, own = nt.shape
    tokens = count * own
    units = gg.shape[0] * LANE
    blocks = units // (2 * LANE)
    tile = 2 * LANE
    hd = heads_out.shape[1]
    head_tiles = hd // (2 * tile)
    down_tiles = (blocks + 1) // 2
    tiles = blocks + head_tiles + down_tiles
    cut = tiles - 4
    rest = units + units // 2 + hd // 2 - cut * tile
    hbm = pl.BlockSpec(memory_space=pl.ANY)
    side = lambda t: jnp.where(t < tiles, 1, 0)

    def pair(t):
        return (2 * jnp.minimum(lax.rem(t, tiles), blocks - 1) + side(t), 0, 0)

    def down(t, shift_by):
        at = jnp.clip(lax.rem(t, tiles) - blocks - head_tiles, 0, down_tiles - 1)
        return (2 * jnp.minimum(2 * at + shift_by, blocks - 1) + side(t), 0, 0)

    block = lambda index: pl.BlockSpec((1, tokens, LANE), index)
    return pl.pallas_call(
        functools.partial(early_kernel, split, cut),
        grid=(2 * tiles,),
        in_specs=[
            hbm,
            block(pair),
            block(pair),
            block(lambda t: down(t, 0)),
            block(lambda t: down(t, 1)),
            hbm,
            hbm,
            hbm,
        ],
        out_specs=[
            pl.BlockSpec((width, tile), lambda t: (0, jnp.clip(t - tiles, 0, cut - 1))),
            pl.BlockSpec((width, tile), lambda t: (0, jnp.maximum(t - tiles - cut, 0))),
        ],
        out_shape=[
            jax.ShapeDtypeStruct((width, cut * tile), BF),
            jax.ShapeDtypeStruct((width, rest), BF),
        ],
        scratch_shapes=[
            pltpu.VMEM((width, tokens), BF),
            pltpu.VMEM((width, tokens), BF),
            pltpu.VMEM((width, tokens), BF),
            pltpu.VMEM((hd, tokens), BF),
            pltpu.VMEM((2, width, tile), BF),
            pltpu.VMEM((tiles, width, tile), BF),
            pltpu.SemaphoreType.DMA((4 * count,)),
            pltpu.SemaphoreType.DMA((tiles,)),
            pltpu.SemaphoreType.DMA((tiles,)),
        ],
        compiler_params=pltpu.CompilerParams(
            vmem_limit_bytes=56 * MIB, collective_id=3, has_side_effects=True
        ),
        cost_estimate=cost(6 * 10**10),
        name="early_grads",
    )(nt, gg, gu, act, act, ogt, gat, heads_out)


def tail_kernel(
    order, x_ref, dq_ref, nt_ref, gain_ref, wq_ref, wkv_ref, cos_ref, sin_ref, gg2_ref,
    nt_all_ref, dq_all_ref, early_ref, near_refs, *refs,
):
    count_d, count_s = lax.axis_size("dp"), lax.axis_size("seq")
    me_d, me_s, core = lax.axis_index("dp"), lax.axis_index("seq"), lax.axis_index("mp")
    (keep_mid, got_mid, keep_end, give_end, update_ref, query_out, small_out, early_out) = refs[:8]
    (
        key_in, sum_mid, sum_end, got_end, query_stage, query_in, query_sum, query_seq, query_part,
        query_dp, early_in, early_own, nt_all, dq_all, load_sems, dw, gg1, small_other, small_in, small_sum, small_seq, small_part,
        small_dp, sends, receives,
    ) = refs[8:]
    rows = query_out.shape[0]
    step = pl.program_id(0)
    other_core = {"mp": 1 - core}
    seq_peers = [{"seq": lax.rem(me_s + k, count_s)} for k in range(1, count_s)]
    dp_peers = [{"dp": lax.rem(me_d + k, count_d)} for k in range(1, count_d)]
    peers = [other_core] + seq_peers + dp_peers
    slots = iter(range(sends.shape[0]))

    def link(source, target, peer):
        slot = next(slots)
        return pltpu.make_async_remote_copy(
            src_ref=source,
            dst_ref=target,
            send_sem=sends.at[slot],
            recv_sem=receives.at[slot],
            device_id=peer,
            device_id_type=pl.DeviceIdType.MESH,
        )

    to_seq = [lax.rem(me_s + k, count_s) for k in range(1, count_s)]
    to_dp = [lax.rem(me_d + k, count_d) for k in range(1, count_d)]
    early_copies = [
        link(early_ref.at[to_dp[k]], early_in.at[k], dp_peers[k]) for k in range(count_d - 1)
    ]
    end_core = link(give_end, got_end, other_core)
    key_copies, at = [], 0
    for part in (sum_mid, sum_end):
        size = part.shape[1]
        key_copies.append(
            [
                link(part.at[k + 1], key_in.at[k, pl.ds(at, size)], seq_peers[k])
                for k in range(count_s - 1)
            ]
        )
        at += size
    query_core = link(query_stage, query_in, other_core)
    query_seqs = [
        link(query_sum.at[to_seq[k]], query_seq.at[k], seq_peers[k]) for k in range(count_s - 1)
    ]
    query_dps = [
        link(query_part.at[to_dp[k]], query_dp.at[k], dp_peers[k]) for k in range(count_d - 1)
    ]
    small_core = link(small_other, small_in, other_core)
    small_seqs = [
        link(small_sum.at[to_seq[k]], small_seq.at[k], seq_peers[k]) for k in range(count_s - 1)
    ]
    small_dps = [
        link(small_part.at[to_dp[k]], small_dp.at[k], dp_peers[k]) for k in range(count_d - 1)
    ]

    def start(copies):
        for copy in copies:
            copy.start()

    def by_seq(total, target):
        for s in range(count_s):
            for d in range(count_d):
                of = (d * count_s + s) * rows
                target[s, d * rows : (d + 1) * rows] = total[of : of + rows].astype(BF)

    def gather(own, copies, arrived):
        total = own.astype(F32)
        for k, copy in enumerate(copies):
            copy.wait()
            total = total + arrived[k].astype(F32)
        return total

    def by_dp(total, target):
        for d in range(count_d):
            target[d] = total[d * rows : (d + 1) * rows].astype(BF)

    loads = side_by_side(nt_all_ref, nt_all, load_sems, 2) + [
        pltpu.make_async_copy(dq_all_ref, dq_all, load_sems.at[0]),
        pltpu.make_async_copy(early_ref.at[me_d], early_own, load_sems.at[1]),
    ]

    def join(mine, got, total):
        for k in range(count_s):
            total[k] = (mine[k].astype(F32) + got[k].astype(F32)).astype(BF)

    def query_product(half):
        size = query_stage.shape[1]
        columns = pl.ds(pl.multiple_of(half * size, size), size)
        return mxu(nt_all[...], dq_all[:, columns], NN)

    @pl.when(step == 0)
    def _():
        start(loads)
        barrier = pltpu.get_barrier_semaphore()
        for peer in peers:
            pl.semaphore_signal(barrier, inc=1, device_id=peer, device_id_type=pl.DeviceIdType.MESH)
        pl.semaphore_wait(barrier, len(peers))
        start([end_core])
        join(keep_mid, got_mid, sum_mid)
        start(key_copies[0])
        start(early_copies)
        for load in loads:
            load.wait()
        query_stage[...] = query_product(1 - core).astype(BF)
        start([query_core])
        end_core.wait()
        join(keep_end, got_end, sum_end)
        start(key_copies[1])
        dw[...] = jnp.zeros(dw.shape, F32)
        gg1[...] = jnp.zeros(gg1.shape, F32)

    @pl.when(step == 1)
    def _():
        product = query_product(core)
        query_core.wait()
        by_seq(product + query_in[...].astype(F32), query_sum)
        start(query_seqs)

    tied = wkv_ref.shape[0] - RD

    def finish(summed):
        turned = rotate_rows(summed[tied:], cos_ref[...], -sin_ref[...])
        dkv = jnp.concatenate([summed[:tied], turned], axis=0).astype(BF)
        grad_normed = mxu(dq_ref[...], wq_ref[...], NN) + mxu(dkv, wkv_ref[...], TN)
        dw[...] += mxu(nt_ref[0], dkv, NT)
        x = x_ref[0].astype(F32)
        inverse = lax.rsqrt(jnp.mean(x * x, axis=-1, keepdims=True) + epsilon)
        scaled = grad_normed * gain_ref[...]
        gg1[...] += jnp.sum(grad_normed * (x * inverse), axis=0, keepdims=True)
        mean = jnp.mean(scaled * x, axis=-1, keepdims=True)
        update = inverse * scaled - x * (inverse * inverse * inverse * mean)
        update_ref[0] = update.astype(BF)

    begin = 0
    for (_, size), terms in zip(order, near_refs):

        @pl.when((step >= begin) & (step < begin + size))
        def _():
            summed = terms[0][0].astype(F32)
            for ref in terms[1:]:
                summed = summed + ref[0].astype(F32)
            finish(summed)

        begin += size

    base = begin
    for part, far in enumerate((sum_mid, sum_end)):
        size = far.shape[1]

        @pl.when(step == begin)
        def _():
            for copy in key_copies[part]:
                copy.wait()

        @pl.when((step >= begin) & (step < begin + size))
        def _():
            at = step - base
            summed = far[0, step - begin].astype(F32)
            for k in range(count_s - 1):
                summed = summed + key_in[k, at].astype(F32)
            finish(summed)

        begin += size

    @pl.when(step == begin - 2)
    def _():
        total = gather(query_sum[me_s], query_seqs, query_seq)
        by_dp(total, query_part)
        start(query_dps)

    @pl.when(step == begin - 1)
    def _():
        width = dw.shape[0]
        pad = jnp.zeros((LANE - RD, width), F32)
        row = lax.broadcasted_iota(jnp.int32, (LANE, width), 0)
        gains = jnp.where(row == RD, gg1[...], 0.0)
        gains = jnp.where(row == RD + 1, gg2_ref[...], gains)
        weights = dw[...]
        rope = jnp.concatenate([weights[:, tied:], jnp.zeros((width, LANE - RD), F32)], axis=1)
        small = rope + gains.T
        half = tied // 2
        first, second = weights[:, :half], weights[:, half:tied]
        mine = jnp.concatenate([jnp.where(core == 0, first, second), small], axis=1)
        other = jnp.concatenate([jnp.where(core == 0, second, first), small], axis=1)
        small_other[...] = other.astype(BF)
        start([small_core])
        small_core.wait()
        by_seq(mine + small_in[...].astype(F32), small_sum)
        start(small_seqs)
        by_dp(gather(small_sum[me_s], small_seqs, small_seq), small_part)
        start(small_dps)
        query_out[...] = gather(query_part[me_d], query_dps, query_dp)
        early_out[...] = gather(early_own[...], early_copies, early_in)
        small_out[...] = gather(small_part[me_d], small_dps, small_dp)


def tail(
    order, x, dq, nt, gain, wq, wkv, cosine, sine_table, grad_gain_two, early, near,
    shares,
):
    count, own, width = x.shape
    count_d, count_s = lax.axis_size("dp"), lax.axis_size("seq")
    rows = width // (count_d * count_s)
    kv_rows = wkv.shape[0]
    tied = kv_rows - RD
    wide = dq.shape[1] // 2
    narrow = tied // 2 + LANE
    middle, end = shares[0].shape, shares[2].shape
    sent = middle[1] + end[1]

    def place(i):
        done, at = 0, i
        for first, size in order:
            at = jnp.where((i >= done) & (i < done + size), first + i - done, at)
            done += size
        return at

    seq = pl.BlockSpec((1, own, width), lambda i: (place(i), 0, 0))
    whole = lambda array: pl.BlockSpec(array.shape, lambda i: (0,) * array.ndim)
    near_specs, done = [], 0
    for (_, size), terms in zip(order, near):
        index = lambda i, done=done, size=size: (jnp.clip(i - done, 0, size - 1), 0, 0)
        near_specs += [pl.BlockSpec((1, kv_rows, own), index)] * len(terms)
        done += size
    fixed = [gain, wq, wkv, cosine, sine_table, grad_gain_two]
    hbm = pl.BlockSpec(memory_space=pl.ANY)
    outs = [
        jax.ShapeDtypeStruct(x.shape, BF),
        jax.ShapeDtypeStruct((rows, wide), F32),
        jax.ShapeDtypeStruct((rows, narrow), F32),
        jax.ShapeDtypeStruct((rows, early.shape[2]), F32),
    ]
    near_all = [term for terms in near for term in terms]

    def kernel(*refs):
        head, rest = refs[:12], refs[12 + len(near_all) :]
        nears = [refs[12 + i * count_s : 12 + (i + 1) * count_s] for i in range(len(near))]
        tail_kernel(order, *head, nears, *rest)

    slots = 3 * (count_d - 1) + 4 * (count_s - 1) + 3
    return pl.pallas_call(
        kernel,
        grid=(count,),
        in_specs=[
            seq,
            pl.BlockSpec((own, dq.shape[1]), lambda i: (place(i), 0)),
            pl.BlockSpec((1, width, own), lambda i: (place(i), 0, 0)),
        ]
        + [whole(array) for array in fixed]
        + [hbm, hbm, hbm]
        + near_specs
        + [whole(array) for array in shares],
        out_specs=[seq] + [whole(out) for out in outs[1:]],
        out_shape=outs,
        scratch_shapes=[
            pltpu.VMEM((count_s - 1, sent, kv_rows, own), BF),
            pltpu.VMEM(middle, BF),
            pltpu.VMEM(end, BF),
            pltpu.VMEM(end, BF),
            pltpu.VMEM((width, wide), BF),
            pltpu.VMEM((width, wide), BF),
            pltpu.VMEM((count_s, count_d * rows, wide), BF),
            pltpu.VMEM((count_s - 1, count_d * rows, wide), BF),
            pltpu.VMEM((count_d, rows, wide), BF),
            pltpu.VMEM((count_d - 1, rows, wide), BF),
            pltpu.VMEM((count_d - 1, rows, early.shape[2]), BF),
            pltpu.VMEM((rows, early.shape[2]), BF),
            pltpu.VMEM((width, count * own), BF),
            pltpu.VMEM(dq.shape, BF),
            pltpu.SemaphoreType.DMA((2 + count,)),
            pltpu.VMEM((width, kv_rows), F32),
            pltpu.VMEM((1, width), F32),
            pltpu.VMEM((width, narrow), BF),
            pltpu.VMEM((width, narrow), BF),
            pltpu.VMEM((count_s, count_d * rows, narrow), BF),
            pltpu.VMEM((count_s - 1, count_d * rows, narrow), BF),
            pltpu.VMEM((count_d, rows, narrow), BF),
            pltpu.VMEM((count_d - 1, rows, narrow), BF),
            pltpu.SemaphoreType.DMA((slots,)),
            pltpu.SemaphoreType.DMA((slots,)),
        ],
        compiler_params=pltpu.CompilerParams(
            vmem_limit_bytes=56 * MIB, collective_id=1, has_side_effects=True
        ),
        cost_estimate=cost(10**8),
        name="tail",
    )(x, dq, nt, *fixed, nt, dq, early, *near_all, *shares)


def turn_tables(cosine, sine_table):
    plain = HD - RD
    one = jnp.ones((cosine.shape[0], plain), F32)
    none = jnp.zeros_like(one)
    quiet = jnp.zeros_like(sine_table)
    straight = jnp.concatenate([one, cosine, cosine], axis=1)
    ahead = jnp.concatenate([none, sine_table, quiet], axis=1)
    behind = jnp.concatenate([none, quiet, -sine_table], axis=1)
    tables = jnp.stack([jnp.concatenate([t, t], axis=1) for t in (straight, ahead, behind)])
    return tables * HD ** (-0.5)


def after(value, *others):
    return lax.optimization_barrier((value, *others))[0]


def on_device_fast(
    inputs, gain_one, w_query, w_tied, w_rope, w_out, gain_two, w_gate, w_up, w_down,
    doc_starts, out_grad,
):
    count, own, width = inputs.shape
    cores = lax.axis_size("mp")
    groups = cores * w_tied.shape[1] // HD
    all_heads = cores * w_query.shape[1] // HD
    heads = all_heads // groups
    mp_index = lax.axis_index("mp")
    split = (lax.axis_size("dp"), lax.axis_size("seq"))
    tied_other, query_other = swap_cores(w_tied), swap_cores(w_query)
    down_other = swap_cores(w_down)
    gain_one_float = gain_one.astype(F32)[None]
    gain_two_float = gain_two.astype(F32)[None]
    cosine, sine_table = rope_tables(my_chunk() * own, own, RD)
    cosine_t, sine_t = cosine.T, sine_table.T
    half = count // 2
    kv, normed_t, q, slopes, queries_weights, keys_weights, kv_near, kv_far = project(
        inputs, out_grad, gain_one_float, (w_query, query_other), (w_tied, tied_other), w_rope,
        (w_down, down_other), cosine_t, sine_t, half,
    )
    kv_late = send_near(kv)
    out_other = swap_cores(after(w_out, kv))
    gate_other, up_other = swap_cores(after(w_gate, kv)), swap_cores(after(w_up, kv))
    span = half - half // 4
    made = attend_forward(doc_starts, q, [kv_near, kv_far], groups, heads, 0, span, 0, ())
    kv_late = send_far([after(part, *made) for part in kv_late])
    made = attend_forward(
        doc_starts, q, [kv_near, kv_far], groups, heads, span, half - span, span, made
    )
    heads_out, lse = attend_forward(doc_starts, q, kv_late, groups, heads, half, half, 0, made)
    out_both = by_core(w_out, after(out_other, lse), 0)
    (
        outputs, normed_two_t, out_grad_t, active, grad_gate, grad_up, grad_hidden, grad_attended_t,
        grad_heads, delta, grad_gain_two,
    ) = feed(
        inputs, out_grad, slopes, heads_out, gain_two_float, out_both, (w_gate, gate_other),
        (w_up, up_other), (w_down, down_other),
    )
    units, head_half = w_gate.shape[1], w_out.shape[0]
    first_sum, rest_sum = early_grads(
        normed_two_t, grad_gate, grad_up, active, out_grad_t, grad_attended_t, heads_out, split
    )
    first_sum, rest_sum, grad_heads = lax.optimization_barrier((first_sum, rest_sum, grad_heads))
    first_sum = lax.psum_scatter(first_sum, "seq", scatter_dimension=0, tiled=True)

    turns = turn_tables(cosine, sine_table)
    quarter = half // 2
    backward = [
        (half, half, kv_late, 0),
        (quarter, half - quarter, [kv_near, kv_far], quarter),
        (0, quarter, [kv_near, kv_far], 0),
    ]
    rest_sum = rest_sum.reshape(split[1], split[0], -1, rest_sum.shape[1])
    rest_sum = add_up(send_steps(rest_sum, "dp", 1)).astype(BF)
    rest_terms = send_steps(rest_sum, "seq", 0)
    dq, near, shares = (), [], []
    for part, (at, size, kv_part, kv_at) in enumerate(backward):
        need = near[0][:1] if part == 2 else []
        made_dq, keep, give = attend_backward(
            doc_starts, after(q, *need), grad_heads, lse, delta, turns, kv_part, groups, heads, at,
            size, kv_at, dq,
        )
        dq = (made_dq,)
        if part == 0:
            first_shares = (keep, swap_cores(after(give, rest_sum)))
        if part == 1:
            give = after(give, *rest_terms)
            near.append(send_keys(join_cores(*first_shares)))
            shares = [keep, swap_cores(give)]
        if part == 2:
            shares += [keep, give]
    early = first_sum.reshape(split[0], -1, first_sum.shape[1])
    order = [span[:2] for span in backward]
    update, query_sum, small_sum, first_sum = tail(
        order, inputs, dq[0], normed_t, gain_one_float, queries_weights, keys_weights,
        cosine_t, sine_t, grad_gain_two, early, near,
        shares,
    )
    grad_inputs = grad_hidden.astype(F32) + update.astype(F32)
    half_tied = groups * HD // cores
    late_sum, small_sum = small_sum[:, :half_tied], small_sum[:, half_tied:]
    rows = small_sum.shape[0] // cores
    small_sum = lax.dynamic_slice_in_dim(small_sum, mp_index * rows, rows, 0)
    pairs = first_sum[:, : 2 * units].reshape(first_sum.shape[0], units // LANE, 2, LANE)
    gate_sum = pairs[:, :, 0].reshape(-1, units)
    up_sum = pairs[:, :, 1].reshape(-1, units)
    out_sum = first_sum[:, 2 * units : 2 * units + head_half]
    down_sum = jnp.concatenate([first_sum[:, 2 * units + head_half :], add_up(rest_terms)], axis=1)
    return (
        outputs,
        grad_inputs,
        small_sum[:, RD],
        query_sum,
        late_sum,
        small_sum[:, :RD],
        out_sum.T,
        small_sum[:, RD + 1],
        gate_sum,
        up_sum,
        down_sum.T,
    )


def solution(mesh):
    in_specs = (
        P("dp", ("seq", "mp"), None),
        P(),
        P(None, "mp"),
        P(None, "mp"),
        P(),
        P("mp", None),
        P(),
        P(None, "mp"),
        P(None, "mp"),
        P("mp", None),
        P("dp", None),
        P("dp", ("seq", "mp"), None),
    )
    out_specs = (
        P("dp", ("seq", "mp"), None),
        P("dp", ("seq", "mp"), None),
        P(("dp", "seq", "mp")),
        P(("dp", "seq"), "mp"),
        P(("dp", "seq"), "mp"),
        P(("dp", "seq", "mp"), None),
        P("mp", ("dp", "seq")),
        P(("dp", "seq", "mp")),
        P(("dp", "seq"), "mp"),
        P(("dp", "seq"), "mp"),
        P("mp", ("dp", "seq")),
    )

    def local(inputs, *rest):
        step = on_device_fast if inputs.shape[1] % (2 * LANE) == 0 else on_device
        return step(inputs, *rest)

    return jax.shard_map(
        local, mesh=mesh, in_specs=in_specs, out_specs=out_specs, check_vma=False
    )
```
